256 devices in a mesh: cls: 4 (over z_hi), grp: 4 (over x), dom: 16 (over y, z_lo, core).
Axes of the slice: x: 4, y: 4, z: 8 (z_hi: 4, z_lo: 2; z = z_hi * 2 + z_lo), core: 2. Of those that a mesh axis runs over, the one named last changes fastest.
Arguments:
- particle_images: bfloat16 [2560, 8192], P(('grp', 'dom')), may hold values from -110 to 110, as said below
- particle_groups: int32 [2560], P(('grp', 'dom')), may hold values from 0 to 7
- live_counts: int32 [64], P(('grp', 'dom')), may hold values from 1 to 40, as said below
- ctf_table: float32 [8, 4096], replicated, may hold values from -1 to 1
- projections: bfloat16 [8192, 8, 200], P(('grp', 'dom'), 'cls'), may hold values from -0.25 to 0.25
Outputs:
- insertions: float32 [8, 200, 8192], P('cls', None, ('grp', 'dom'))
- class_weights: float32 [8, 8, 200], P('cls')
- log_evidence: float32 [2560], P(('grp', 'dom'))
The draws below stay inside these ranges and needn't reach their ends.
Inputs may be any that keep to these rules, and one draw needn't show every extreme that they name: `particle_images`: particle image coefficients. `live_counts`: live particles of one shard; in every draw some shard has all 40 slots live.
All inputs are finite; a program needn't handle non-finite values.
Results may differ from the reference program's by a relative error of at most 0.012.
The reference program's roundings to bfloat16 on the way count: a program that leaves them out, or rounds other values in their place, can miss the bound.
Values may be sent and summed in bfloat16 or wider, within the bound.
No kernel may reach another device: no remote copies, remote signals or barrier semaphores. Data moves between devices by JAX's collectives and lax.ppermute only.
A program may use at most 128 MiB of HBM per device.

```python
import math
import jax
import jax.numpy as jnp
from jax import lax

K = 8
IMG = 64
ROTS = 200
SIDE = 5
GROUPS = 8
NP_DEV = 40
F = 4096
TWOF = 8192
SHARDS = 64
PARTICLES = 2560


def common_fields(key):
    keys = jax.random.split(jax.random.fold_in(key, 101), 8)
    groups = jax.random.randint(keys[0], (PARTICLES,), 0, GROUPS).astype(jnp.int32)
    ctf = jax.random.uniform(keys[1], (GROUPS, F), jnp.float32, -1.0, 1.0)
    stack = 0.04 * jax.random.truncated_normal(keys[2], -6.0, 6.0, (TWOF, K, ROTS), jnp.float32)
    return (groups, ctf, stack, keys)


def draw_particle_groups(key, part):
    groups, ctf, stack, keys = common_fields(key)
    return groups


def draw_ctf_table(key, part):
    groups, ctf, stack, keys = common_fields(key)
    return ctf


def draw_projections(key, part):
    groups, ctf, stack, keys = common_fields(key)
    return stack.astype(jnp.bfloat16)


def draw_particle_images(key, part):
    groups, ctf, stack, keys = common_fields(key)
    key = jax.random.fold_in(key, 11)
    first = jax.random.fold_in(key, 0)
    values = jax.random.truncated_normal(first, -4.0, 4.0, (PARTICLES, TWOF), jnp.float32)
    strength = jnp.exp(jax.random.uniform(keys[3], (PARTICLES,), jnp.float32, jnp.log(150.0), jnp.log(400.0)))
    picks = jax.random.randint(keys[4], (PARTICLES, 2), 0, K * ROTS)
    slots = jnp.arange(PARTICLES, dtype=jnp.int32) % NP_DEV
    chosen = (slots == 0) | (jax.random.uniform(keys[5], (PARTICLES,), jnp.float32) < 0.25)
    amplitude = strength / (2.0 * F * 0.0016 / 3.0)
    columns = stack.reshape(TWOF, K * ROTS).T
    ctf_rows = jnp.concatenate([ctf, ctf], axis=1)[groups]
    aligned = ctf_rows * (columns[picks[:, 0]] + 0.99 * columns[picks[:, 1]])
    aligned = amplitude[:, None] * aligned
    values = values + jnp.where(chosen[:, None], aligned, jnp.float32(0.0))
    return values.astype(jnp.bfloat16)


def draw_live_counts(key, part):
    key = jax.random.fold_in(key, 5)
    first, second = jax.random.split(key)
    values = jax.random.randint(first, (SHARDS,), 1, NP_DEV + 1)
    fullest = jax.random.randint(second, (), 0, SHARDS)
    return jnp.where(jnp.arange(SHARDS) == fullest, NP_DEV, values).astype(jnp.int32)


def setup_inputs(seed: int = 0) -> dict:
    splits = jax.random.split(jax.random.key(seed), 6)
    return {
        "particle_images": draw_particle_images(jax.random.fold_in(splits[5], 71), 0),
        "particle_groups": draw_particle_groups(jax.random.fold_in(splits[5], 71), 0),
        "live_counts": draw_live_counts(jax.random.fold_in(splits[5], 71), 0),
        "ctf_table": draw_ctf_table(jax.random.fold_in(splits[5], 71), 0),
        "projections": draw_projections(jax.random.fold_in(splits[5], 71), 0),
    }


def build_shifted(images, groups, ctf_table):
    freqs = IMG * IMG
    index = jnp.arange(freqs, dtype=jnp.int32)
    rowf = index // IMG
    colf = index % IMG
    shift_index = jnp.arange(SIDE * SIDE, dtype=jnp.int32)
    offx = shift_index // SIDE - SIDE // 2
    offy = shift_index % SIDE - SIDE // 2
    phase = (offx[:, None] * rowf[None, :] + offy[:, None] * colf[None, :]) % IMG
    theta = phase.astype(jnp.float32) * (2.0 * math.pi / IMG)
    cosv = jnp.cos(theta)[None]
    sinv = jnp.sin(theta)[None]
    onehot = (groups[:, None] == jnp.arange(GROUPS, dtype=jnp.int32)[None, :]).astype(jnp.float32)
    ctf_rows = jnp.dot(onehot, ctf_table, precision=lax.Precision.HIGHEST)[:, None, :]
    real = images[:, :freqs].astype(jnp.float32)[:, None, :]
    imag = images[:, freqs:].astype(jnp.float32)[:, None, :]
    shifted_real = ctf_rows * (real * cosv + imag * sinv)
    shifted_imag = ctf_rows * (imag * cosv - real * sinv)
    shifted = jnp.concatenate([shifted_real, shifted_imag], axis=2).astype(jnp.bfloat16)
    return shifted.reshape(images.shape[0] * SIDE * SIDE, 2 * freqs), onehot


def reference(particle_images, particle_groups, live_counts, ctf_table, projections):
    width = K * ROTS
    shifts = SIDE * SIDE
    stack = projections.astype(jnp.float32).reshape(TWOF, width)
    ctf_square = jnp.concatenate([ctf_table, ctf_table], axis=1) ** 2
    power = jnp.dot(ctf_square, stack * stack, precision=lax.Precision.HIGHEST)
    images = particle_images.reshape(SHARDS, NP_DEV, TWOF)
    groups = particle_groups.reshape(SHARDS, NP_DEV)

    def one_shard(carry, inputs):
        sums, weights = carry
        block, block_groups, count = inputs
        shifted, onehot = build_shifted(block, block_groups, ctf_table)
        scores = jnp.dot(shifted.astype(jnp.float32), stack).reshape(NP_DEV, shifts, width)
        power_rows = jnp.dot(onehot, power, precision=lax.Precision.HIGHEST)
        loglik = scores - 0.5 * power_rows[:, None, :]
        top = jnp.max(loglik, axis=(1, 2))
        total = jnp.sum(jnp.exp(loglik - top[:, None, None]), axis=(1, 2))
        live = jnp.arange(NP_DEV, dtype=jnp.int32) < count
        posterior = jnp.exp(loglik - top[:, None, None]) / total[:, None, None]
        posterior = jnp.where(live[:, None, None], posterior, jnp.float32(0.0))
        evidence = jnp.where(live, top + jnp.log(total), jnp.float32(0.0))
        low = posterior.astype(jnp.bfloat16).astype(jnp.float32).reshape(NP_DEV * shifts, width)
        sums = sums + jnp.dot(low.T, shifted.astype(jnp.float32))
        weights = weights + jnp.dot(onehot.T, jnp.sum(posterior, axis=1), precision=lax.Precision.HIGHEST)
        return (sums, weights), evidence

    init = (jnp.zeros((width, TWOF), jnp.float32), jnp.zeros((GROUPS, width), jnp.float32))
    (sums, weights), evidence = lax.scan(one_shard, init, (images, groups, live_counts))
    insertions = sums.reshape(K, ROTS, TWOF)
    class_weights = jnp.transpose(weights.reshape(GROUPS, K, ROTS), (1, 0, 2))
    return insertions, class_weights, evidence.reshape(PARTICLES)
```

```python
import math

import jax
import jax.numpy as jnp
import numpy as np
from jax import lax
from jax.experimental import pallas as pl
from jax.experimental.pallas import tpu as pltpu
from jax.sharding import Mesh, PartitionSpec as P

IMG = 64
SIDE = 5
SHIFTS = SIDE * SIDE
HALF = SHIFTS // 2
GROUPS = 8
FREQS = IMG * IMG
TWOF = 2 * FREQS
LANE = 128
HIGHEST = lax.Precision.HIGHEST
F32 = jnp.float32
BF16 = jnp.bfloat16
BLOCKS = FREQS // (2 * LANE)
COLS = FREQS // 2


def shift_tables():
    index = np.arange(FREQS)
    shift = np.arange(HALF)
    offx = shift // SIDE - SIDE // 2
    offy = shift % SIDE - SIDE // 2
    phase = (offx[:, None] * (index // IMG)[None, :] + offy[:, None] * (index % IMG)[None, :]) % IMG
    theta = phase.astype(np.float32) * np.float32(2.0 * math.pi / IMG)
    return np.cos(theta.astype(np.float64)).astype(np.float32), np.sin(theta.astype(np.float64)).astype(np.float32)


def build_kernel(core_ref, re_ref, im_ref, hot_ref, ctf_ref, cos_ref, sin_ref, out_ref):
    npart = re_ref.shape[0]
    ctf = jnp.dot(hot_ref[...], ctf_ref[...], precision=HIGHEST, preferred_element_type=F32)
    for g in range(npart // 16):
        rows = slice(16 * g, 16 * g + 16)
        re = ctf[rows] * re_ref[rows, :].astype(F32)
        im = ctf[rows] * im_ref[rows, :].astype(F32)

        def put(s, real, imag):
            at = s * npart + 16 * g
            out_ref[0, 0, at : at + 16, :] = real.astype(BF16)
            out_ref[0, 1, at : at + 16, :] = imag.astype(BF16)

        put(HALF, re, im)
        for s in range(HALF):
            co = cos_ref[s : s + 1, :]
            si = sin_ref[s : s + 1, :]
            a, b, d, e = re * co, im * si, im * co, re * si
            put(s, a + b, d - e)
            put(SHIFTS - 1 - s, a - b, d + e)


def build_shifted(core, images, hot, ctf_table):
    npart = images.shape[0]
    cosv, sinv = shift_tables()

    def place(i, j, core):
        return 2 * j + (core[0] + i) % 2

    grid = pltpu.PrefetchScalarGridSpec(
        num_scalar_prefetch=1,
        grid=(2, BLOCKS),
        in_specs=[
            pl.BlockSpec((npart, LANE), lambda i, j, c: (0, place(i, j, c))),
            pl.BlockSpec((npart, LANE), lambda i, j, c: (0, 2 * BLOCKS + place(i, j, c))),
            pl.BlockSpec((npart, GROUPS), lambda i, j, c: (0, 0)),
            pl.BlockSpec((GROUPS, LANE), lambda i, j, c: (0, place(i, j, c))),
            pl.BlockSpec((HALF, LANE), lambda i, j, c: (0, place(i, j, c))),
            pl.BlockSpec((HALF, LANE), lambda i, j, c: (0, place(i, j, c))),
        ],
        out_specs=pl.BlockSpec((1, 2, npart * SHIFTS, LANE), lambda i, j, c: (i, 0, 0, j)),
    )
    return pl.pallas_call(
        build_kernel,
        grid_spec=grid,
        out_shape=jax.ShapeDtypeStruct((2, 2, npart * SHIFTS, COLS), BF16),
        cost_estimate=pl.CostEstimate(flops=12 * npart * SHIFTS * FREQS, bytes_accessed=4 * npart * SHIFTS * FREQS, transcendentals=0),
        name="build_shifted",
    )(core, images, images, hot, ctf_table, cosv, sinv)


def add_scores(shifted, proj, ctf_ref, acc_ref, power_ref):
    rows = acc_ref.shape[0]
    step = rows // 5
    weights = proj[...]

    for k in range(5):
        at = slice(k * step, k * step + step)
        acc_ref[at, :] += jnp.dot(shifted[0, 0, at, :], weights, preferred_element_type=F32)

    square = weights.astype(F32)
    square = square * square
    high = square.astype(BF16)
    low = (square - high.astype(F32)).astype(BF16)
    left = ctf_ref[0]
    left = left * left
    first = left.astype(BF16)
    rest = left - first.astype(F32)
    second = rest.astype(BF16)
    third = (rest - second.astype(F32)).astype(BF16)
    parts = jnp.concatenate([first.astype(F32), second.astype(F32), third.astype(F32)], axis=0).astype(BF16)
    both = jnp.dot(parts, high, preferred_element_type=F32) + jnp.dot(parts, low, preferred_element_type=F32)
    power_ref[...] += both[:GROUPS] + both[GROUPS : 2 * GROUPS] + both[2 * GROUPS :]


def first_kernel(core_ref, shifted_ref, proj_ref, ctf_ref, acc_ref, power_ref):
    @pl.when((pl.program_id(0) == 0) & (pl.program_id(1) == 0))
    def _():
        acc_ref[...] = jnp.zeros_like(acc_ref)
        power_ref[...] = jnp.zeros_like(power_ref)

    add_scores(shifted_ref, proj_ref, ctf_ref, acc_ref, power_ref)


def second_kernel(core_ref, shifted_ref, proj_ref, ctf_ref, acc0_ref, power0_ref, hot_ref, log_ref, stats_ref, power_ref):
    @pl.when((pl.program_id(0) == 0) & (pl.program_id(1) == 0))
    def _():
        log_ref[...] = acc0_ref[...]
        power_ref[...] = power0_ref[...]

    add_scores(shifted_ref, proj_ref, ctf_ref, log_ref, power_ref)

    @pl.when((pl.program_id(0) == pl.num_programs(0) - 1) & (pl.program_id(1) == pl.num_programs(1) - 1))
    def _():
        npart = hot_ref.shape[0]
        half = 0.5 * jnp.dot(hot_ref[...], power_ref[...], precision=HIGHEST, preferred_element_type=F32)
        best = None
        for s in range(SHIFTS):
            at = slice(s * npart, s * npart + npart)
            value = log_ref[at, :] - half
            log_ref[at, :] = value
            best = value if best is None else jnp.maximum(best, value)
        top = jnp.max(best, axis=1, keepdims=True)
        total = jnp.zeros_like(best)
        for s in range(SHIFTS):
            total = total + jnp.exp(log_ref[s * npart : s * npart + npart, :] - top)
        total = jnp.sum(total, axis=1, keepdims=True)
        lane = lax.broadcasted_iota(jnp.int32, (npart, LANE), 1)
        stats_ref[...] = jnp.where(lane == 0, top, total).T[:8, :]


def score_call(core, shifted, proj, ctf_parts, which, carried=None):
    rows = shifted.shape[2]
    width = proj.shape[1]
    npart = rows // SHIFTS
    depth = 1024
    steps = COLS // depth
    in_specs = [
        pl.BlockSpec((1, 1, rows, depth), lambda i, k, c: (which, i, 0, k)),
        pl.BlockSpec((depth, width), lambda i, k, c: (i * steps + k, 0)),
        pl.BlockSpec((1, GROUPS, depth), lambda i, k, c: ((c[0] + which) % 2, 0, k)),
    ]

    def whole(*shape):
        return pl.BlockSpec(shape, lambda i, k, c: (0,) * len(shape))

    args = [core, shifted, proj, ctf_parts]
    scratch = []
    if carried is None:
        kernel = first_kernel
        out_shape = [jax.ShapeDtypeStruct((rows, width), F32), jax.ShapeDtypeStruct((GROUPS, width), F32)]
        out_specs = [whole(rows, width), whole(GROUPS, width)]
    else:
        kernel = second_kernel
        in_specs += [whole(rows, width), whole(GROUPS, width), whole(npart, GROUPS)]
        args += list(carried)
        out_shape = [jax.ShapeDtypeStruct((rows, width), F32), jax.ShapeDtypeStruct((8, npart), F32)]
        out_specs = [whole(rows, width), whole(8, npart)]
        scratch = [pltpu.VMEM((GROUPS, width), F32)]
    return pl.pallas_call(
        kernel,
        grid_spec=pltpu.PrefetchScalarGridSpec(
            num_scalar_prefetch=1, grid=(2, steps), in_specs=in_specs, out_specs=out_specs, scratch_shapes=scratch
        ),
        out_shape=out_shape,
        cost_estimate=pl.CostEstimate(flops=2 * rows * width * FREQS, bytes_accessed=2 * rows * FREQS, transcendentals=0),
        compiler_params=pltpu.CompilerParams(vmem_limit_bytes=40 * 1024 * 1024),
        name="scores_first" if carried is None else "scores_second",
    )(*args)


def posterior_kernel(log_ref, stats_ref, live_ref, hot_ref, low_ref, weights_ref, evidence_ref, turn_ref):
    npart = hot_ref.shape[1]
    tops = stats_ref[:, 0, :]
    totals = stats_ref[:, 1, :]
    top = jnp.max(tops, axis=0, keepdims=True)
    total = jnp.sum(totals * jnp.exp(tops - top), axis=0, keepdims=True)
    live = live_ref[...]
    evidence_ref[...] = jnp.where(live > 0.0, top + jnp.log(total), 0.0)
    row = lax.broadcasted_iota(jnp.int32, (8, npart), 0)
    turn_ref[...] = jnp.where(row == 0, top, live / total).T
    col_top = turn_ref[:, 0:1]
    scale = turn_ref[:, 1:2]
    gathered = None
    for s in range(SHIFTS):
        at = slice(s * npart, s * npart + npart)
        posterior = jnp.exp(log_ref[at, :] - col_top) * scale
        low_ref[at, :] = posterior.astype(BF16)
        gathered = posterior if gathered is None else gathered + posterior
    weights_ref[...] = jnp.dot(hot_ref[...], gathered, precision=HIGHEST, preferred_element_type=F32)


def posterior_call(loglik, stats, live, hot_t):
    rows, width = loglik.shape
    npart = hot_t.shape[1]
    return pl.pallas_call(
        posterior_kernel,
        out_shape=[
            jax.ShapeDtypeStruct((rows, width), BF16),
            jax.ShapeDtypeStruct((GROUPS, width), F32),
            jax.ShapeDtypeStruct((1, npart), F32),
        ],
        scratch_shapes=[pltpu.VMEM((npart, 8), F32)],
        compiler_params=pltpu.CompilerParams(vmem_limit_bytes=16 * 1024 * 1024),
        name="posterior",
    )(loglik, stats, live, hot_t)


def insert_kernel(low_ref, shifted_ref, out_ref, turn_ref):
    @pl.when((pl.program_id(0) == 0) & (pl.program_id(1) == 0))
    def _():
        turn_ref[...] = low_ref[...].astype(F32).T.astype(BF16)

    sums = jnp.dot(turn_ref[...], shifted_ref[0, 0], preferred_element_type=F32)
    for b in range(out_ref.shape[0]):
        out_ref[b] = sums[:, b * LANE : b * LANE + LANE].astype(out_ref.dtype)


def insert_call(low, shifted, which, dtype):
    rows, width = low.shape
    depth = 512
    steps = COLS // depth
    return pl.pallas_call(
        insert_kernel,
        grid=(2, steps),
        in_specs=[
            pl.BlockSpec((rows, width), lambda i, k: (0, 0)),
            pl.BlockSpec((1, 1, rows, depth), lambda i, k: (which, i, 0, k)),
        ],
        out_specs=pl.BlockSpec((depth // LANE, width, LANE), lambda i, k: (i * steps + k, 0, 0)),
        out_shape=jax.ShapeDtypeStruct((2 * BLOCKS, width, LANE), dtype),
        scratch_shapes=[pltpu.VMEM((width, rows), BF16)],
        cost_estimate=pl.CostEstimate(flops=2 * rows * width * FREQS, bytes_accessed=2 * rows * FREQS, transcendentals=0),
        compiler_params=pltpu.CompilerParams(vmem_limit_bytes=40 * 1024 * 1024),
        name="insert_first" if which else "insert_second",
    )(low, shifted)


CHIPS = ("grp", "y", "zl")
SWAP = [(0, 1), (1, 0)]
SENT = BF16


def body(particle_images, particle_groups, live_counts, ctf_table, projections):
    core = lax.axis_index("core")
    core_arg = core.reshape(1).astype(jnp.int32)
    slots = particle_images.shape[0]
    images = lax.all_gather(particle_images, "core", axis=0, tiled=True)
    groups = lax.all_gather(particle_groups, "core", axis=0, tiled=True)
    counts = lax.all_gather(live_counts, "core", axis=0, tiled=True)
    npart = images.shape[0]
    mine = lax.dynamic_index_in_dim(projections, core, axis=1, keepdims=False)
    theirs = lax.dynamic_index_in_dim(projections, 1 - core, axis=1, keepdims=False)
    given = lax.ppermute(theirs, "core", SWAP)
    proj_own = lax.all_gather(mine, CHIPS, axis=0, tiled=True)
    proj_other = lax.all_gather(given, CHIPS, axis=0, tiled=True)

    group_row = jnp.arange(GROUPS, dtype=jnp.int32)
    hot = (groups[:, None] == group_row[None, :]).astype(F32)
    hot_t = (groups[None, :] == group_row[:, None]).astype(F32)
    slot = jnp.arange(npart, dtype=jnp.int32)
    live = (slot % slots < jnp.repeat(counts, slots)).astype(F32)[None, :]
    ctf_parts = ctf_table.reshape(GROUPS, BLOCKS, 2, LANE).transpose(2, 0, 1, 3).reshape(2, GROUPS, COLS)

    shifted = build_shifted(core_arg, images, hot, ctf_table)
    acc, power = score_call(core_arg, shifted, proj_own, ctf_parts, 0)
    loglik, stats = score_call(core_arg, shifted, proj_other, ctf_parts, 1, (acc, power, hot))
    stats = lax.all_gather(stats[:2], ("cls", "core"), axis=0)
    low, weights, evidence = posterior_call(loglik, stats, live, hot_t)

    sums_other = insert_call(low, shifted, 1, SENT)
    part_other = lax.psum_scatter(sums_other, CHIPS, scatter_dimension=0, tiled=True)
    sums_own = insert_call(low, shifted, 0, SENT)
    part_own = lax.psum_scatter(sums_own, CHIPS, scatter_dimension=0, tiled=True)
    part_other = lax.ppermute(part_other, "core", SWAP)
    own = part_own.reshape(1, -1, LANE).astype(F32)
    other = part_other.reshape(1, -1, LANE).astype(F32)
    insertions = jnp.where(core == 0, jnp.concatenate([own, other]), jnp.concatenate([other, own]))

    weights = lax.psum(weights, CHIPS)
    class_weights = lax.all_gather(weights, "core", axis=0)
    evidence = lax.dynamic_slice_in_dim(evidence[0], core * slots, slots)
    return insertions, class_weights, evidence


def solution(mesh):
    fine = Mesh(mesh.devices.reshape(4, 4, 4, 2, 2), ("cls", "grp", "y", "zl", "core"))
    shards = ("grp", "y", "zl", "core")
    return jax.shard_map(
        body,
        mesh=fine,
        in_specs=(P(shards, None), P(shards), P(shards), P(), P(shards, "cls", None)),
        out_specs=(P("cls", None, shards), P("cls", None, None), P(shards)),
        check_vma=False,
    )
```

```python
import math

import jax
import jax.numpy as jnp
import numpy as np
from jax import lax
from jax.experimental import pallas as pl
from jax.experimental.pallas import tpu as pltpu
from jax.sharding import Mesh, PartitionSpec as P

IMG = 64
SIDE = 5
SHIFTS = SIDE * SIDE
HALF = SHIFTS // 2
GROUPS = 8
FREQS = IMG * IMG
LANE = 128
SLOTS = 40
ROWS = SLOTS * SHIFTS + 8
WIDTH = 200
BLOCKS = 32
DEPTH = BLOCKS * LANE
HIGHEST = lax.Precision.HIGHEST
F32 = jnp.float32
BF16 = jnp.bfloat16
MIB = 2**20
VMEM = pl.BlockSpec(memory_space=pltpu.VMEM)
SMEM = pl.BlockSpec(memory_space=pltpu.SMEM)
SWAP = [(0, 1), (1, 0)]


def shift_tables():
    index = np.arange(FREQS)
    shift = np.arange(HALF)
    offx = shift // SIDE - SIDE // 2
    offy = shift % SIDE - SIDE // 2
    phase = (offx[:, None] * (index // IMG)[None, :] + offy[:, None] * (index % IMG)[None, :]) % IMG
    theta = (phase.astype(np.float32) * np.float32(2.0 * math.pi / IMG)).astype(np.float64)
    return np.cos(theta).astype(np.float32), np.sin(theta).astype(np.float32)


def call(kernel, name, out, args, limit, flops=0, moved=0):
    return pl.pallas_call(
        kernel,
        name=name,
        in_specs=[SMEM] + [VMEM] * (len(args) - 1),
        out_specs=jax.tree.map(lambda _: VMEM, out),
        out_shape=out,
        cost_estimate=pl.CostEstimate(flops=flops, bytes_accessed=moved, transcendentals=0),
        compiler_params=pltpu.CompilerParams(vmem_limit_bytes=limit * MIB),
    )(*args)


def shape(*dims, dtype=F32):
    return jax.ShapeDtypeStruct(dims, dtype)


def lanes(block):
    return pl.ds(pl.multiple_of(block * LANE, LANE), LANE)


def split_kernel(place, images, meta, kept, given):
    core = place[3]

    def turn(j, carry):
        kept[:, lanes(j)] = images[:, lanes(2 * j + core)]
        given[:, lanes(j)] = images[:, lanes(2 * j + 1 - core)]
        return carry

    lax.fori_loop(0, BLOCKS, turn, 0)
    kept[:, DEPTH:] = meta[...]
    given[:, DEPTH:] = meta[...]


def owner_block(place, p):
    later = p // 16
    first, second = (p % 16) // 4, p % 4
    dx = jnp.where(later == 0, first, second)
    dy = jnp.where(later == 0, second, first)
    return ((place[0] + dx) % 4) * 8 + ((place[1] + dy) % 4) * 2 + later


def build_kernel(place, images, ctf, cosv, sinv, out):
    core = place[3]
    group = images[:, DEPTH : DEPTH + 1].astype(F32)

    def turn(p, carry):
        j = owner_block(place, p)
        at = lanes(2 * (j % 16) + core)
        sign = jnp.where(j < 16, 1.0, -1.0).astype(F32)
        row = jnp.broadcast_to(ctf[0:1, at], (SLOTS, LANE))
        for g in range(1, GROUPS):
            row = jnp.where(group == float(g), ctf[g : g + 1, at], row)
        first = images[:, lanes(j)].astype(F32) * row
        second = images[:, lanes((j + 16) % 32)].astype(F32) * (row * sign)
        here = lanes(p)
        for s in range(HALF):
            a = first * cosv[s : s + 1, at]
            b = second * sinv[s : s + 1, at]
            out[2 * SLOTS * s : 2 * SLOTS * (s + 1), here] = jnp.concatenate([a + b, a - b], axis=0).astype(BF16)
        tail = jnp.concatenate([first, jnp.zeros((8, LANE), F32)], axis=0)
        out[2 * SLOTS * HALF : ROWS, here] = tail.astype(BF16)
        return carry

    lax.fori_loop(0, BLOCKS, turn, 0)


def hot_rows(meta):
    group = meta[:, 0:1].astype(F32)
    lane = lax.broadcasted_iota(jnp.int32, (SLOTS, GROUPS), 1).astype(F32)
    return jnp.where(group == lane, 1.0, 0.0).astype(F32)


def weigh_kernel(place, ctf, a0, a1, a2, a3, b0, b1, b2, b3, out, power):
    core = place[3]
    pieces_a = (a0, a1, a2, a3)
    pieces_b = (b0, b1, b2, b3)
    total = jnp.zeros((3 * GROUPS, WIDTH), F32)
    for q in range(8):
        for r in range(4):
            piece = pieces_a[r][q] if q < 4 else pieces_b[r][q - 4]
            p = 4 * q + r
            out[:, p * LANE : (p + 1) * LANE] = piece
    for q in range(8):
        left = []
        for r in range(4):
            j = owner_block(place, jnp.int32(4 * q + r))
            left.append(ctf[:, lanes(2 * (j % 16) + core)])
        left = jnp.concatenate(left, axis=1)
        left = left * left
        first = left.astype(BF16).astype(F32)
        rest = left - first
        second = rest.astype(BF16).astype(F32)
        parts = jnp.concatenate([first, second, rest - second], axis=0).astype(BF16)
        square = out[:, 512 * q : 512 * (q + 1)].astype(F32)
        square = square * square
        high = square.astype(BF16)
        low = (square - high.astype(F32)).astype(BF16)
        dims = (((1,), (1,)), ((), ()))
        total = total + lax.dot_general(parts, high, dims, preferred_element_type=F32)
        total = total + lax.dot_general(parts, low, dims, preferred_element_type=F32)
    power[...] = total[:GROUPS] + total[GROUPS : 2 * GROUPS] + total[2 * GROUPS :]


def score_kernel(place, weights, power, shifted_a, shifted_b, meta_a, meta_b, out_a, out_b):
    for shifted, meta, out in ((shifted_a, meta_a, out_a), (shifted_b, meta_b, out_b)):
        half = 0.5 * jnp.dot(hot_rows(meta[...]), power[...], precision=HIGHEST, preferred_element_type=F32)
        out[...] = lax.dot_general(
            shifted[...], weights[...], (((1,), (1,)), ((), ())), preferred_element_type=F32
        )
        for s in range(SHIFTS):
            out[SLOTS * s : SLOTS * (s + 1), :] -= half


def settle_kernel(place, mine_a, mine_b, theirs_a, theirs_b, log_a, log_b, stats):
    columns = []
    for mine, theirs, log in ((mine_a, theirs_a, log_a), (mine_b, theirs_b, log_b)):
        best = None
        for s in range(SHIFTS):
            at = slice(SLOTS * s, SLOTS * (s + 1))
            value = mine[at, :] + theirs[at, :]
            log[at, :] = value
            best = value if best is None else jnp.maximum(best, value)
        top = jnp.max(best, axis=1, keepdims=True)
        total = jnp.zeros_like(best)
        for s in range(SHIFTS):
            total = total + jnp.exp(log[SLOTS * s : SLOTS * (s + 1), :] - top)
        columns += [top, jnp.sum(total, axis=1, keepdims=True)]
    lane = lax.broadcasted_iota(jnp.int32, (SLOTS, LANE), 1)
    spread = jnp.where(lane == 0, columns[0], jnp.where(lane == 1, columns[1], jnp.where(lane == 2, columns[2], columns[3])))
    stats[...] = spread.T[:8, :]


def posterior_kernel(place, log_a, log_b, stats, meta_a, meta_b, low_a, low_b, weights, evidence, spare):
    parity = place[2]
    total_weights = jnp.zeros((GROUPS, WIDTH), F32)
    for k, (log, meta, low) in enumerate(((log_a, meta_a, low_a), (log_b, meta_b, low_b))):
        tops, totals = [], []
        for d in range(8):
            same = (parity == d % 2) == (k == 0)
            here = stats[d]
            tops.append(jnp.where(same, here[0:1], here[2:3]))
            totals.append(jnp.where(same, here[1:2], here[3:4]))
        tops = jnp.concatenate(tops, axis=0)
        totals = jnp.concatenate(totals, axis=0)
        top = jnp.max(tops, axis=0, keepdims=True)
        total = jnp.sum(totals * jnp.exp(tops - top), axis=0, keepdims=True)
        row = lax.broadcasted_iota(jnp.int32, (8, SLOTS), 0)
        columns = jnp.where(row == 0, top, jnp.where(row == 1, total, top + jnp.log(total))).T
        live = meta[:, 1:2].astype(F32)
        scale = live / columns[:, 1:2]
        if k == 0:
            known = jnp.where(live > 0.0, columns[:, 2:3], 0.0)
            evidence[...] = jnp.broadcast_to(known, (SLOTS, LANE)).T[:8, :]
        gathered = None
        for s in range(SHIFTS):
            at = slice(SLOTS * s, SLOTS * (s + 1))
            value = jnp.exp(log[at, :] - columns[:, 0:1]) * scale
            spare[at, :] = value
            gathered = value if gathered is None else gathered + value
        spare[SLOTS * SHIFTS :, :] = jnp.zeros((8, WIDTH), F32)
        low[...] = spare[...].T.astype(BF16)
        hot = hot_rows(meta[...])
        total_weights = total_weights + lax.dot_general(
            hot, gathered, (((0,), (0,)), ((), ())), precision=HIGHEST, preferred_element_type=F32
        )
    weights[...] = total_weights


def posterior_call(*args):
    low = shape(WIDTH, ROWS, dtype=BF16)
    out = [low, low, shape(GROUPS, WIDTH), shape(8, SLOTS)]
    return pl.pallas_call(
        posterior_kernel,
        name="posterior",
        in_specs=[SMEM] + [VMEM] * (len(args) - 1),
        out_specs=[VMEM] * 4,
        out_shape=out,
        scratch_shapes=[pltpu.VMEM((ROWS, WIDTH), F32)],
        compiler_params=pltpu.CompilerParams(vmem_limit_bytes=12 * MIB),
    )(*args)


def insert_kernel(q):
    def kernel(place, l0, l1, l2, l3, s0, s1, s2, s3, out_a, out_b):
        for out, start in ((out_a, q * 512), (out_b, 2048 + q * 512)):
            sums = None
            for low, shifted in ((l0, s0), (l1, s1), (l2, s2), (l3, s3)):
                part = jnp.dot(low[...], shifted[:, start : start + 512], preferred_element_type=F32)
                sums = part if sums is None else sums + part
            for r in range(4):
                out[r] = sums[:, r * LANE : (r + 1) * LANE].astype(out.dtype)

    return kernel


def take(value, axis, d, n=4):
    return lax.ppermute(value, axis, [(i, (i - d) % n) for i in range(n)])


def push(value, axis, d, n=4):
    return lax.ppermute(value, axis, [(i, (i + d) % n) for i in range(n)])


def body(particle_images, particle_groups, live_counts, ctf_table, projections):
    x, y, zl, core = (lax.axis_index(a) for a in ("grp", "y", "zl", "core"))
    place = jnp.stack([x, y, zl, core]).astype(jnp.int32)
    ring = ("cls", "zl")

    slot = jnp.arange(SLOTS, dtype=jnp.int32)
    live = slot < live_counts[0]
    lane = jnp.arange(LANE, dtype=jnp.int32)[None, :]
    meta = jnp.where(lane == 0, particle_groups[:, None], jnp.where(lane == 1, live.astype(jnp.int32)[:, None], 0)).astype(BF16)

    stacks = jnp.transpose(projections, (1, 2, 0))
    mine = lax.dynamic_index_in_dim(stacks, zl, axis=0, keepdims=False)
    theirs = lax.dynamic_index_in_dim(stacks, 1 - zl, axis=0, keepdims=False)
    given = lax.ppermute(theirs, "zl", SWAP)
    unit_a = jnp.where(zl == 0, mine, given)
    unit_b = jnp.where(zl == 0, given, mine)

    half = shape(SLOTS, DEPTH + LANE, dtype=BF16)
    kept, other = call(split_kernel, "split", [half, half], (place, particle_images, meta), 8)
    halves = [kept, lax.ppermute(other, "core", SWAP)]

    across_a = jnp.stack([unit_a] + [take(unit_a, "grp", d) for d in (1, 2, 3)])
    across_b = jnp.stack([unit_b] + [take(unit_b, "y", d) for d in (1, 2, 3)])
    next_kept = push(kept, ring, 1, 8)
    next_other = push(other, ring, 7, 8)
    halves += [next_kept, lax.ppermute(next_other, "core", SWAP)]
    all_a = [across_a] + [take(across_a, "y", d) for d in (1, 2, 3)]
    all_b = [across_b] + [take(across_b, "grp", d) for d in (1, 2, 3)]

    cosv, sinv = shift_tables()
    metas = [h[:, DEPTH:] for h in halves]
    shifted = [
        call(build_kernel, f"build_{i}", shape(ROWS, DEPTH, dtype=BF16), (place, h, ctf_table, cosv, sinv), 14, 6 * ROWS * DEPTH, 2 * ROWS * DEPTH)
        for i, h in enumerate(halves)
    ]
    weights, power = call(
        weigh_kernel, "weigh", [shape(WIDTH, DEPTH, dtype=BF16), shape(GROUPS, WIDTH)], (place, ctf_table, *all_a, *all_b), 12
    )
    score = shape(ROWS, WIDTH)
    flops = 4 * ROWS * WIDTH * DEPTH
    given = call(score_kernel, "score_given", [score, score], (place, weights, power, shifted[1], shifted[3], metas[1], metas[3]), 28, flops)
    taken = [lax.ppermute(g, "core", SWAP) for g in given]
    own = call(score_kernel, "score_own", [score, score], (place, weights, power, shifted[0], shifted[2], metas[0], metas[2]), 28, flops)
    log_a, log_b, stats = call(settle_kernel, "settle", [score, score, shape(8, SLOTS)], (place, *own, *taken), 16)
    stats = lax.all_to_all(jnp.broadcast_to(stats[None], (8, 8, SLOTS)), ring, 0, 0, tiled=True)
    low_a, low_b, counted, evidence = posterior_call(place, log_a, log_b, stats, metas[0], metas[2])
    low = [low_a, lax.ppermute(low_a, "core", SWAP), low_b, lax.ppermute(low_b, "core", SWAP)]

    chunk = shape(4, WIDTH, LANE, dtype=BF16)
    flops = 2 * 4 * ROWS * WIDTH * 1024
    parts = {q: call(insert_kernel(q), f"insert_{q}", [chunk, chunk], (place, *low, *shifted), 42, flops) for q in (2, 1, 3, 0)}

    def total(own, axis, sent):
        got = [push(v, axis, q) for q, v in sent]
        return sum((g.astype(F32) for g in got), own.astype(F32))

    sum_a = total(parts[0][0], "grp", [(q, parts[q][0]) for q in (2, 1, 3)])
    sum_b = total(parts[0][1], "y", [(q, parts[q][1]) for q in (2, 1, 3)])
    out_a = total(sum_a[0], "y", [(q, sum_a[q].astype(BF16)) for q in (2, 1, 3)])
    out_b = total(sum_b[0], "grp", [(q, sum_b[q].astype(BF16)) for q in (2, 1, 3)])
    stay = jnp.where(zl == 0, out_a, out_b)
    leave = jnp.where(zl == 0, out_b, out_a)
    came = lax.ppermute(leave, "zl", SWAP)
    insertions = jnp.stack([jnp.where(zl == 0, stay, came), jnp.where(zl == 0, came, stay)])

    everyone = lax.all_gather(counted, ("grp", "y", "core", "zl"), axis=0)
    class_weights = jnp.sum(everyone.reshape(32, 2, GROUPS, WIDTH), axis=0)
    return insertions, class_weights, evidence[0]


def solution(mesh):
    fine = Mesh(mesh.devices.reshape(4, 4, 4, 2, 2), ("cls", "grp", "y", "zl", "core"))
    shards = ("grp", "y", "zl", "core")
    return jax.shard_map(
        body,
        mesh=fine,
        in_specs=(P(shards, None), P(shards), P(shards), P(), P(shards, "cls", None)),
        out_specs=(P("cls", None, shards), P("cls", None, None), P(shards)),
        check_vma=False,
    )
```

```python
import math

import jax
import jax.numpy as jnp
import numpy as np
from jax import lax
from jax.experimental import pallas as pl
from jax.experimental.pallas import tpu as pltpu
from jax.sharding import Mesh, PartitionSpec as P

IMG = 64
SIDE = 5
SHIFTS = SIDE * SIDE
HALF = SHIFTS // 2
GROUPS = 8
FREQS = IMG * IMG
LANE = 128
SLOTS = 40
ROWS = 1024
WIDTH = 200
WIDE = 256
TALL = WIDTH + 16
BLOCKS = 32
DEPTH = BLOCKS * LANE
HIGHEST = lax.Precision.HIGHEST
F32 = jnp.float32
BF16 = jnp.bfloat16
MIB = 2**20
VMEM = pl.BlockSpec(memory_space=pltpu.VMEM)
SMEM = pl.BlockSpec(memory_space=pltpu.SMEM)
SWAP = [(0, 1), (1, 0)]


def shift_tables():
    index = np.arange(FREQS)
    shift = np.arange(HALF)
    offx = shift // SIDE - SIDE // 2
    offy = shift % SIDE - SIDE // 2
    phase = (offx[:, None] * (index // IMG)[None, :] + offy[:, None] * (index % IMG)[None, :]) % IMG
    theta = (phase.astype(np.float32) * np.float32(2.0 * math.pi / IMG)).astype(np.float64)
    return np.cos(theta).astype(np.float32), np.sin(theta).astype(np.float32)


def call(kernel, name, out, args, limit, flops=0, moved=0):
    return pl.pallas_call(
        kernel,
        name=name,
        in_specs=[SMEM] + [VMEM] * (len(args) - 1),
        out_specs=jax.tree.map(lambda _: VMEM, out),
        out_shape=out,
        cost_estimate=pl.CostEstimate(flops=flops, bytes_accessed=moved, transcendentals=0),
        compiler_params=pltpu.CompilerParams(vmem_limit_bytes=limit * MIB),
    )(*args)


def shape(*dims, dtype=F32):
    return jax.ShapeDtypeStruct(dims, dtype)


def lanes(block):
    return pl.ds(pl.multiple_of(block * LANE, LANE), LANE)


def cut(value):
    first = value.astype(BF16)
    rest = value - first.astype(F32)
    second = rest.astype(BF16)
    return first, second, (rest - second.astype(F32)).astype(BF16)


def split_kernel(place, images, meta, ctf, kept, given, parts):
    core = place[3]
    for i, part in enumerate(cut(ctf[...])):
        parts[16 * i : 16 * i + 16, :] = jnp.concatenate([part.astype(F32), jnp.zeros((8, FREQS), F32)], axis=0).astype(BF16)

    def turn(j, carry):
        kept[:, lanes(j)] = images[:, lanes(2 * j + core)]
        given[:, lanes(j)] = images[:, lanes(2 * j + 1 - core)]
        return carry

    lax.fori_loop(0, BLOCKS, turn, 0)
    kept[:, DEPTH:] = meta[...]
    given[:, DEPTH:] = meta[...]


def owner_block(place, p):
    later = p // 16
    first, second = (p % 16) // 4, p % 4
    dx = jnp.where(later == 0, first, second)
    dy = jnp.where(later == 0, second, first)
    return ((place[0] + dx) % 4) * 8 + ((place[1] + dy) % 4) * 2 + later


def build_kernel(place, images, parts, cosv, sinv, out, token, rows):
    core = place[3]
    group = images[:, DEPTH : DEPTH + 1].astype(F32)
    lane = lax.broadcasted_iota(jnp.int32, (SLOTS, 48), 1)
    hot = jnp.where((group == (lane % 16).astype(F32)) & (lane % 16 < GROUPS), 1.0, 0.0).astype(BF16)
    rows[...] = jnp.dot(hot, parts[...], preferred_element_type=F32)

    def turn(p, carry):
        j = owner_block(place, p)
        at = lanes(2 * (j % 16) + core)
        sign = jnp.where(j < 16, 1.0, -1.0).astype(F32)
        row = rows[:, at]
        first = images[:, lanes(j)].astype(F32) * row
        second = images[:, lanes((j + 16) % 32)].astype(F32) * (row * sign)
        here = lanes(p)
        for s in range(HALF):
            a = first * cosv[s : s + 1, at]
            b = second * sinv[s : s + 1, at]
            out[2 * SLOTS * s : 2 * SLOTS * (s + 1), here] = jnp.concatenate([a + b, a - b], axis=0).astype(BF16)
        tail = jnp.concatenate([first, jnp.zeros((ROWS - SLOTS * SHIFTS, LANE), F32)], axis=0)
        out[2 * SLOTS * HALF : ROWS, here] = tail.astype(BF16)
        return carry

    lax.fori_loop(0, BLOCKS, turn, 0, unroll=2)
    token[...] = jnp.zeros_like(token)


def build_call(place, images, parts, cosv, sinv, name):
    return pl.pallas_call(
        build_kernel,
        name=name,
        in_specs=[SMEM] + [VMEM] * 4,
        out_specs=[VMEM, VMEM],
        out_shape=[shape(ROWS, DEPTH, dtype=BF16), shape(8, LANE)],
        scratch_shapes=[pltpu.VMEM((SLOTS, FREQS), F32)],
        cost_estimate=pl.CostEstimate(flops=6 * 10**9, bytes_accessed=2 * ROWS * DEPTH, transcendentals=0),
        compiler_params=pltpu.CompilerParams(vmem_limit_bytes=10 * MIB),
    )(place, images, parts, cosv, sinv)


def hot_rows(meta):
    group = meta[:, 0:1].astype(F32)
    lane = lax.broadcasted_iota(jnp.int32, (SLOTS, GROUPS), 1).astype(F32)
    return jnp.where(group == lane, 1.0, 0.0).astype(F32)


def weigh_kernel(place, ctf, t0, t1, t2, t3, a0, a1, a2, a3, b0, b1, b2, b3, out, power):
    core = place[3]
    pieces_a = (a0, a1, a2, a3)
    pieces_b = (b0, b1, b2, b3)
    total = jnp.zeros((3 * GROUPS, WIDE), F32)
    for q in range(8):
        for r in range(4):
            piece = pieces_a[r][q] if q < 4 else pieces_b[r][q - 4]
            p = 4 * q + r
            out[:WIDTH, p * LANE : (p + 1) * LANE] = piece
    out[WIDTH - 8 :, :] = jnp.concatenate([out[WIDTH - 8 : WIDTH, :], jnp.zeros((WIDE - WIDTH, DEPTH), BF16)], axis=0)
    for q in range(8):
        left = []
        for r in range(4):
            j = owner_block(place, jnp.int32(4 * q + r))
            left.append(ctf[:, lanes(2 * (j % 16) + core)])
        left = jnp.concatenate(left, axis=1)
        left = left * left
        parts = jnp.concatenate([part.astype(F32) for part in cut(left)], axis=0).astype(BF16)
        square = out[:, 512 * q : 512 * (q + 1)].astype(F32)
        square = square * square
        high = square.astype(BF16)
        low = (square - high.astype(F32)).astype(BF16)
        dims = (((1,), (1,)), ((), ()))
        total = total + lax.dot_general(parts, high, dims, preferred_element_type=F32)
        total = total + lax.dot_general(parts, low, dims, preferred_element_type=F32)
    power[...] = total[:GROUPS] + total[GROUPS : 2 * GROUPS] + total[2 * GROUPS :]


def score_kernel(place, weights, power, shifted_a, shifted_b, meta_a, meta_b, out_a, out_b):
    for shifted, meta, out in ((shifted_a, meta_a, out_a), (shifted_b, meta_b, out_b)):
        half = 0.5 * jnp.dot(hot_rows(meta[...]), power[...], precision=HIGHEST, preferred_element_type=F32)
        out[...] = lax.dot_general(
            shifted[...], weights[...], (((1,), (1,)), ((), ())), preferred_element_type=F32
        )
        for s in range(SHIFTS):
            out[SLOTS * s : SLOTS * (s + 1), :] -= half


def settle_kernel(place, mine_a, mine_b, theirs_a, theirs_b, log_a, log_b, stats):
    columns = []
    for mine, theirs, log in ((mine_a, theirs_a, log_a), (mine_b, theirs_b, log_b)):
        best = None
        for s in range(SHIFTS):
            at = slice(SLOTS * s, SLOTS * (s + 1))
            value = mine[at, :WIDTH] + theirs[at, :WIDTH]
            log[at, :] = value
            best = value if best is None else jnp.maximum(best, value)
        top = jnp.max(best, axis=1, keepdims=True)
        total = jnp.zeros_like(best)
        for s in range(SHIFTS):
            total = total + jnp.exp(log[SLOTS * s : SLOTS * (s + 1), :] - top)
        columns += [top, jnp.sum(total, axis=1, keepdims=True)]
    lane = lax.broadcasted_iota(jnp.int32, (SLOTS, LANE), 1)
    spread = jnp.where(lane == 0, columns[0], jnp.where(lane == 1, columns[1], jnp.where(lane == 2, columns[2], columns[3])))
    stats[...] = spread.T[:8, :]


def posterior_kernel(place, log_a, log_b, stats, meta_a, meta_b, low_a, low_b, weights, evidence, spare):
    parity = place[2]
    total_weights = jnp.zeros((GROUPS, WIDTH), F32)
    for k, (log, meta, low) in enumerate(((log_a, meta_a, low_a), (log_b, meta_b, low_b))):
        tops, totals = [], []
        for d in range(8):
            same = (parity == d % 2) == (k == 0)
            here = stats[d]
            tops.append(jnp.where(same, here[0:1], here[2:3]))
            totals.append(jnp.where(same, here[1:2], here[3:4]))
        tops = jnp.concatenate(tops, axis=0)
        totals = jnp.concatenate(totals, axis=0)
        top = jnp.max(tops, axis=0, keepdims=True)
        total = jnp.sum(totals * jnp.exp(tops - top), axis=0, keepdims=True)
        row = lax.broadcasted_iota(jnp.int32, (8, SLOTS), 0)
        columns = jnp.where(row == 0, top, jnp.where(row == 1, total, top + jnp.log(total))).T
        live = meta[:, 1:2].astype(F32)
        scale = live / columns[:, 1:2]
        if k == 0:
            known = jnp.where(live > 0.0, columns[:, 2:3], 0.0)
            evidence[...] = jnp.broadcast_to(known, (SLOTS, LANE)).T[:8, :]
        gathered = None
        for s in range(SHIFTS):
            at = slice(SLOTS * s, SLOTS * (s + 1))
            value = jnp.exp(log[at, :] - columns[:, 0:1]) * scale
            spare[at, :] = value
            gathered = value if gathered is None else gathered + value
        spare[SLOTS * SHIFTS :, :] = jnp.zeros((ROWS - SLOTS * SHIFTS, WIDTH), F32)
        low[...] = spare[...].T.astype(BF16)
        hot = hot_rows(meta[...])
        total_weights = total_weights + lax.dot_general(
            hot, gathered, (((0,), (0,)), ((), ())), precision=HIGHEST, preferred_element_type=F32
        )
    weights[...] = jnp.concatenate([total_weights, jnp.zeros((GROUPS, WIDE - WIDTH), F32)], axis=1)


def posterior_call(*args):
    low = shape(WIDTH, ROWS, dtype=BF16)
    out = [low, low, shape(GROUPS, WIDE), shape(8, SLOTS)]
    return pl.pallas_call(
        posterior_kernel,
        name="posterior",
        in_specs=[SMEM] + [VMEM] * (len(args) - 1),
        out_specs=[VMEM] * 4,
        out_shape=out,
        scratch_shapes=[pltpu.VMEM((ROWS, WIDTH), F32)],
        compiler_params=pltpu.CompilerParams(vmem_limit_bytes=10 * MIB),
    )(*args)


def insert_kernel(q):
    def kernel(place, counted, other, l0, l1, l2, l3, s0, s1, s2, s3, out_a, out_b):
        low = jnp.concatenate([l0[...], l1[...], l2[...], l3[...]], axis=1)
        for out, start in ((out_a, q * 512), (out_b, 2048 + q * 512)):
            for n in (0, 2):
                at = slice(start + LANE * n, start + LANE * (n + 2))
                shifted = jnp.concatenate([s0[:, at], s1[:, at], s2[:, at], s3[:, at]], axis=0)
                sums = jnp.dot(low, shifted, preferred_element_type=F32)
                for r in range(2):
                    out[n + r, :WIDTH, :] = sums[:, r * LANE : (r + 1) * LANE].astype(BF16)
        both = counted[...] + other[...]
        both = jnp.concatenate([both[:, :LANE], both[:, LANE:]], axis=0).astype(BF16)
        for n in range(4):
            out_a[n, WIDTH:, :] = both

    return kernel


def take(value, axis, d, n=4):
    return lax.ppermute(value, axis, [(i, (i - d) % n) for i in range(n)])


def push(value, axis, d, n=4):
    return lax.ppermute(value, axis, [(i, (i + d) % n) for i in range(n)])


def body(particle_images, particle_groups, live_counts, ctf_table, projections):
    x, y, zl, core = (lax.axis_index(a) for a in ("grp", "y", "zl", "core"))
    place = jnp.stack([x, y, zl, core]).astype(jnp.int32)
    ring = ("cls", "zl")

    slot = jnp.arange(SLOTS, dtype=jnp.int32)
    live = slot < live_counts[0]
    lane = jnp.arange(LANE, dtype=jnp.int32)[None, :]
    meta = jnp.where(lane == 0, particle_groups[:, None], jnp.where(lane == 1, live.astype(jnp.int32)[:, None], 0)).astype(BF16)

    stacks = jnp.transpose(projections, (1, 2, 0))
    mine = lax.dynamic_index_in_dim(stacks, zl, axis=0, keepdims=False)
    theirs = lax.dynamic_index_in_dim(stacks, 1 - zl, axis=0, keepdims=False)
    given = lax.ppermute(theirs, "zl", SWAP)
    unit_a = jnp.where(zl == 0, mine, given)
    unit_b = jnp.where(zl == 0, given, mine)

    half = shape(SLOTS, DEPTH + LANE, dtype=BF16)
    kept, other, parts = call(
        split_kernel, "split", [half, half, shape(48, FREQS, dtype=BF16)], (place, particle_images, meta, ctf_table), 8
    )
    halves = [kept, lax.ppermute(other, "core", SWAP)]

    across_a = jnp.stack([unit_a] + [take(unit_a, "grp", d) for d in (1, 2, 3)])
    across_b = jnp.stack([unit_b] + [take(unit_b, "y", d) for d in (1, 2, 3)])
    next_kept = push(kept, ring, 1, 8)
    next_other = push(other, ring, 7, 8)
    halves += [next_kept, lax.ppermute(next_other, "core", SWAP)]
    all_a = [across_a] + [take(across_a, "y", d) for d in (1, 2, 3)]
    all_b = [across_b] + [take(across_b, "grp", d) for d in (1, 2, 3)]

    cosv, sinv = shift_tables()
    metas = [h[:, DEPTH:] for h in halves]
    built = [build_call(place, h, parts, cosv, sinv, f"build_{i}") for i, h in enumerate(halves)]
    shifted = [b[0] for b in built]
    tokens = [b[1] for b in built]
    weights, power = call(
        weigh_kernel,
        "weigh",
        [shape(WIDE, DEPTH, dtype=BF16), shape(GROUPS, WIDE)],
        (place, ctf_table, *tokens, *all_a, *all_b),
        8,
    )
    score = shape(ROWS, WIDE)
    flops = 4 * ROWS * WIDE * DEPTH
    given = call(score_kernel, "score_given", [score, score], (place, weights, power, shifted[1], shifted[3], metas[1], metas[3]), 8, flops)
    taken = [lax.ppermute(g, "core", SWAP) for g in given]
    own = call(score_kernel, "score_own", [score, score], (place, weights, power, shifted[0], shifted[2], metas[0], metas[2]), 8, flops)
    log = shape(ROWS, WIDTH)
    log_a, log_b, stats = call(settle_kernel, "settle", [log, log, shape(8, SLOTS)], (place, *own, *taken), 8)
    stats = lax.all_to_all(jnp.broadcast_to(stats[None], (8, 8, SLOTS)), ring, 0, 0, tiled=True)
    low_a, low_b, counted, evidence = posterior_call(place, log_a, log_b, stats, metas[0], metas[2])
    low = [low_a, lax.ppermute(low_a, "core", SWAP), low_b, lax.ppermute(low_b, "core", SWAP)]
    counts = [counted, lax.ppermute(counted, "core", SWAP)]

    chunks = [shape(4, TALL, LANE, dtype=BF16), shape(4, WIDTH, LANE, dtype=BF16)]
    flops = 2 * 4 * ROWS * WIDE * 1024
    parts = {q: call(insert_kernel(q), f"insert_{q}", chunks, (place, *counts, *low, *shifted), 8, flops) for q in (2, 1, 3, 0)}

    def total(own, axis, sent):
        got = [push(v, axis, q) for q, v in sent]
        return sum((g.astype(F32) for g in got), own.astype(F32))

    sum_a = total(parts[0][0], "grp", [(q, parts[q][0]) for q in (2, 1, 3)])
    sum_b = total(parts[0][1], "y", [(q, parts[q][1]) for q in (2, 1, 3)])
    out_a = total(sum_a[0], "y", [(q, sum_a[q].astype(BF16)) for q in (2, 1, 3)])
    out_b = total(sum_b[0], "grp", [(q, sum_b[q].astype(BF16)) for q in (2, 1, 3)])
    tally, out_a = out_a[WIDTH:], out_a[:WIDTH]
    stay = jnp.where(zl == 0, out_a, out_b)
    leave = jnp.where(zl == 0, out_b, out_a)
    came = lax.ppermute(jnp.concatenate([leave, tally]), "zl", SWAP)
    came, tally_came = came[:WIDTH], came[WIDTH:]
    insertions = jnp.stack([jnp.where(zl == 0, stay, came), jnp.where(zl == 0, came, stay)])

    def table(rows):
        return jnp.concatenate([rows[:GROUPS], rows[GROUPS:]], axis=1)[:, :WIDTH]

    here, there = table(tally), table(tally_came)
    class_weights = jnp.stack([jnp.where(zl == 0, here, there), jnp.where(zl == 0, there, here)])
    return insertions, class_weights, evidence[0]


def solution(mesh):
    fine = Mesh(mesh.devices.reshape(4, 4, 4, 2, 2), ("cls", "grp", "y", "zl", "core"))
    shards = ("grp", "y", "zl", "core")
    return jax.shard_map(
        body,
        mesh=fine,
        in_specs=(P(shards, None), P(shards), P(shards), P(), P(shards, "cls", None)),
        out_specs=(P("cls", None, shards), P("cls", None, None), P(shards)),
        check_vma=False,
    )
```

```python
import math

import jax
import jax.numpy as jnp
import numpy as np
from jax import lax
from jax.experimental import pallas as pl
from jax.experimental.pallas import tpu as pltpu
from jax.sharding import Mesh, PartitionSpec as P

IMG = 64
SIDE = 5
SHIFTS = SIDE * SIDE
HALF = SHIFTS // 2
GROUPS = 8
FREQS = IMG * IMG
LANE = 128
SLOTS = 40
ROWS = 1024
WIDTH = 200
WIDE = 256
TALL = WIDTH + 8
COUNTED = SLOTS * SHIFTS
BLOCKS = 32
DEPTH = BLOCKS * LANE
HIGHEST = lax.Precision.HIGHEST
F32 = jnp.float32
BF16 = jnp.bfloat16
MIB = 2**20
VMEM = pl.BlockSpec(memory_space=pltpu.VMEM)
SMEM = pl.BlockSpec(memory_space=pltpu.SMEM)
SWAP = [(0, 1), (1, 0)]


def shift_tables():
    index = np.arange(FREQS)
    shift = np.arange(HALF)
    offx = shift // SIDE - SIDE // 2
    offy = shift % SIDE - SIDE // 2
    phase = (offx[:, None] * (index // IMG)[None, :] + offy[:, None] * (index % IMG)[None, :]) % IMG
    theta = (phase.astype(np.float32) * np.float32(2.0 * math.pi / IMG)).astype(np.float64)
    return np.cos(theta).astype(np.float32), np.sin(theta).astype(np.float32)


def call(kernel, name, out, args, limit, flops=0, moved=0):
    return pl.pallas_call(
        kernel,
        name=name,
        in_specs=[SMEM] + [VMEM] * (len(args) - 1),
        out_specs=jax.tree.map(lambda _: VMEM, out),
        out_shape=out,
        cost_estimate=pl.CostEstimate(flops=flops, bytes_accessed=moved, transcendentals=0),
        compiler_params=pltpu.CompilerParams(vmem_limit_bytes=limit * MIB),
    )(*args)


def shape(*dims, dtype=F32):
    return jax.ShapeDtypeStruct(dims, dtype)


def lanes(block):
    return pl.ds(pl.multiple_of(block * LANE, LANE), LANE)


def cut(value):
    first = value.astype(BF16)
    rest = value - first.astype(F32)
    second = rest.astype(BF16)
    return first, second, (rest - second.astype(F32)).astype(BF16)


def split_kernel(place, images, meta, ctf, kept, given, parts):
    core = place[3]
    for i, part in enumerate(cut(ctf[...])):
        parts[16 * i : 16 * i + 16, :] = jnp.concatenate([part.astype(F32), jnp.zeros((8, FREQS), F32)], axis=0).astype(BF16)

    def turn(j, carry):
        kept[:, lanes(j)] = images[:, lanes(2 * j + core)]
        given[:, lanes(j)] = images[:, lanes(2 * j + 1 - core)]
        return carry

    lax.fori_loop(0, BLOCKS, turn, 0)
    kept[:, DEPTH:] = meta[...]
    given[:, DEPTH:] = meta[...]


def owner_block(place, p):
    return ((place[0] + p // 8) % 4) * 8 + ((place[1] + p % 8 // 2) % 4) * 2 + p % 2


def build_kernel(place, images, parts, cosv, sinv, out, token, rows):
    core = place[3]
    group = images[:, DEPTH : DEPTH + 1].astype(F32)
    lane = lax.broadcasted_iota(jnp.int32, (SLOTS, 48), 1)
    hot = jnp.where((group == (lane % 16).astype(F32)) & (lane % 16 < GROUPS), 1.0, 0.0).astype(BF16)
    rows[...] = jnp.dot(hot, parts[...], preferred_element_type=F32)

    def turn(p, carry):
        j = owner_block(place, p)
        at = lanes(2 * (j % 16) + core)
        sign = jnp.where(j < 16, 1.0, -1.0).astype(F32)
        row = rows[:, at]
        first = images[:, lanes(j)].astype(F32) * row
        second = images[:, lanes((j + 16) % 32)].astype(F32) * (row * sign)
        here = lanes(p)
        for s in range(HALF):
            a = first * cosv[s : s + 1, at]
            b = second * sinv[s : s + 1, at]
            out[2 * SLOTS * s : 2 * SLOTS * (s + 1), here] = jnp.concatenate([a + b, a - b], axis=0).astype(BF16)
        tail = jnp.concatenate([first, jnp.zeros((ROWS - SLOTS * SHIFTS, LANE), F32)], axis=0)
        out[2 * SLOTS * HALF : ROWS, here] = tail.astype(BF16)
        return carry

    lax.fori_loop(0, BLOCKS, turn, 0, unroll=2)
    token[...] = jnp.zeros_like(token)


def build_call(place, images, parts, cosv, sinv, name):
    return pl.pallas_call(
        build_kernel,
        name=name,
        in_specs=[SMEM] + [VMEM] * 4,
        out_specs=[VMEM, VMEM],
        out_shape=[shape(ROWS, DEPTH, dtype=BF16), shape(8, LANE)],
        scratch_shapes=[pltpu.VMEM((SLOTS, FREQS), F32)],
        cost_estimate=pl.CostEstimate(flops=6 * 10**9, bytes_accessed=2 * ROWS * DEPTH, transcendentals=0),
        compiler_params=pltpu.CompilerParams(vmem_limit_bytes=10 * MIB),
    )(place, images, parts, cosv, sinv)


def hot_rows(meta):
    group = meta[:, 0:1].astype(F32)
    lane = lax.broadcasted_iota(jnp.int32, (SLOTS, GROUPS), 1).astype(F32)
    return jnp.where(group == lane, 1.0, 0.0).astype(F32)


def pair_kernel(place, stacks, came, out):
    parity = place[2]
    out[parity] = stacks[parity]
    out[1 - parity] = came[...]


def weigh_kernel(place, ctf, t0, t1, t2, t3, p0, p1, p2, p3, out, power):
    core = place[3]
    total = jnp.zeros((3 * GROUPS, WIDE), F32)
    for q, piece in enumerate((p0, p1, p2, p3)):
        for r in range(8):
            p = 8 * q + r
            out[:WIDTH, p * LANE : (p + 1) * LANE] = piece[r]
    out[WIDTH - 8 :, :] = jnp.concatenate([out[WIDTH - 8 : WIDTH, :], jnp.zeros((WIDE - WIDTH, DEPTH), BF16)], axis=0)
    for q in range(8):
        left = []
        for r in range(4):
            j = owner_block(place, jnp.int32(4 * q + r))
            left.append(ctf[:, lanes(2 * (j % 16) + core)])
        left = jnp.concatenate(left, axis=1)
        left = left * left
        parts = jnp.concatenate([part.astype(F32) for part in cut(left)], axis=0).astype(BF16)
        square = out[:, 512 * q : 512 * (q + 1)].astype(F32)
        square = square * square
        high = square.astype(BF16)
        low = (square - high.astype(F32)).astype(BF16)
        dims = (((1,), (1,)), ((), ()))
        total = total + lax.dot_general(parts, high, dims, preferred_element_type=F32)
        total = total + lax.dot_general(parts, low, dims, preferred_element_type=F32)
    power[...] = total[:GROUPS] + total[GROUPS : 2 * GROUPS] + total[2 * GROUPS :]


def score_kernel(place, weights, power, shifted_a, shifted_b, meta_a, meta_b, out):
    for k, (shifted, meta) in enumerate(((shifted_a, meta_a), (shifted_b, meta_b))):
        half = 0.5 * jnp.dot(hot_rows(meta[...]), power[...], precision=HIGHEST, preferred_element_type=F32)
        out[k] = lax.dot_general(shifted[...], weights[...], (((1,), (1,)), ((), ())), preferred_element_type=F32)
        for s in range(SHIFTS):
            out[k, SLOTS * s : SLOTS * (s + 1), :] -= half


def settle_kernel(place, mine, theirs, log, stats):
    columns = []
    for k in range(2):
        best = None
        for s in range(SHIFTS):
            at = slice(SLOTS * s, SLOTS * (s + 1))
            value = mine[k, at, :WIDTH] + theirs[k, at, :WIDTH]
            log[k, at, :] = value
            best = value if best is None else jnp.maximum(best, value)
        top = jnp.max(best, axis=1, keepdims=True)
        total = jnp.zeros_like(best)
        for s in range(SHIFTS):
            total = total + jnp.exp(log[k, SLOTS * s : SLOTS * (s + 1), :] - top)
        columns += [top, jnp.sum(total, axis=1, keepdims=True)]
    lane = lax.broadcasted_iota(jnp.int32, (SLOTS, LANE), 1)
    spread = jnp.where(lane == 0, columns[0], jnp.where(lane == 1, columns[1], jnp.where(lane == 2, columns[2], columns[3])))
    spread = jnp.concatenate([spread, jnp.zeros((LANE - SLOTS, LANE), F32)], axis=0).T[:8, :]
    for d in range(8):
        stats[d] = spread


def posterior_kernel(place, log, stats, meta_a, meta_b, low, evidence, spare):
    parity = place[2]
    counted = jnp.zeros((GROUPS, WIDTH), F32)
    for k, meta in ((1, meta_b), (0, meta_a)):
        tops, totals = [], []
        for d in range(8):
            same = (parity == d % 2) == (k == 0)
            here = stats[d, :, :SLOTS]
            tops.append(jnp.where(same, here[0:1], here[2:3]))
            totals.append(jnp.where(same, here[1:2], here[3:4]))
        tops = jnp.concatenate(tops, axis=0)
        totals = jnp.concatenate(totals, axis=0)
        top = jnp.max(tops, axis=0, keepdims=True)
        total = jnp.sum(totals * jnp.exp(tops - top), axis=0, keepdims=True)
        row = lax.broadcasted_iota(jnp.int32, (8, SLOTS), 0)
        columns = jnp.where(row == 0, top, jnp.where(row == 1, total, top + jnp.log(total))).T
        live = meta[:, 1:2].astype(F32)
        scale = live / columns[:, 1:2]
        if k == 0:
            known = jnp.where(live > 0.0, columns[:, 2:3], 0.0)
            evidence[...] = jnp.broadcast_to(known, (SLOTS, LANE)).T[:8, :]
        gathered = None
        for s in range(SHIFTS):
            at = slice(SLOTS * s, SLOTS * (s + 1))
            value = jnp.exp(log[k, at, :] - columns[:, 0:1]) * scale
            spare[at, :] = value
            gathered = value if gathered is None else gathered + value
        hot = hot_rows(meta[...])
        counted = counted + lax.dot_general(
            hot, gathered, (((0,), (0,)), ((), ())), precision=HIGHEST, preferred_element_type=F32
        )
        spare[SLOTS * SHIFTS :, :] = jnp.zeros((ROWS - SLOTS * SHIFTS, WIDTH), F32)
        if k == 0:
            first = counted.astype(BF16).astype(F32)
            spare[COUNTED : COUNTED + GROUPS, :] = first
            spare[COUNTED + GROUPS : COUNTED + 2 * GROUPS, :] = counted - first
        low[k] = spare[...].T.astype(BF16)


def posterior_call(*args):
    out = [shape(2, WIDTH, ROWS, dtype=BF16), shape(8, SLOTS)]
    return pl.pallas_call(
        posterior_kernel,
        name="posterior",
        in_specs=[SMEM] + [VMEM] * (len(args) - 1),
        out_specs=[VMEM] * 2,
        out_shape=out,
        scratch_shapes=[pltpu.VMEM((ROWS, WIDTH), F32)],
        compiler_params=pltpu.CompilerParams(vmem_limit_bytes=10 * MIB),
    )(*args)


def insert_kernel(q):
    def kernel(place, mine, theirs, s0, s1, s2, s3, out):
        low = jnp.concatenate([mine[0], theirs[0], mine[1], theirs[1]], axis=1)
        for n in range(0, 8, 2):
            at = slice(q * 1024 + LANE * n, q * 1024 + LANE * (n + 2))
            shifted = jnp.concatenate([s0[:, at], s1[:, at], s2[:, at], s3[:, at]], axis=0)
            sums = jnp.dot(low, shifted, preferred_element_type=F32)
            for r in range(2):
                out[n + r, :WIDTH, :] = sums[:, r * LANE : (r + 1) * LANE].astype(BF16)
        tail = slice(ROWS - LANE, ROWS)
        start = COUNTED - ROWS + LANE
        both = (mine[0, :, tail].astype(F32) + theirs[0, :, tail].astype(F32)).T
        both = both[start : start + GROUPS] + both[start + GROUPS : start + 2 * GROUPS]
        both = jnp.concatenate([both, jnp.zeros((GROUPS, WIDE - WIDTH), F32)], axis=1).astype(BF16)
        for n in range(8):
            out[n, WIDTH:, :] = both[:, LANE * (n % 2) : LANE * (n % 2 + 1)]

    return kernel


def take(value, axis, d, n=4):
    return lax.ppermute(value, axis, [(i, (i - d) % n) for i in range(n)])


def push(value, axis, d, n=4):
    return lax.ppermute(value, axis, [(i, (i + d) % n) for i in range(n)])


def body(particle_images, particle_groups, live_counts, ctf_table, projections):
    x, y, zl, core = (lax.axis_index(a) for a in ("grp", "y", "zl", "core"))
    place = jnp.stack([x, y, zl, core]).astype(jnp.int32)
    ring = ("cls", "zl")

    slot = jnp.arange(SLOTS, dtype=jnp.int32)
    live = slot < live_counts[0]
    lane = jnp.arange(LANE, dtype=jnp.int32)[None, :]
    meta = jnp.where(lane == 0, particle_groups[:, None], jnp.where(lane == 1, live.astype(jnp.int32)[:, None], 0)).astype(BF16)

    stacks = jnp.transpose(projections, (1, 2, 0))
    theirs = lax.dynamic_index_in_dim(stacks, 1 - zl, axis=0, keepdims=False)
    came = lax.ppermute(theirs, "zl", SWAP)
    unit = call(pair_kernel, "pair", shape(2, WIDTH, LANE, dtype=BF16), (place, stacks, came), 4)

    half = shape(SLOTS, DEPTH + LANE, dtype=BF16)
    kept, other, parts = call(
        split_kernel, "split", [half, half, shape(48, FREQS, dtype=BF16)], (place, particle_images, meta, ctf_table), 8
    )
    halves = [kept, lax.ppermute(other, "core", SWAP)]

    column = jnp.concatenate([unit] + [take(unit, "y", d) for d in (1, 2, 3)])
    next_kept = push(kept, ring, 1, 8)
    next_other = push(other, ring, 7, 8)
    halves += [next_kept, lax.ppermute(next_other, "core", SWAP)]
    pieces = [column] + [take(column, "grp", d) for d in (1, 2, 3)]

    cosv, sinv = shift_tables()
    metas = [h[:, DEPTH:] for h in halves]
    built = [build_call(place, h, parts, cosv, sinv, f"build_{i}") for i, h in enumerate(halves)]
    shifted = [b[0] for b in built]
    tokens = [b[1] for b in built]
    weights, power = call(
        weigh_kernel,
        "weigh",
        [shape(WIDE, DEPTH, dtype=BF16), shape(GROUPS, WIDE)],
        (place, ctf_table, *tokens, *pieces),
        8,
    )
    score = shape(2, ROWS, WIDE)
    flops = 4 * ROWS * WIDE * DEPTH
    given = call(score_kernel, "score_given", score, (place, weights, power, shifted[1], shifted[3], metas[1], metas[3]), 8, flops)
    taken = lax.ppermute(given, "core", SWAP)
    own = call(score_kernel, "score_own", score, (place, weights, power, shifted[0], shifted[2], metas[0], metas[2]), 8, flops)
    log, stats = call(settle_kernel, "settle", [shape(2, ROWS, WIDTH), shape(8, 8, LANE)], (place, own, taken), 8)
    stats = lax.all_to_all(stats, ring, 0, 0, tiled=True)
    low, evidence = posterior_call(place, log, stats, metas[0], metas[2])
    other_low = lax.ppermute(low, "core", SWAP)

    flops = 2 * 4 * ROWS * WIDE * 1024
    chunk = shape(8, TALL, LANE, dtype=BF16)
    parts = {q: call(insert_kernel(q), f"insert_{q}", chunk, (place, low, other_low, *shifted), 8, flops) for q in (2, 1, 3, 0)}

    def total(own, axis, sent):
        got = [push(v, axis, q) for q, v in sent]
        return sum((g.astype(F32) for g in got), own.astype(F32))

    row = total(parts[0], "grp", [(q, parts[q]) for q in (2, 1, 3)])
    cell = total(row[:2], "y", [(q, row[2 * q : 2 * q + 2].astype(BF16)) for q in (2, 1, 3)])
    tally = jnp.concatenate([cell[0, WIDTH:], cell[1, WIDTH:]])
    out_a, out_b = cell[0, :WIDTH], cell[1, :WIDTH]
    stay = jnp.where(zl == 0, out_a, out_b)
    leave = jnp.where(zl == 0, out_b, out_a)
    came = lax.ppermute(jnp.concatenate([leave, tally]), "zl", SWAP)
    came, tally_came = came[:WIDTH], came[WIDTH:]
    insertions = jnp.stack([jnp.where(zl == 0, stay, came), jnp.where(zl == 0, came, stay)])

    def table(rows):
        return jnp.concatenate([rows[:GROUPS], rows[GROUPS:]], axis=1)[:, :WIDTH]

    here, there = table(tally), table(tally_came)
    class_weights = jnp.stack([jnp.where(zl == 0, here, there), jnp.where(zl == 0, there, here)])
    return insertions, class_weights, evidence[0]


def solution(mesh):
    fine = Mesh(mesh.devices.reshape(4, 4, 4, 2, 2), ("cls", "grp", "y", "zl", "core"))
    shards = ("grp", "y", "zl", "core")
    return jax.shard_map(
        body,
        mesh=fine,
        in_specs=(P(shards, None), P(shards), P(shards), P(), P(shards, "cls", None)),
        out_specs=(P("cls", None, shards), P("cls", None, None), P(shards)),
        check_vma=False,
    )
```

```python
import math

import jax
import jax.numpy as jnp
import numpy as np
from jax import lax
from jax.experimental import pallas as pl
from jax.experimental.pallas import tpu as pltpu
from jax.sharding import Mesh, PartitionSpec as P

IMG = 64
SIDE = 5
SHIFTS = SIDE * SIDE
HALF = SHIFTS // 2
GROUPS = 8
FREQS = IMG * IMG
LANE = 128
SLOTS = 40
ROWS = 1024
WIDTH = 200
WIDE = 256
TALL = WIDTH + 8
COUNTED = SLOTS * SHIFTS
BLOCKS = 32
DEPTH = BLOCKS * LANE
CHUNK = DEPTH // 4
HIGHEST = lax.Precision.HIGHEST
F32 = jnp.float32
BF16 = jnp.bfloat16
MIB = 2**20
LIMIT = 4
VMEM = pl.BlockSpec(memory_space=pltpu.VMEM)
SMEM = pl.BlockSpec(memory_space=pltpu.SMEM)
SWAP = [(0, 1), (1, 0)]


def shift_tables():
    index = np.arange(FREQS)
    shift = np.arange(HALF)
    offx = shift // SIDE - SIDE // 2
    offy = shift % SIDE - SIDE // 2
    phase = (offx[:, None] * (index // IMG)[None, :] + offy[:, None] * (index % IMG)[None, :]) % IMG
    theta = (phase.astype(np.float32) * np.float32(2.0 * math.pi / IMG)).astype(np.float64)
    return np.cos(theta).astype(np.float32), np.sin(theta).astype(np.float32)


def call(kernel, name, out, args, limit, flops=0, moved=0):
    return pl.pallas_call(
        kernel,
        name=name,
        in_specs=[SMEM] + [VMEM] * (len(args) - 1),
        out_specs=jax.tree.map(lambda _: VMEM, out),
        out_shape=out,
        cost_estimate=pl.CostEstimate(flops=flops, bytes_accessed=moved, transcendentals=0),
        compiler_params=pltpu.CompilerParams(vmem_limit_bytes=limit * MIB),
    )(*args)


def shape(*dims, dtype=F32):
    return jax.ShapeDtypeStruct(dims, dtype)


def lanes(block):
    return pl.ds(pl.multiple_of(block * LANE, LANE), LANE)


def cut(value):
    first = value.astype(BF16)
    rest = value - first.astype(F32)
    second = rest.astype(BF16)
    return first, second, (rest - second.astype(F32)).astype(BF16)


def split_kernel(place, meta, unit, images, ctf, tables, kept, given, parts, turns, held, images_in, ctf_in, sems):
    core = place[3]
    copies = [
        pltpu.make_async_copy(source, target, sems.at[i])
        for i, (source, target) in enumerate(((images, images_in), (ctf, ctf_in), (tables, turns)))
    ]
    for copy in copies:
        copy.start()
    copies[1].wait()
    held[...] = ctf_in[...]
    for i, part in enumerate(cut(ctf_in[...])):
        parts[16 * i : 16 * i + 16, :] = jnp.concatenate([part.astype(F32), jnp.zeros((8, FREQS), F32)], axis=0).astype(BF16)
    copies[0].wait()

    def turn(j, carry):
        kept[:, lanes(j)] = images_in[:, lanes(2 * j + core)]
        given[:, lanes(j)] = images_in[:, lanes(2 * j + 1 - core)]
        return carry

    lax.fori_loop(0, BLOCKS, turn, 0)
    kept[:, DEPTH:] = meta[...]
    given[:, DEPTH:] = meta[...]
    copies[2].wait()


def split_call(place, meta, unit, images, ctf, tables):
    half = shape(SLOTS, DEPTH + LANE, dtype=BF16)
    anywhere = pl.BlockSpec(memory_space=pltpu.HBM)
    return pl.pallas_call(
        split_kernel,
        name="split",
        in_specs=[SMEM, VMEM, VMEM, anywhere, anywhere, anywhere],
        out_specs=[VMEM] * 5,
        out_shape=[half, half, shape(48, FREQS, dtype=BF16), shape(2 * HALF, FREQS), shape(GROUPS, FREQS)],
        scratch_shapes=[
            pltpu.VMEM((SLOTS, 2 * DEPTH), BF16),
            pltpu.VMEM((GROUPS, FREQS), F32),
            pltpu.SemaphoreType.DMA((3,)),
        ],
        compiler_params=pltpu.CompilerParams(vmem_limit_bytes=LIMIT * MIB),
    )(place, meta, unit, images, ctf, tables)


def owner_block(place, p):
    return (place[0] ^ (p // 8)) * 8 + (place[1] ^ (p % 8 // 2)) * 2 + (place[2] ^ (p % 2))


def build_kernel(place, after, images, parts, turns, out0, out1, out2, out3, token, rows):
    core = place[3]
    group = images[:, DEPTH : DEPTH + 1].astype(F32)
    lane = lax.broadcasted_iota(jnp.int32, (SLOTS, 48), 1)
    hot = jnp.where((group == (lane % 16).astype(F32)) & (lane % 16 < GROUPS), 1.0, 0.0).astype(BF16)
    rows[...] = jnp.dot(hot, parts[...], preferred_element_type=F32)
    for dx, out in enumerate((out0, out1, out2, out3)):

        def turn(p, carry):
            j = owner_block(place, 8 * dx + p)
            at = lanes(2 * (j % 16) + core)
            sign = jnp.where(j < 16, 1.0, -1.0).astype(F32)
            row = rows[:, at]
            first = images[:, lanes(j)].astype(F32) * row
            second = images[:, lanes(j ^ 16)].astype(F32) * (row * sign)
            here = lanes(p)
            for s in range(HALF):
                a = first * turns[s : s + 1, at]
                b = second * turns[HALF + s : HALF + s + 1, at]
                out[2 * SLOTS * s : 2 * SLOTS * (s + 1), here] = jnp.concatenate([a + b, a - b], axis=0).astype(BF16)
            tail = jnp.concatenate([first, jnp.zeros((ROWS - SLOTS * SHIFTS, LANE), F32)], axis=0)
            out[2 * SLOTS * HALF : ROWS, here] = tail.astype(BF16)
            return carry

        lax.fori_loop(0, 8, turn, 0, unroll=2)
    token[...] = jnp.zeros_like(token)


def build_call(place, after, images, parts, turns, name):
    return pl.pallas_call(
        build_kernel,
        name=name,
        in_specs=[SMEM] + [VMEM] * 4,
        out_specs=[VMEM] * 5,
        out_shape=[shape(ROWS, CHUNK, dtype=BF16)] * 4 + [shape(8, LANE)],
        scratch_shapes=[pltpu.VMEM((SLOTS, FREQS), F32)],
        cost_estimate=pl.CostEstimate(flops=6 * 10**9, bytes_accessed=2 * ROWS * DEPTH, transcendentals=0),
        compiler_params=pltpu.CompilerParams(vmem_limit_bytes=LIMIT * MIB),
    )(place, after, images, parts, turns)


def hot_rows(meta):
    group = meta[:, 0:1].astype(F32)
    lane = lax.broadcasted_iota(jnp.int32, (SLOTS, GROUPS), 1).astype(F32)
    return jnp.where(group == lane, 1.0, 0.0).astype(F32)


def stack_of(piece):
    return jnp.concatenate([piece[r] for r in range(8)], axis=1)


def weigh_kernel(place, ctf, t0, t1, t2, t3, p0, p1, p2, p3, power):
    core = place[3]
    total = jnp.zeros((3 * GROUPS, WIDTH), F32)
    for q, piece in enumerate((p0, p1, p2, p3)):
        left = jnp.concatenate([ctf[:, lanes(2 * (owner_block(place, 8 * q + r) % 16) + core)] for r in range(8)], axis=1)
        parts = jnp.concatenate([part.astype(F32) for part in cut(left * left)], axis=0).astype(BF16)
        square = stack_of(piece).astype(F32)
        square = square * square
        high = square.astype(BF16)
        low = (square - high.astype(F32)).astype(BF16)
        dims = (((1,), (1,)), ((), ()))
        total = total + lax.dot_general(parts, high, dims, preferred_element_type=F32)
        total = total + lax.dot_general(parts, low, dims, preferred_element_type=F32)
    power[...] = total[:GROUPS] + total[GROUPS : 2 * GROUPS] + total[2 * GROUPS :]


def score_kernel(place, power, meta_a, meta_b, p0, p1, p2, p3, *refs):
    out = refs[8]
    for k, meta in enumerate((meta_a, meta_b)):
        half = 0.5 * jnp.dot(hot_rows(meta[...]), power[...], precision=HIGHEST, preferred_element_type=F32)
        sums = None
        for dx, piece in enumerate((p0, p1, p2, p3)):
            part = lax.dot_general(
                refs[4 * k + dx][...], stack_of(piece), (((1,), (1,)), ((), ())), preferred_element_type=F32
            )
            sums = part if sums is None else sums + part
        spare = jnp.zeros((ROWS - SLOTS * SHIFTS, WIDTH), F32)
        out[k, :, :WIDTH] = sums - jnp.concatenate([half] * SHIFTS + [spare], axis=0)


def settle_kernel(place, mine, theirs, stats):
    columns = []
    for k in range(2):

        def value(s):
            at = slice(SLOTS * s, SLOTS * (s + 1))
            return mine[k, at, :WIDTH] + theirs[k, at, :WIDTH]

        best = value(0)
        for s in range(1, SHIFTS):
            best = jnp.maximum(best, value(s))
        top = jnp.max(best, axis=1, keepdims=True)
        total = jnp.exp(value(0) - top)
        for s in range(1, SHIFTS):
            total = total + jnp.exp(value(s) - top)
        columns += [top, jnp.sum(total, axis=1, keepdims=True)]
    lane = lax.broadcasted_iota(jnp.int32, (SLOTS, LANE), 1)
    spread = jnp.where(lane == 0, columns[0], jnp.where(lane == 1, columns[1], jnp.where(lane == 2, columns[2], columns[3])))
    spread = jnp.concatenate([spread, jnp.zeros((LANE - SLOTS, LANE), F32)], axis=0).T[:8, :]
    for d in range(8):
        stats[d] = spread


def posterior_kernel(place, mine, theirs, stats, meta_a, meta_b, low, evidence, spare):
    parity = place[2]
    counted = jnp.zeros((GROUPS, WIDTH), F32)
    for k, meta in ((1, meta_b), (0, meta_a)):
        tops, totals = [], []
        for d in range(8):
            same = (parity == d % 2) == (k == 0)
            here = stats[d, :, :SLOTS]
            tops.append(jnp.where(same, here[0:1], here[2:3]))
            totals.append(jnp.where(same, here[1:2], here[3:4]))
        tops = jnp.concatenate(tops, axis=0)
        totals = jnp.concatenate(totals, axis=0)
        top = jnp.max(tops, axis=0, keepdims=True)
        total = jnp.sum(totals * jnp.exp(tops - top), axis=0, keepdims=True)
        row = lax.broadcasted_iota(jnp.int32, (8, SLOTS), 0)
        columns = jnp.where(row == 0, top, jnp.where(row == 1, total, top + jnp.log(total))).T
        live = meta[:, 1:2].astype(F32)
        scale = live / columns[:, 1:2]
        if k == 0:
            known = jnp.where(live > 0.0, columns[:, 2:3], 0.0)
            evidence[...] = jnp.broadcast_to(known, (SLOTS, LANE)).T[:8, :]
        gathered = None
        for s in range(SHIFTS):
            at = slice(SLOTS * s, SLOTS * (s + 1))
            value = jnp.exp(mine[k, at, :WIDTH] + theirs[k, at, :WIDTH] - columns[:, 0:1]) * scale
            spare[at, :] = value
            gathered = value if gathered is None else gathered + value
        hot = hot_rows(meta[...])
        counted = counted + lax.dot_general(
            hot, gathered, (((0,), (0,)), ((), ())), precision=HIGHEST, preferred_element_type=F32
        )
        spare[SLOTS * SHIFTS :, :] = jnp.zeros((ROWS - SLOTS * SHIFTS, WIDTH), F32)
        if k == 0:
            first = counted.astype(BF16).astype(F32)
            spare[COUNTED : COUNTED + GROUPS, :] = first
            spare[COUNTED + GROUPS : COUNTED + 2 * GROUPS, :] = counted - first
        low[k] = spare[...].T.astype(BF16)


def posterior_call(*args):
    out = [shape(2, WIDTH, ROWS, dtype=BF16), shape(8, SLOTS)]
    return pl.pallas_call(
        posterior_kernel,
        name="posterior",
        in_specs=[SMEM] + [VMEM] * (len(args) - 1),
        out_specs=[VMEM] * 2,
        out_shape=out,
        scratch_shapes=[pltpu.VMEM((ROWS, WIDTH), F32)],
        compiler_params=pltpu.CompilerParams(vmem_limit_bytes=LIMIT * MIB),
    )(*args)


def insert_kernel(chunks):
    def kernel(place, after, mine, theirs, *refs):
        shifted_refs, outs = refs[: 4 * chunks], refs[4 * chunks :]
        low = jnp.concatenate([mine[0], theirs[0], mine[1], theirs[1]], axis=1)
        tail = slice(ROWS - LANE, ROWS)
        start = COUNTED - ROWS + LANE
        both = (mine[0, :, tail].astype(F32) + theirs[0, :, tail].astype(F32)).T
        both = both[start : start + GROUPS] + both[start + GROUPS : start + 2 * GROUPS]
        both = jnp.concatenate([both, jnp.zeros((GROUPS, WIDE - WIDTH), F32)], axis=1)
        outs[-1][...] = jnp.zeros((8, LANE), F32)
        for i, out in enumerate(outs[:-1]):
            columns = shifted_refs[4 * i : 4 * i + 4]
            for n in range(0, 8, 2):
                at = slice(LANE * n, LANE * (n + 2))
                shifted = jnp.concatenate([s[:, at] for s in columns], axis=0)
                sums = jnp.dot(low, shifted, preferred_element_type=F32)
                for r in range(2):
                    out[n + r, :WIDTH, :] = sums[:, r * LANE : (r + 1) * LANE].astype(out.dtype)
            for n in range(8):
                out[n, WIDTH:, :] = both[:, LANE * (n % 2) : LANE * (n % 2 + 1)].astype(out.dtype)

    return kernel


def absorb_kernel(place, own, far, out):
    out[...] = own[...] + far[...].astype(F32)


def gather_kernel(place, own, one, three, out):
    def total(n, rows):
        return own[n, rows] + one[n, rows].astype(F32) + three[n, rows].astype(F32)

    tail = slice(WIDTH, TALL)
    both = jnp.concatenate([total(0, tail), total(1, tail)], axis=0).astype(BF16)
    for n in range(8):
        to = (place[1] ^ (n // 2)) * 2 + (place[2] ^ (n % 2))
        out[to, :WIDTH] = total(n, slice(0, WIDTH)).astype(BF16)
        out[to, WIDTH:] = both


def finish_kernel(place, blocks, insertions, weights):
    for k in range(2):
        parts = [blocks[2 * n + k].astype(F32) for n in range(4)]
        sums = (parts[0] + parts[1]) + (parts[2] + parts[3])
        insertions[k] = sums[:WIDTH]
        weights[k] = jnp.concatenate([sums[WIDTH:TALL], sums[TALL:]], axis=1)[:, :WIDTH]


def swap(value, axis, d, n=4):
    return lax.ppermute(value, axis, [(i, i ^ d) for i in range(n)])


def body(particle_images, particle_groups, live_counts, ctf_table, projections):
    x, y, zl, core = (lax.axis_index(a) for a in ("grp", "y", "zl", "core"))
    place = jnp.stack([x, y, zl, core]).astype(jnp.int32)
    ring = ("cls", "zl")

    slot = jnp.arange(SLOTS, dtype=jnp.int32)
    live = slot < live_counts[0]
    lane = jnp.arange(LANE, dtype=jnp.int32)[None, :]
    meta = jnp.where(lane == 0, particle_groups[:, None], jnp.where(lane == 1, live.astype(jnp.int32)[:, None], 0)).astype(BF16)

    stacks = jnp.transpose(projections, (1, 2, 0))
    mine = lax.dynamic_index_in_dim(stacks, zl, axis=0)
    theirs = lax.dynamic_index_in_dim(stacks, 1 - zl, axis=0)
    unit = jnp.concatenate([mine, lax.ppermute(theirs, "zl", SWAP)])

    tables = np.concatenate(shift_tables())
    kept, other, parts, turns, ctf = split_call(place, meta, unit, particle_images, ctf_table, tables)
    halves = [kept, lax.ppermute(other, "core", SWAP)]

    column = jnp.concatenate([unit] + [swap(unit, "y", d) for d in (1, 2, 3)])
    next_kept = lax.ppermute(kept, "zl", SWAP)
    next_other = lax.ppermute(other, ring, [(i, (i + 1) % 8 if i % 2 else (i + 7) % 8) for i in range(8)])
    halves += [next_kept, lax.ppermute(next_other, "core", SWAP)]
    pieces = [column] + [swap(column, "grp", d) for d in (1, 2, 3)]

    metas = [h[:, DEPTH:] for h in halves]
    built = [build_call(place, column, h, parts, turns, f"build_{i}") for i, h in enumerate(halves)]
    shifted = [b[:4] for b in built]
    tokens = [b[4] for b in built]
    power = call(
        weigh_kernel,
        "weigh",
        shape(GROUPS, WIDTH),
        (place, ctf, *tokens, *pieces),
        LIMIT,
    )
    score = shape(2, ROWS, WIDE)
    flops = 4 * ROWS * WIDE * DEPTH
    given = call(score_kernel, "score_given", score, (place, power, metas[1], metas[3], *pieces, *shifted[1], *shifted[3]), LIMIT, flops)
    taken = lax.ppermute(given, "core", SWAP)
    kept_score = call(score_kernel, "score_own", score, (place, power, metas[0], metas[2], *pieces, *shifted[0], *shifted[2]), LIMIT, flops)
    stats = call(settle_kernel, "settle", shape(8, 8, LANE), (place, kept_score, taken), LIMIT)
    stats = lax.all_to_all(stats, ring, 0, 0, tiled=True)
    low, evidence = posterior_call(place, kept_score, taken, stats, metas[0], metas[2])
    other_low = lax.ppermute(low, "core", SWAP)

    flops = 2 * 4 * ROWS * WIDE * 1024
    chunk = shape(8, TALL, LANE, dtype=BF16)
    token = shape(8, LANE)

    def columns(*chunks):
        return [group[q] for q in chunks for group in shifted]

    send, after = call(insert_kernel(1), "insert_far", [chunk, token], (place, evidence, low, other_low, *columns(2)), LIMIT, flops)
    far = swap(send, "grp", 2)
    one, three, after = call(
        insert_kernel(2), "insert_near", [chunk, chunk, token], (place, after, low, other_low, *columns(1, 3)), LIMIT, 2 * flops
    )
    near = [swap(one, "grp", 1), swap(three, "grp", 3)]
    own, _ = call(insert_kernel(1), "insert_own", [shape(8, TALL, LANE), token], (place, after, low, other_low, *columns(0)), LIMIT, flops)
    own = call(absorb_kernel, "absorb", shape(8, TALL, LANE), (place, own, far), LIMIT)
    mixed = call(gather_kernel, "gather", shape(8, TALL + GROUPS, LANE, dtype=BF16), (place, own, *near), LIMIT)
    blocks = lax.all_to_all(mixed, ("y", "zl"), 0, 0, tiled=True)
    insertions, tally = call(finish_kernel, "finish", [shape(2, WIDTH, LANE), shape(2, GROUPS, WIDTH)], (place, blocks), LIMIT)
    return insertions, tally, evidence[0]


def solution(mesh):
    fine = Mesh(mesh.devices.reshape(4, 4, 4, 2, 2), ("cls", "grp", "y", "zl", "core"))
    shards = ("grp", "y", "zl", "core")
    return jax.shard_map(
        body,
        mesh=fine,
        in_specs=(P(shards, None), P(shards), P(shards), P(), P(shards, "cls", None)),
        out_specs=(P("cls", None, shards), P("cls", None, None), P(shards)),
        check_vma=False,
    )
```

```python
import math

import jax
import jax.numpy as jnp
import numpy as np
from jax import lax
from jax.experimental import pallas as pl
from jax.experimental.pallas import tpu as pltpu
from jax.sharding import Mesh, PartitionSpec as P

IMG = 64
SIDE = 5
SHIFTS = SIDE * SIDE
HALF = SHIFTS // 2
GROUPS = 8
FREQS = IMG * IMG
LANE = 128
SLOTS = 40
ROWS = 1024
WIDTH = 200
WIDE = 256
TALL = WIDTH + 8
COUNTED = SLOTS * SHIFTS
BLOCKS = 32
DEPTH = BLOCKS * LANE
CHUNK = DEPTH // 4
HIGHEST = lax.Precision.HIGHEST
F32 = jnp.float32
BF16 = jnp.bfloat16
MIB = 2**20
LIMIT = 4
VMEM = pl.BlockSpec(memory_space=pltpu.VMEM)
SMEM = pl.BlockSpec(memory_space=pltpu.SMEM)
SWAP = [(0, 1), (1, 0)]


def shift_tables():
    index = np.arange(FREQS)
    shift = np.arange(HALF)
    offx = shift // SIDE - SIDE // 2
    offy = shift % SIDE - SIDE // 2
    phase = (offx[:, None] * (index // IMG)[None, :] + offy[:, None] * (index % IMG)[None, :]) % IMG
    theta = (phase.astype(np.float32) * np.float32(2.0 * math.pi / IMG)).astype(np.float64)
    return np.cos(theta).astype(np.float32), np.sin(theta).astype(np.float32)


def call(kernel, name, out, args, limit, flops=0, moved=0):
    return pl.pallas_call(
        kernel,
        name=name,
        in_specs=[SMEM] + [VMEM] * (len(args) - 1),
        out_specs=jax.tree.map(lambda _: VMEM, out),
        out_shape=out,
        cost_estimate=pl.CostEstimate(flops=flops, bytes_accessed=moved, transcendentals=0),
        compiler_params=pltpu.CompilerParams(vmem_limit_bytes=limit * MIB),
    )(*args)


def shape(*dims, dtype=F32):
    return jax.ShapeDtypeStruct(dims, dtype)


def lanes(block):
    return pl.ds(pl.multiple_of(block * LANE, LANE), LANE)


def cut(value):
    first = value.astype(BF16)
    rest = value - first.astype(F32)
    second = rest.astype(BF16)
    return first, second, (rest - second.astype(F32)).astype(BF16)


def split_kernel(place, meta, unit, images, ctf, tables, kept, given, parts, turns, held, images_in, ctf_in, sems):
    core = place[3]
    copies = [
        pltpu.make_async_copy(source, target, sems.at[i])
        for i, (source, target) in enumerate(((images, images_in), (ctf, ctf_in), (tables, turns)))
    ]
    for copy in copies:
        copy.start()
    copies[1].wait()
    held[...] = ctf_in[...]
    for i, part in enumerate(cut(ctf_in[...])):
        parts[16 * i : 16 * i + 16, :] = jnp.concatenate([part.astype(F32), jnp.zeros((8, FREQS), F32)], axis=0).astype(BF16)
    copies[0].wait()

    def turn(j, carry):
        kept[:, lanes(j)] = images_in[:, lanes(2 * j + core)]
        given[:, lanes(j)] = images_in[:, lanes(2 * j + 1 - core)]
        return carry

    lax.fori_loop(0, BLOCKS, turn, 0)
    kept[:, DEPTH:] = meta[...]
    given[:, DEPTH:] = meta[...]
    copies[2].wait()


def split_call(place, meta, unit, images, ctf, tables):
    half = shape(SLOTS, DEPTH + LANE, dtype=BF16)
    anywhere = pl.BlockSpec(memory_space=pltpu.HBM)
    return pl.pallas_call(
        split_kernel,
        name="split",
        in_specs=[SMEM, VMEM, VMEM, anywhere, anywhere, anywhere],
        out_specs=[VMEM] * 5,
        out_shape=[half, half, shape(48, FREQS, dtype=BF16), shape(2 * HALF, FREQS), shape(GROUPS, FREQS)],
        scratch_shapes=[
            pltpu.VMEM((SLOTS, 2 * DEPTH), BF16),
            pltpu.VMEM((GROUPS, FREQS), F32),
            pltpu.SemaphoreType.DMA((3,)),
        ],
        compiler_params=pltpu.CompilerParams(vmem_limit_bytes=LIMIT * MIB),
    )(place, meta, unit, images, ctf, tables)


def owner_block(place, p):
    return (place[0] ^ (p // 8)) * 8 + (place[1] ^ (p % 8 // 2)) * 2 + (place[2] ^ (p % 2))


def build_kernel(place, after, images, parts, turns, out0, out1, out2, out3, token, rows):
    core = place[3]
    group = images[:, DEPTH : DEPTH + 1].astype(F32)
    lane = lax.broadcasted_iota(jnp.int32, (SLOTS, 48), 1)
    hot = jnp.where((group == (lane % 16).astype(F32)) & (lane % 16 < GROUPS), 1.0, 0.0).astype(BF16)
    rows[...] = jnp.dot(hot, parts[...], preferred_element_type=F32)
    for dx, out in enumerate((out0, out1, out2, out3)):

        def turn(p, carry):
            j = owner_block(place, 8 * dx + p)
            at = lanes(2 * (j % 16) + core)
            sign = jnp.where(j < 16, 1.0, -1.0).astype(F32)
            row = rows[:, at]
            first = images[:, lanes(j)].astype(F32) * row
            second = images[:, lanes(j ^ 16)].astype(F32) * (row * sign)
            here = lanes(p)
            for s in range(HALF):
                a = first * turns[s : s + 1, at]
                b = second * turns[HALF + s : HALF + s + 1, at]
                out[2 * SLOTS * s : 2 * SLOTS * (s + 1), here] = jnp.concatenate([a + b, a - b], axis=0).astype(BF16)
            tail = jnp.concatenate([first, jnp.zeros((ROWS - SLOTS * SHIFTS, LANE), F32)], axis=0)
            out[2 * SLOTS * HALF : ROWS, here] = tail.astype(BF16)
            return carry

        lax.fori_loop(0, 8, turn, 0, unroll=8)
    token[...] = jnp.zeros_like(token)


def build_call(place, after, images, parts, turns, name):
    return pl.pallas_call(
        build_kernel,
        name=name,
        in_specs=[SMEM] + [VMEM] * 4,
        out_specs=[VMEM] * 5,
        out_shape=[shape(ROWS, CHUNK, dtype=BF16)] * 4 + [shape(8, LANE)],
        scratch_shapes=[pltpu.VMEM((SLOTS, FREQS), F32)],
        cost_estimate=pl.CostEstimate(flops=6 * 10**9, bytes_accessed=2 * ROWS * DEPTH, transcendentals=0),
        compiler_params=pltpu.CompilerParams(vmem_limit_bytes=LIMIT * MIB),
    )(place, after, images, parts, turns)


def hot_rows(meta):
    group = meta[:, 0:1].astype(F32)
    lane = lax.broadcasted_iota(jnp.int32, (SLOTS, GROUPS), 1).astype(F32)
    return jnp.where(group == lane, 1.0, 0.0).astype(F32)


def stack_of(piece):
    return jnp.concatenate([piece[r] for r in range(8)], axis=1)


def weigh_kernel(place, ctf, t0, t1, t2, t3, p0, p1, p2, p3, power):
    core = place[3]
    total = jnp.zeros((3 * GROUPS, WIDTH), F32)
    for q, piece in enumerate((p0, p1, p2, p3)):
        left = jnp.concatenate([ctf[:, lanes(2 * (owner_block(place, 8 * q + r) % 16) + core)] for r in range(8)], axis=1)
        parts = jnp.concatenate([part.astype(F32) for part in cut(left * left)], axis=0).astype(BF16)
        square = stack_of(piece).astype(F32)
        square = square * square
        high = square.astype(BF16)
        low = (square - high.astype(F32)).astype(BF16)
        dims = (((1,), (1,)), ((), ()))
        total = total + lax.dot_general(parts, high, dims, preferred_element_type=F32)
        total = total + lax.dot_general(parts, low, dims, preferred_element_type=F32)
    power[...] = total[:GROUPS] + total[GROUPS : 2 * GROUPS] + total[2 * GROUPS :]


def score_kernel(place, power, meta_a, meta_b, p0, p1, p2, p3, *refs):
    out = refs[8]
    for k, meta in enumerate((meta_a, meta_b)):
        half = 0.5 * jnp.dot(hot_rows(meta[...]), power[...], precision=HIGHEST, preferred_element_type=F32)
        sums = None
        for dx, piece in enumerate((p0, p1, p2, p3)):
            part = lax.dot_general(
                refs[4 * k + dx][...], stack_of(piece), (((1,), (1,)), ((), ())), preferred_element_type=F32
            )
            sums = part if sums is None else sums + part
        spare = jnp.zeros((ROWS - SLOTS * SHIFTS, WIDTH), F32)
        out[k, :, :WIDTH] = sums - jnp.concatenate([half] * SHIFTS + [spare], axis=0)


def settle_kernel(place, mine, theirs, stats):
    columns = []
    for k in range(2):

        def value(s):
            at = slice(SLOTS * s, SLOTS * (s + 1))
            return mine[k, at, :WIDTH] + theirs[k, at, :WIDTH]

        best = value(0)
        for s in range(1, SHIFTS):
            best = jnp.maximum(best, value(s))
        top = jnp.max(best, axis=1, keepdims=True)
        total = jnp.exp(value(0) - top)
        for s in range(1, SHIFTS):
            total = total + jnp.exp(value(s) - top)
        columns += [top, jnp.sum(total, axis=1, keepdims=True)]
    lane = lax.broadcasted_iota(jnp.int32, (SLOTS, LANE), 1)
    spread = jnp.where(lane == 0, columns[0], jnp.where(lane == 1, columns[1], jnp.where(lane == 2, columns[2], columns[3])))
    spread = jnp.concatenate([spread, jnp.zeros((LANE - SLOTS, LANE), F32)], axis=0).T[:8, :]
    stats[...] = spread


def merge_kernel(place, mine, theirs, out):
    for k in range(2):
        here, there = 2 * k, 2 - 2 * k
        first, second = mine[here : here + 1, :], theirs[there : there + 1, :]
        top = jnp.maximum(first, second)
        out[here : here + 1, :] = top
        out[here + 1 : here + 2, :] = mine[here + 1 : here + 2, :] * jnp.exp(first - top) + theirs[there + 1 : there + 2, :] * jnp.exp(second - top)
    out[4:, :] = jnp.zeros((4, LANE), F32)


def posterior_kernel(place, mine, theirs, stats0, stats1, stats2, stats3, meta_a, meta_b, low, evidence, spare):
    counted = jnp.zeros((GROUPS, WIDTH), F32)
    for k, meta in ((1, meta_b), (0, meta_a)):
        stats = (stats0, stats1, stats2, stats3)
        tops = jnp.concatenate([here[2 * k : 2 * k + 1, :SLOTS] for here in stats], axis=0)
        totals = jnp.concatenate([here[2 * k + 1 : 2 * k + 2, :SLOTS] for here in stats], axis=0)
        top = jnp.max(tops, axis=0, keepdims=True)
        total = jnp.sum(totals * jnp.exp(tops - top), axis=0, keepdims=True)
        row = lax.broadcasted_iota(jnp.int32, (8, SLOTS), 0)
        columns = jnp.where(row == 0, top, jnp.where(row == 1, total, top + jnp.log(total))).T
        live = meta[:, 1:2].astype(F32)
        scale = live / columns[:, 1:2]
        if k == 0:
            known = jnp.where(live > 0.0, columns[:, 2:3], 0.0)
            evidence[...] = jnp.broadcast_to(known, (SLOTS, LANE)).T[:8, :]
        gathered = None
        for s in range(SHIFTS):
            at = slice(SLOTS * s, SLOTS * (s + 1))
            value = jnp.exp(mine[k, at, :WIDTH] + theirs[k, at, :WIDTH] - columns[:, 0:1]) * scale
            spare[at, :] = value
            gathered = value if gathered is None else gathered + value
        hot = hot_rows(meta[...])
        counted = counted + lax.dot_general(
            hot, gathered, (((0,), (0,)), ((), ())), precision=HIGHEST, preferred_element_type=F32
        )
        spare[SLOTS * SHIFTS :, :] = jnp.zeros((ROWS - SLOTS * SHIFTS, WIDTH), F32)
        if k == 0:
            first = counted.astype(BF16).astype(F32)
            spare[COUNTED : COUNTED + GROUPS, :] = first
            spare[COUNTED + GROUPS : COUNTED + 2 * GROUPS, :] = counted - first
        low[k] = spare[...].T.astype(BF16)


def posterior_call(*args):
    out = [shape(2, WIDTH, ROWS, dtype=BF16), shape(8, SLOTS)]
    return pl.pallas_call(
        posterior_kernel,
        name="posterior",
        in_specs=[SMEM] + [VMEM] * (len(args) - 1),
        out_specs=[VMEM] * 2,
        out_shape=out,
        scratch_shapes=[pltpu.VMEM((ROWS, WIDTH), F32)],
        compiler_params=pltpu.CompilerParams(vmem_limit_bytes=LIMIT * MIB),
    )(*args)


def insert_kernel(chunks, halves=1):
    def kernel(place, after, mine, theirs, *refs):
        shifted_refs, outs = refs[: 4 * chunks], refs[4 * chunks :]
        low = jnp.concatenate([mine[0], theirs[0], mine[1], theirs[1]], axis=1)
        tail = slice(ROWS - LANE, ROWS)
        start = COUNTED - ROWS + LANE
        both = (mine[0, :, tail].astype(F32) + theirs[0, :, tail].astype(F32)).T
        both = both[start : start + GROUPS] + both[start + GROUPS : start + 2 * GROUPS]
        both = jnp.concatenate([both, jnp.zeros((GROUPS, WIDE - WIDTH), F32)], axis=1)
        outs[-1][...] = jnp.zeros((8, LANE), F32)
        for i in range(chunks):
            columns = shifted_refs[4 * i : 4 * i + 4]
            planes = [outs[i * halves + n * halves // 8].at[n % (8 // halves)] for n in range(8)]
            for n in range(0, 8, 2):
                at = slice(LANE * n, LANE * (n + 2))
                shifted = jnp.concatenate([s[:, at] for s in columns], axis=0)
                sums = jnp.dot(low, shifted, preferred_element_type=F32)
                for r in range(2):
                    planes[n + r][:WIDTH, :] = sums[:, r * LANE : (r + 1) * LANE].astype(outs[i].dtype)
            for n in range(8):
                planes[n][WIDTH:, :] = both[:, LANE * (n % 2) : LANE * (n % 2 + 1)].astype(outs[i].dtype)

    return kernel


def forward_kernel(place, one, three, far_one, far_three, out_one, out_three):
    out_one[:4] = one[:4]
    out_one[4:] = (one[4:].astype(F32) + far_three[...].astype(F32)).astype(BF16)
    out_three[:4] = (three[:4].astype(F32) + far_one[...].astype(F32)).astype(BF16)
    out_three[4:] = three[4:]


def gather_kernel(place, own, one, three, *outs):
    def total(n, rows):
        return own[n, rows] + one[n, rows].astype(F32) + three[n, rows].astype(F32)

    tail = slice(WIDTH, TALL)
    both = jnp.concatenate([total(0, tail), total(1, tail)], axis=0)
    for n, out in enumerate(outs):
        out[:WIDTH] = total(n, slice(0, WIDTH)).astype(out.dtype)
        out[WIDTH:] = both.astype(out.dtype)


def finish_kernel(place, *refs):
    insertions, weights = refs[8:]
    for k in range(2):
        parts = [refs[2 * n + k][...].astype(F32) for n in range(4)]
        sums = (parts[0] + parts[1]) + (parts[2] + parts[3])
        to = place[2] ^ k
        insertions[to] = sums[:WIDTH]
        weights[to] = jnp.concatenate([sums[WIDTH:TALL], sums[TALL:]], axis=1)[:, :WIDTH]


def swap(value, axis, d, n=4):
    return lax.ppermute(value, axis, [(i, i ^ d) for i in range(n)])


def body(particle_images, particle_groups, live_counts, ctf_table, projections):
    x, y, zl, core = (lax.axis_index(a) for a in ("grp", "y", "zl", "core"))
    place = jnp.stack([x, y, zl, core]).astype(jnp.int32)
    ring = ("cls", "zl")

    slot = jnp.arange(SLOTS, dtype=jnp.int32)
    live = slot < live_counts[0]
    lane = jnp.arange(LANE, dtype=jnp.int32)[None, :]
    meta = jnp.where(lane == 0, particle_groups[:, None], jnp.where(lane == 1, live.astype(jnp.int32)[:, None], 0)).astype(BF16)

    stacks = jnp.transpose(projections, (1, 2, 0))
    mine = lax.dynamic_index_in_dim(stacks, zl, axis=0)
    theirs = lax.dynamic_index_in_dim(stacks, 1 - zl, axis=0)
    unit = jnp.concatenate([mine, lax.ppermute(theirs, "zl", SWAP)])

    tables = np.concatenate(shift_tables())
    kept, other, parts, turns, ctf = split_call(place, meta, unit, particle_images, ctf_table, tables)
    halves = [kept, lax.ppermute(other, "core", SWAP)]

    column = jnp.concatenate([unit] + [swap(unit, "y", d) for d in (1, 2, 3)])
    next_kept = lax.ppermute(kept, "zl", SWAP)
    next_other = lax.ppermute(other, ring, [(i, (i + 1) % 8 if i % 2 else (i + 7) % 8) for i in range(8)])
    halves += [next_kept, lax.ppermute(next_other, "core", SWAP)]
    pieces = [column] + [swap(column, "grp", d) for d in (1, 2, 3)]

    metas = [h[:, DEPTH:] for h in halves]
    built = [build_call(place, column, h, parts, turns, f"build_{i}") for i, h in enumerate(halves)]
    shifted = [b[:4] for b in built]
    tokens = [b[4] for b in built]
    power = call(
        weigh_kernel,
        "weigh",
        shape(GROUPS, WIDTH),
        (place, ctf, *tokens, *pieces),
        LIMIT,
    )
    score = shape(2, ROWS, WIDE)
    flops = 4 * ROWS * WIDE * DEPTH
    given = call(score_kernel, "score_given", score, (place, power, metas[1], metas[3], *pieces, *shifted[1], *shifted[3]), LIMIT, flops)
    taken = lax.ppermute(given, "core", SWAP)
    kept_score = call(score_kernel, "score_own", score, (place, power, metas[0], metas[2], *pieces, *shifted[0], *shifted[2]), LIMIT, flops)
    stats = call(settle_kernel, "settle", shape(8, LANE), (place, kept_score, taken), LIMIT)
    stats = call(merge_kernel, "merge", shape(8, LANE), (place, stats, lax.ppermute(stats, "zl", SWAP)), LIMIT)
    stats = [stats] + [swap(stats, "cls", d) for d in (1, 2, 3)]
    low, evidence = posterior_call(place, kept_score, taken, *stats, metas[0], metas[2])
    other_low = lax.ppermute(low, "core", SWAP)

    flops = 2 * 4 * ROWS * WIDE * 1024
    chunk = shape(8, TALL, LANE, dtype=BF16)
    token = shape(8, LANE)

    def columns(*chunks):
        return [group[q] for q in chunks for group in shifted]

    half = shape(4, TALL, LANE, dtype=BF16)
    send_one, send_three, after = call(
        insert_kernel(1, 2), "insert_far", [half, half, token], (place, evidence, low, other_low, *columns(2)), LIMIT, flops
    )
    far = [swap(send_one, "grp", 1), swap(send_three, "grp", 3)]
    one, three, after = call(
        insert_kernel(2), "insert_near", [chunk, chunk, token], (place, after, low, other_low, *columns(1, 3)), LIMIT, 2 * flops
    )
    one, three = call(forward_kernel, "forward", [chunk, chunk], (place, one, three, *far), LIMIT)
    near = [swap(one, "grp", 1), swap(three, "grp", 3)]
    own, _ = call(insert_kernel(1), "insert_own", [shape(8, TALL, LANE), token], (place, after, low, other_low, *columns(0)), LIMIT, flops)
    tile = (TALL + GROUPS, LANE)
    kept, *sent = call(gather_kernel, "gather", [shape(*tile)] + [shape(*tile, dtype=BF16)] * 7, (place, own, *near), LIMIT)
    blocks = [kept] + [swap(v, ("y", "zl"), n, 8) for n, v in enumerate(sent, 1)]
    insertions, tally = call(finish_kernel, "finish", [shape(2, WIDTH, LANE), shape(2, GROUPS, WIDTH)], (place, *blocks), LIMIT)
    return insertions, tally, evidence[0]


def solution(mesh):
    fine = Mesh(mesh.devices.reshape(4, 4, 4, 2, 2), ("cls", "grp", "y", "zl", "core"))
    shards = ("grp", "y", "zl", "core")
    return jax.shard_map(
        body,
        mesh=fine,
        in_specs=(P(shards, None), P(shards), P(shards), P(), P(shards, "cls", None)),
        out_specs=(P("cls", None, shards), P("cls", None, None), P(shards)),
        check_vma=False,
    )
```

```python
import math

import jax
import jax.numpy as jnp
import numpy as np
from jax import lax
from jax.experimental import pallas as pl
from jax.experimental.pallas import tpu as pltpu
from jax.sharding import Mesh, PartitionSpec as P

IMG = 64
SIDE = 5
SHIFTS = SIDE * SIDE
HALF = SHIFTS // 2
GROUPS = 8
FREQS = IMG * IMG
LANE = 128
SLOTS = 40
ROWS = 1024
WIDTH = 200
WIDE = 256
TALL = WIDTH + 16
COUNTED = SLOTS * SHIFTS
BLOCKS = 32
DEPTH = BLOCKS * LANE
CHUNK = DEPTH // 8
HIGHEST = lax.Precision.HIGHEST
F32 = jnp.float32
BF16 = jnp.bfloat16
MIB = 2**20
LIMIT = 4
VMEM = pl.BlockSpec(memory_space=pltpu.VMEM)
SMEM = pl.BlockSpec(memory_space=pltpu.SMEM)
SWAP = [(0, 1), (1, 0)]


def shift_tables():
    index = np.arange(FREQS)
    shift = np.arange(HALF)
    offx = shift // SIDE - SIDE // 2
    offy = shift % SIDE - SIDE // 2
    phase = (offx[:, None] * (index // IMG)[None, :] + offy[:, None] * (index % IMG)[None, :]) % IMG
    theta = (phase.astype(np.float32) * np.float32(2.0 * math.pi / IMG)).astype(np.float64)
    return np.cos(theta).astype(np.float32), np.sin(theta).astype(np.float32)


def call(kernel, name, out, args, limit, flops=0, moved=0):
    return pl.pallas_call(
        kernel,
        name=name,
        in_specs=[SMEM] + [VMEM] * (len(args) - 1),
        out_specs=jax.tree.map(lambda _: VMEM, out),
        out_shape=out,
        cost_estimate=pl.CostEstimate(flops=flops, bytes_accessed=moved, transcendentals=0),
        compiler_params=pltpu.CompilerParams(vmem_limit_bytes=limit * MIB),
    )(*args)


def shape(*dims, dtype=F32):
    return jax.ShapeDtypeStruct(dims, dtype)


def lanes(block):
    return pl.ds(pl.multiple_of(block * LANE, LANE), LANE)


def cut(value):
    first = value.astype(BF16)
    rest = value - first.astype(F32)
    second = rest.astype(BF16)
    return first, second, (rest - second.astype(F32)).astype(BF16)


def spread_kernel(stacks, out, held, sem):
    copy = pltpu.make_async_copy(stacks, held, sem)
    copy.start()
    copy.wait()
    for n in range(8):
        out[n] = held[n % 2]


def spread_call(stacks):
    return pl.pallas_call(
        spread_kernel,
        name="spread",
        in_specs=[pl.BlockSpec(memory_space=pltpu.HBM)],
        out_specs=VMEM,
        out_shape=shape(8, WIDTH, LANE, dtype=BF16),
        scratch_shapes=[pltpu.VMEM((2, WIDTH, LANE), BF16), pltpu.SemaphoreType.DMA],
        compiler_params=pltpu.CompilerParams(vmem_limit_bytes=LIMIT * MIB),
    )(pltpu.with_memory_space_constraint(stacks, pltpu.HBM))


def split_kernel(place, groups, count, images, ctf, tables, kept, given, parts, turns, held, images_in, ctf_in, sems):
    core = place[3]
    copies = [
        pltpu.make_async_copy(source, target, sems.at[i])
        for i, (source, target) in enumerate(((images, images_in), (ctf, ctf_in), (tables, turns)))
    ]
    for copy in copies:
        copy.start()
    copies[1].wait()
    held[...] = ctf_in[...]
    for i, part in enumerate(cut(ctf_in[...])):
        parts[16 * i : 16 * i + 16, :] = jnp.concatenate([part.astype(F32), jnp.zeros((8, FREQS), F32)], axis=0).astype(BF16)
    copies[0].wait()

    def turn(j, carry):
        kept[:, lanes(j)] = images_in[:, lanes(2 * j + core)]
        given[:, lanes(j)] = images_in[:, lanes(2 * j + 1 - core)]
        return carry

    lax.fori_loop(0, BLOCKS, turn, 0)
    row = lax.broadcasted_iota(jnp.int32, (SLOTS, LANE), 0)
    lane = lax.broadcasted_iota(jnp.int32, (SLOTS, LANE), 1)
    group = jnp.zeros((SLOTS, LANE), jnp.int32)
    for i in range(SLOTS):
        group = jnp.where(row == i, groups[i], group)
    live = jnp.where(row < count[0], 1, 0)
    meta = jnp.where(lane == 0, group, jnp.where(lane == 1, live, 0)).astype(F32).astype(BF16)
    kept[:, DEPTH:] = meta
    given[:, DEPTH:] = meta
    copies[2].wait()


def split_call(place, groups, count, images, ctf, tables):
    half = shape(SLOTS, DEPTH + LANE, dtype=BF16)
    anywhere = pl.BlockSpec(memory_space=pltpu.HBM)
    return pl.pallas_call(
        split_kernel,
        name="split",
        in_specs=[SMEM, SMEM, SMEM, anywhere, anywhere, anywhere],
        out_specs=[VMEM] * 5,
        out_shape=[half, half, shape(48, FREQS, dtype=BF16), shape(2 * HALF, FREQS), shape(GROUPS, FREQS)],
        scratch_shapes=[
            pltpu.VMEM((SLOTS, 2 * DEPTH), BF16),
            pltpu.VMEM((GROUPS, FREQS), F32),
            pltpu.SemaphoreType.DMA((3,)),
        ],
        compiler_params=pltpu.CompilerParams(vmem_limit_bytes=LIMIT * MIB),
    )(place, groups, count, *(pltpu.with_memory_space_constraint(v, pltpu.HBM) for v in (images, ctf, tables)))


def owner_block(place, p):
    later, first, second = p // 16, p % 16 // 4, p % 4
    across = jnp.where(later == 0, first, second)
    along = jnp.where(later == 0, second, place[1] ^ first)
    return (place[0] ^ across) * 8 + along * 2 + later


def build_kernel(place, after, images_a, images_b, parts, turns, *refs):
    outs, (token, rows) = refs[:8], refs[8:]
    core = place[3]
    lane = lax.broadcasted_iota(jnp.int32, (SLOTS, 48), 1)

    def member(k, carry):
        def read(at):
            return jnp.where(k == 0, images_a[:, at].astype(F32), images_b[:, at].astype(F32))

        group = read(slice(DEPTH, DEPTH + LANE))[:, :1]
        hot = jnp.where((group == (lane % 16).astype(F32)) & (lane % 16 < GROUPS), 1.0, 0.0).astype(BF16)
        rows[...] = jnp.dot(hot, parts[...], preferred_element_type=F32)
        for t, out in enumerate(outs):

            def turn(p, carry):
                j = owner_block(place, 4 * t + p)
                at = lanes(2 * (j % 16) + core)
                sign = jnp.where(j < 16, 1.0, -1.0).astype(F32)
                row = rows[:, at]
                first = read(lanes(j)) * row
                second = read(lanes(j ^ 16)) * (row * sign)
                here = lanes(p)
                for s in range(HALF):
                    a = first * turns[s : s + 1, at]
                    b = second * turns[HALF + s : HALF + s + 1, at]
                    pair = jnp.concatenate([a + b, a - b], axis=0).astype(BF16)
                    out[k, 2 * SLOTS * s : 2 * SLOTS * (s + 1), here] = pair
                tail = jnp.concatenate([first, jnp.zeros((ROWS - SLOTS * SHIFTS, LANE), F32)], axis=0)
                out[k, 2 * SLOTS * HALF : ROWS, here] = tail.astype(BF16)
                return carry

            lax.fori_loop(0, 4, turn, 0, unroll=4)
        return carry

    lax.fori_loop(0, 2, member, 0)
    token[...] = jnp.zeros_like(token)


def build_call(place, after, images_a, images_b, parts, turns, name, flops):
    return pl.pallas_call(
        build_kernel,
        name=name,
        in_specs=[SMEM] + [VMEM] * 5,
        out_specs=[VMEM] * 9,
        out_shape=[shape(2, ROWS, CHUNK, dtype=BF16)] * 8 + [shape(8, WIDE)],
        scratch_shapes=[pltpu.VMEM((SLOTS, FREQS), F32)],
        cost_estimate=pl.CostEstimate(flops=flops, bytes_accessed=10**5, transcendentals=0),
        compiler_params=pltpu.CompilerParams(vmem_limit_bytes=LIMIT * MIB),
    )(place, after, images_a, images_b, parts, turns)


def hot_rows(meta):
    group = meta[:, DEPTH : DEPTH + 1].astype(F32)
    lane = lax.broadcasted_iota(jnp.int32, (SLOTS, GROUPS), 1).astype(F32)
    return jnp.where(group == lane, 1.0, 0.0).astype(F32)


def stack_of(piece):
    return jnp.concatenate([piece[r] for r in range(8)], axis=1)


def weigh_kernel(chunks):
    def kernel(place, ctf, after, *refs):
        pieces, power = refs[:-1], refs[-1]
        core = place[3]
        total = jnp.zeros((3 * GROUPS, WIDTH), F32)
        for q, piece in zip(chunks, pieces):
            left = jnp.concatenate([ctf[:, lanes(2 * (((place[0] ^ q) * 8 + r) % 16) + core)] for r in range(8)], axis=1)
            parts = jnp.concatenate([part.astype(F32) for part in cut(left * left)], axis=0).astype(BF16)
            square = stack_of(piece).astype(F32)
            square = square * square
            high = square.astype(BF16)
            low = (square - high.astype(F32)).astype(BF16)
            dims = (((1,), (1,)), ((), ()))
            total = total + lax.dot_general(parts, high, dims, preferred_element_type=F32)
            total = total + lax.dot_general(parts, low, dims, preferred_element_type=F32)
        power[...] = after[:, :WIDTH] + total[:GROUPS] + total[GROUPS : 2 * GROUPS] + total[2 * GROUPS :]

    return kernel


def score_kernel(member):
    def kernel(place, power, meta_a, meta_b, *refs):
        pieces, out = refs[:4], refs[20]
        for k, meta in enumerate((meta_a, meta_b)):
            half = 0.5 * jnp.dot(hot_rows(meta), power[...], precision=HIGHEST, preferred_element_type=F32)
            sums = None
            for t in range(4):
                weights = [pieces[t][2 * n] for n in range(4)] + [pieces[n][2 * (place[1] ^ t) + 1] for n in range(4)]
                shifted = jnp.concatenate([refs[4 + 8 * k + t][member], refs[8 + 8 * k + t][member]], axis=1)
                part = lax.dot_general(
                    shifted, jnp.concatenate(weights, axis=1), (((1,), (1,)), ((), ())), preferred_element_type=F32
                )
                sums = part if sums is None else sums + part
            spare = jnp.zeros((ROWS - SLOTS * SHIFTS, WIDTH), F32)
            out[k, :, :WIDTH] = sums - jnp.concatenate([half] * SHIFTS + [spare], axis=0)

    return kernel


def settle_kernel(place, mine, theirs, stats):
    columns = []
    for k in range(2):

        def value(s):
            at = slice(SLOTS * s, SLOTS * (s + 1))
            return mine[k, at, :WIDTH] + theirs[k, at, :WIDTH]

        best = value(0)
        for s in range(1, SHIFTS):
            best = jnp.maximum(best, value(s))
        top = jnp.max(best, axis=1, keepdims=True)
        total = jnp.exp(value(0) - top)
        for s in range(1, SHIFTS):
            total = total + jnp.exp(value(s) - top)
        columns += [top, jnp.sum(total, axis=1, keepdims=True)]
    lane = lax.broadcasted_iota(jnp.int32, (SLOTS, LANE), 1)
    spread = jnp.where(lane == 0, columns[0], jnp.where(lane == 1, columns[1], jnp.where(lane == 2, columns[2], columns[3])))
    spread = jnp.concatenate([spread, jnp.zeros((LANE - SLOTS, LANE), F32)], axis=0).T[:8, :]
    for d in range(8):
        stats[d] = spread


def posterior_kernel(place, mine, theirs, stats, meta_a, meta_b, low, evidence, spare):
    parity = place[2]
    counted = jnp.zeros((GROUPS, WIDTH), F32)
    for k, meta in ((1, meta_b), (0, meta_a)):
        tops, totals = [], []
        for d in range(8):
            same = (parity == d % 2) == (k == 0)
            here = stats[d, :, :SLOTS]
            tops.append(jnp.where(same, here[0:1], here[2:3]))
            totals.append(jnp.where(same, here[1:2], here[3:4]))
        tops = jnp.concatenate(tops, axis=0)
        totals = jnp.concatenate(totals, axis=0)
        top = jnp.max(tops, axis=0, keepdims=True)
        total = jnp.sum(totals * jnp.exp(tops - top), axis=0, keepdims=True)
        row = lax.broadcasted_iota(jnp.int32, (8, SLOTS), 0)
        columns = jnp.where(row == 0, top, jnp.where(row == 1, total, top + jnp.log(total))).T
        live = meta[:, DEPTH + 1 : DEPTH + 2].astype(F32)
        scale = live / columns[:, 1:2]
        if k == 0:
            known = jnp.where(live > 0.0, columns[:, 2:3], 0.0)
            evidence[...] = jnp.broadcast_to(known, (SLOTS, LANE)).T[:8, :]
        gathered = None
        for s in range(SHIFTS):
            at = slice(SLOTS * s, SLOTS * (s + 1))
            value = jnp.exp(mine[k, at, :WIDTH] + theirs[k, at, :WIDTH] - columns[:, 0:1]) * scale
            spare[at, :] = value
            gathered = value if gathered is None else gathered + value
        hot = hot_rows(meta)
        counted = counted + lax.dot_general(
            hot, gathered, (((0,), (0,)), ((), ())), precision=HIGHEST, preferred_element_type=F32
        )
        spare[SLOTS * SHIFTS :, :] = jnp.zeros((ROWS - SLOTS * SHIFTS, WIDTH), F32)
        if k == 0:
            first = counted.astype(BF16).astype(F32)
            spare[COUNTED : COUNTED + GROUPS, :] = first
            spare[COUNTED + GROUPS : COUNTED + 2 * GROUPS, :] = counted - first
        low[k] = spare[...].T.astype(BF16)


def posterior_call(*args):
    out = [shape(2, WIDTH, ROWS, dtype=BF16), shape(8, SLOTS)]
    return pl.pallas_call(
        posterior_kernel,
        name="posterior",
        in_specs=[SMEM] + [VMEM] * (len(args) - 1),
        out_specs=[VMEM] * 2,
        out_shape=out,
        scratch_shapes=[pltpu.VMEM((ROWS, WIDTH), F32)],
        compiler_params=pltpu.CompilerParams(vmem_limit_bytes=LIMIT * MIB),
    )(*args)


def block_sums(low, groups, put):
    for n in (0, 2):
        at = slice(LANE * n, LANE * (n + 2))
        sums = jnp.dot(low, jnp.concatenate([g[:, at] for g in groups], axis=0), preferred_element_type=F32)
        for r in range(2):
            put(n + r, sums[:, r * LANE : (r + 1) * LANE])


def own_kernel(place, mine, a0, a1, b0, b1, out_a, out_b):
    low = jnp.concatenate([mine[0], mine[1]], axis=1)
    for groups, out in (((a0.at[0], a1.at[0]), out_a), ((b0.at[0], b1.at[0]), out_b)):

        def put(n, value):
            out[n] = value

        block_sums(low, groups, put)


def insert_kernel(chunks, begun=False):
    def kernel(place, after, mine, theirs, *refs):
        starts, refs = (refs[:2], refs[2:]) if begun else ((None, None), refs)
        members = (1,) if begun else (0, 1)
        shifted, outs = refs[: 4 * chunks], refs[4 * chunks :]
        lows = [theirs[0], theirs[1]] if begun else [mine[0], theirs[0], mine[1], theirs[1]]
        low = jnp.concatenate(lows, axis=1)
        tail = slice(ROWS - LANE, ROWS)
        first = COUNTED - ROWS + LANE
        both = (mine[0, :, tail].astype(F32) + theirs[0, :, tail].astype(F32)).T
        both = both[first : first + GROUPS] + both[first + GROUPS : first + 2 * GROUPS]
        both = jnp.concatenate([both, jnp.zeros((GROUPS, WIDE - WIDTH), F32)], axis=1)
        both = jnp.concatenate([both[:, :LANE], both[:, LANE:]], axis=0)
        outs[-1][...] = jnp.zeros((8, LANE), F32)
        for i, out in enumerate(outs[:-1]):
            start = starts[i % 2]

            def put(n, value):
                if start is not None:
                    value = value + start[n]
                out[n, :WIDTH, :] = value.astype(out.dtype)

            block_sums(low, [pair.at[k] for pair in shifted[2 * i : 2 * i + 2] for k in members], put)
            if i % 2 == 0:
                for n in range(4):
                    out[n, WIDTH:, :] = both.astype(out.dtype)

    return kernel


def absorb_kernel(place, own_a, own_b, far_a, far_b, out_a, out_b):
    out_a[...] = own_a[...] + far_a[...].astype(F32)
    out_b[...] = own_b[...] + far_b[...].astype(F32)


def gather_kernel(place, own_a, own_b, one_a, one_b, three_a, three_b, kept_a, kept_b, sent_a, sent_b):
    y = place[1]
    for out, planes in ((kept_a, (y, y ^ 3)), (sent_a, (y ^ 1, y ^ 2))):
        for i, n in enumerate(planes):
            out[i] = (own_a[n] + one_a[n].astype(F32) + three_a[n].astype(F32)).astype(out.dtype)
    for out, planes in ((kept_b, (0, 3)), (sent_b, (1, 2))):
        for i, n in enumerate(planes):
            out[i] = (own_b[n] + one_b[n].astype(F32) + three_b[n].astype(F32)).astype(out.dtype)


def middle_kernel(place, kept_a, kept_b, got_a, got_b, out_a, out_b, sent_a, sent_b):
    for kept, got, out, sent in ((kept_a, got_a, out_a, sent_a), (kept_b, got_b, out_b, sent_b)):
        out[...] = kept[0] + got[0].astype(F32)
        sent[...] = (kept[1] + got[1].astype(F32)).astype(BF16)


def part_kernel(place, kept_a, kept_b, got_a, got_b, stay, leave):
    even = kept_a[...] + got_a[...].astype(F32)
    odd = kept_b[...] + got_b[...].astype(F32)
    stay[WIDTH:] = even[WIDTH:]
    leave[WIDTH:] = even[WIDTH:].astype(BF16)
    stay[:WIDTH] = jnp.where(place[2] == 0, even[:WIDTH], odd)
    leave[:WIDTH] = jnp.where(place[2] == 0, odd, even[:WIDTH]).astype(BF16)


def finish_kernel(place, stay, came, insertions, weights):
    for k, sums in ((place[2], stay[...]), (1 - place[2], came[...].astype(F32))):
        insertions[k] = sums[:WIDTH]
        weights[k] = jnp.concatenate([sums[WIDTH : WIDTH + GROUPS], sums[WIDTH + GROUPS :]], axis=1)[:, :WIDTH]


def swap(value, axis, d, n=4):
    return lax.ppermute(value, axis, [(i, i ^ d) for i in range(n)])


def body(particle_images, particle_groups, live_counts, ctf_table, projections):
    x, y, zl, core = (lax.axis_index(a) for a in ("grp", "y", "zl", "core"))
    place = jnp.stack([x, y, zl, core]).astype(jnp.int32)
    ring = ("cls", "zl")

    stacks = jnp.transpose(projections, (1, 2, 0))
    column = lax.all_to_all(spread_call(stacks), ("y", "zl"), 0, 0, tiled=True)

    tables = np.concatenate(shift_tables())
    kept, other, parts, turns, ctf = split_call(place, particle_groups, live_counts, particle_images, ctf_table, jnp.asarray(tables))
    halves = [kept, lax.ppermute(other, "core", SWAP)]

    column, to_pair, to_next = lax.optimization_barrier((column, kept, other))
    next_kept = lax.ppermute(to_pair, "zl", SWAP)
    next_other = lax.ppermute(to_next, ring, [(i, (i + 1) % 8 if i % 2 else (i + 7) % 8) for i in range(8)])
    pieces = [column] + [swap(column, "grp", d) for d in (1, 2, 3)]

    built = [build_call(place, column, halves[0], halves[1], parts, turns, "build_here", 6 * 10**9)]
    next_kept, next_other, _ = lax.optimization_barrier((next_kept, next_other, built[0][8]))
    halves += [next_kept, lax.ppermute(next_other, "core", SWAP)]
    built += [build_call(place, column, halves[2], halves[3], parts, turns, "build_next", 10**8)]
    shifted = [b[:8] for b in built]
    tokens = [b[8] for b in built]
    power = call(weigh_kernel((0,)), "weigh_own", shape(GROUPS, WIDTH), (place, ctf, tokens[0], column), LIMIT, 10**8)
    power = call(weigh_kernel((1, 2, 3)), "weigh", shape(GROUPS, WIDTH), (place, ctf, power, *pieces[1:], *tokens[1:]), LIMIT)
    score = shape(2, ROWS, WIDE)
    flops = 4 * ROWS * WIDE * DEPTH
    given = call(score_kernel(1), "score_given", score, (place, power, halves[1], halves[3], *pieces, *shifted[0], *shifted[1]), LIMIT, flops)
    taken = lax.ppermute(given, "core", SWAP)
    kept_score = call(score_kernel(0), "score_own", score, (place, power, halves[0], halves[2], *pieces, *shifted[0], *shifted[1]), LIMIT, flops)
    stats = call(settle_kernel, "settle", shape(8, 8, LANE), (place, kept_score, taken), LIMIT)
    stats = lax.all_to_all(stats, ring, 0, 0, tiled=True)
    low, evidence = posterior_call(place, kept_score, taken, stats, halves[0], halves[2])
    other_low = lax.ppermute(low, "core", SWAP)

    flops = 2 * 4 * ROWS * WIDE * 1024
    token = shape(8, LANE)

    def block(kind):
        return [shape(4, TALL, LANE, dtype=kind), shape(4, WIDTH, LANE, dtype=kind)]

    def columns(chunk):
        return [pair[part + chunk] for part in (0, 4) for pair in shifted]

    begun = call(own_kernel, "insert_begin", [shape(4, WIDTH, LANE)] * 2, (place, low, *columns(2)), LIMIT, flops // 2)
    *send, after = call(
        insert_kernel(1, True), "insert_far", [*block(BF16), token], (place, evidence, low, other_low, *begun, *columns(2)), LIMIT, flops // 2
    )
    far = [swap(send[0], "grp", 2), swap(send[1], "y", 2)]
    *send, after = call(
        insert_kernel(2),
        "insert_near",
        [*block(BF16), *block(BF16), token],
        (place, after, low, other_low, *columns(1), *columns(3)),
        LIMIT,
        2 * flops,
    )
    near = [swap(send[0], "grp", 1), swap(send[1], "y", 1), swap(send[2], "grp", 3), swap(send[3], "y", 3)]
    *own, _ = call(insert_kernel(1), "insert_own", [*block(F32), token], (place, after, low, other_low, *columns(0)), LIMIT, flops)
    own = call(absorb_kernel, "absorb", block(F32), (place, *own, *far), LIMIT)
    tall, wide = (TALL, LANE), (WIDTH, LANE)
    out = [shape(2, *tall), shape(2, *wide), shape(2, *tall, dtype=BF16), shape(2, *wide, dtype=BF16)]
    *kept, send_a, send_b = call(gather_kernel, "gather", out, (place, *own, *near), LIMIT)
    out = [shape(*tall), shape(*wide), shape(*tall, dtype=BF16), shape(*wide, dtype=BF16)]
    *kept, send_a, send_b = call(middle_kernel, "middle", out, (place, *kept, swap(send_a, "y", 1), swap(send_b, "grp", 1)), LIMIT)
    out = [shape(*tall), shape(*tall, dtype=BF16)]
    stay, leave = call(part_kernel, "part", out, (place, *kept, swap(send_a, "y", 3), swap(send_b, "grp", 3)), LIMIT)
    came = lax.ppermute(leave, "zl", SWAP)
    insertions, tally = call(finish_kernel, "finish", [shape(2, WIDTH, LANE), shape(2, GROUPS, WIDTH)], (place, stay, came), LIMIT)
    return insertions, tally, evidence[0]


def solution(mesh):
    fine = Mesh(mesh.devices.reshape(4, 4, 4, 2, 2), ("cls", "grp", "y", "zl", "core"))
    shards = ("grp", "y", "zl", "core")
    return jax.shard_map(
        body,
        mesh=fine,
        in_specs=(P(shards, None), P(shards), P(shards), P(), P(shards, "cls", None)),
        out_specs=(P("cls", None, shards), P("cls", None, None), P(shards)),
        check_vma=False,
    )
```

```python
import math

import jax
import jax.numpy as jnp
import numpy as np
from jax import lax
from jax.experimental import pallas as pl
from jax.experimental.pallas import tpu as pltpu
from jax.sharding import Mesh, PartitionSpec as P

IMG = 64
SIDE = 5
SHIFTS = SIDE * SIDE
HALF = SHIFTS // 2
GROUPS = 8
FREQS = IMG * IMG
LANE = 128
SLOTS = 40
ROWS = 1024
WIDTH = 200
WIDE = 256
TALL = WIDTH + 16
COUNTED = SLOTS * SHIFTS
BLOCKS = 32
DEPTH = BLOCKS * LANE
CHUNK = DEPTH // 8
HIGHEST = lax.Precision.HIGHEST
F32 = jnp.float32
BF16 = jnp.bfloat16
MIB = 2**20
LIMIT = 4
VMEM = pl.BlockSpec(memory_space=pltpu.VMEM)
SMEM = pl.BlockSpec(memory_space=pltpu.SMEM)
SWAP = [(0, 1), (1, 0)]


def shift_tables():
    index = np.arange(FREQS)
    shift = np.arange(HALF)
    offx = shift // SIDE - SIDE // 2
    offy = shift % SIDE - SIDE // 2
    phase = (offx[:, None] * (index // IMG)[None, :] + offy[:, None] * (index % IMG)[None, :]) % IMG
    theta = (phase.astype(np.float32) * np.float32(2.0 * math.pi / IMG)).astype(np.float64)
    return np.cos(theta).astype(np.float32), np.sin(theta).astype(np.float32)


def call(kernel, name, out, args, limit, flops=0, moved=0):
    return pl.pallas_call(
        kernel,
        name=name,
        in_specs=[SMEM] + [VMEM] * (len(args) - 1),
        out_specs=jax.tree.map(lambda _: VMEM, out),
        out_shape=out,
        cost_estimate=pl.CostEstimate(flops=flops, bytes_accessed=moved, transcendentals=0),
        compiler_params=pltpu.CompilerParams(vmem_limit_bytes=limit * MIB),
    )(*args)


def shape(*dims, dtype=F32):
    return jax.ShapeDtypeStruct(dims, dtype)


def lanes(block):
    return pl.ds(pl.multiple_of(block * LANE, LANE), LANE)


def cut(value):
    first = value.astype(BF16)
    rest = value - first.astype(F32)
    second = rest.astype(BF16)
    return first, second, (rest - second.astype(F32)).astype(BF16)


def spread_kernel(stacks, out, held, sem):
    copy = pltpu.make_async_copy(stacks, held, sem)
    copy.start()
    copy.wait()
    for n in range(8):
        out[n] = held[n % 2]


def spread_call(stacks):
    return pl.pallas_call(
        spread_kernel,
        name="spread",
        in_specs=[pl.BlockSpec(memory_space=pltpu.HBM)],
        out_specs=VMEM,
        out_shape=shape(8, WIDTH, LANE, dtype=BF16),
        scratch_shapes=[pltpu.VMEM((2, WIDTH, LANE), BF16), pltpu.SemaphoreType.DMA],
        compiler_params=pltpu.CompilerParams(vmem_limit_bytes=LIMIT * MIB),
    )(pltpu.with_memory_space_constraint(stacks, pltpu.HBM))


def split_kernel(place, groups, count, images, ctf, tables, kept, given, parts, turns, held, images_in, ctf_in, sems):
    core = place[3]
    copies = [
        pltpu.make_async_copy(source, target, sems.at[i])
        for i, (source, target) in enumerate(((images, images_in), (ctf, ctf_in), (tables, turns)))
    ]
    for copy in copies:
        copy.start()
    copies[1].wait()
    held[...] = ctf_in[...]
    for i, part in enumerate(cut(ctf_in[...])):
        parts[16 * i : 16 * i + 16, :] = jnp.concatenate([part.astype(F32), jnp.zeros((8, FREQS), F32)], axis=0).astype(BF16)
    copies[0].wait()

    def turn(j, carry):
        kept[:, lanes(j)] = images_in[:, lanes(2 * j + core)]
        given[:, lanes(j)] = images_in[:, lanes(2 * j + 1 - core)]
        return carry

    lax.fori_loop(0, BLOCKS, turn, 0)
    row = lax.broadcasted_iota(jnp.int32, (SLOTS, LANE), 0)
    lane = lax.broadcasted_iota(jnp.int32, (SLOTS, LANE), 1)
    group = jnp.zeros((SLOTS, LANE), jnp.int32)
    for i in range(SLOTS):
        group = jnp.where(row == i, groups[i], group)
    live = jnp.where(row < count[0], 1, 0)
    meta = jnp.where(lane == 0, group, jnp.where(lane == 1, live, 0)).astype(F32).astype(BF16)
    kept[:, DEPTH:] = meta
    given[:, DEPTH:] = meta
    copies[2].wait()


def split_call(place, groups, count, images, ctf, tables):
    half = shape(SLOTS, DEPTH + LANE, dtype=BF16)
    anywhere = pl.BlockSpec(memory_space=pltpu.HBM)
    return pl.pallas_call(
        split_kernel,
        name="split",
        in_specs=[SMEM, SMEM, SMEM, anywhere, anywhere, anywhere],
        out_specs=[VMEM] * 5,
        out_shape=[half, half, shape(48, FREQS, dtype=BF16), shape(2 * HALF, FREQS), shape(GROUPS, FREQS)],
        scratch_shapes=[
            pltpu.VMEM((SLOTS, 2 * DEPTH), BF16),
            pltpu.VMEM((GROUPS, FREQS), F32),
            pltpu.SemaphoreType.DMA((3,)),
        ],
        compiler_params=pltpu.CompilerParams(vmem_limit_bytes=LIMIT * MIB),
    )(place, groups, count, *(pltpu.with_memory_space_constraint(v, pltpu.HBM) for v in (images, ctf, tables)))


def owner_block(place, p):
    later, first, second = p // 16, p % 16 // 4, p % 4
    across = jnp.where(later == 0, first, second)
    along = jnp.where(later == 0, second, place[1] ^ first)
    return (place[0] ^ across) * 8 + along * 2 + later


def build_kernel(place, after, images_a, images_b, parts, turns, *refs):
    outs, (token, rows) = refs[:8], refs[8:]
    core = place[3]
    lane = lax.broadcasted_iota(jnp.int32, (SLOTS, 48), 1)

    def member(k, carry):
        def read(at):
            return jnp.where(k == 0, images_a[:, at].astype(F32), images_b[:, at].astype(F32))

        group = read(slice(DEPTH, DEPTH + LANE))[:, :1]
        hot = jnp.where((group == (lane % 16).astype(F32)) & (lane % 16 < GROUPS), 1.0, 0.0).astype(BF16)
        rows[...] = jnp.dot(hot, parts[...], preferred_element_type=F32)
        for t, out in enumerate(outs):

            def turn(p, carry):
                j = owner_block(place, 4 * t + p)
                at = lanes(2 * (j % 16) + core)
                sign = jnp.where(j < 16, 1.0, -1.0).astype(F32)
                row = rows[:, at]
                first = read(lanes(j)) * row
                second = read(lanes(j ^ 16)) * (row * sign)
                here = lanes(p)
                for s in range(HALF):
                    a = first * turns[s : s + 1, at]
                    b = second * turns[HALF + s : HALF + s + 1, at]
                    pair = jnp.concatenate([a + b, a - b], axis=0).astype(BF16)
                    out[k, 2 * SLOTS * s : 2 * SLOTS * (s + 1), here] = pair
                tail = jnp.concatenate([first, jnp.zeros((ROWS - SLOTS * SHIFTS, LANE), F32)], axis=0)
                out[k, 2 * SLOTS * HALF : ROWS, here] = tail.astype(BF16)
                return carry

            lax.fori_loop(0, 4, turn, 0, unroll=4)
        return carry

    lax.fori_loop(0, 2, member, 0)
    token[...] = jnp.zeros_like(token)


def build_call(place, after, images_a, images_b, parts, turns, name, flops):
    return pl.pallas_call(
        build_kernel,
        name=name,
        in_specs=[SMEM] + [VMEM] * 5,
        out_specs=[VMEM] * 9,
        out_shape=[shape(2, ROWS, CHUNK, dtype=BF16)] * 8 + [shape(8, WIDE)],
        scratch_shapes=[pltpu.VMEM((SLOTS, FREQS), F32)],
        cost_estimate=pl.CostEstimate(flops=flops, bytes_accessed=10**5, transcendentals=0),
        compiler_params=pltpu.CompilerParams(vmem_limit_bytes=LIMIT * MIB),
    )(place, after, images_a, images_b, parts, turns)


def hot_rows(meta):
    group = meta[:, DEPTH : DEPTH + 1].astype(F32)
    lane = lax.broadcasted_iota(jnp.int32, (SLOTS, GROUPS), 1).astype(F32)
    return jnp.where(group == lane, 1.0, 0.0).astype(F32)


def stack_of(piece):
    return jnp.concatenate([piece[r] for r in range(8)], axis=1)


def weigh_kernel(chunks):
    def kernel(place, ctf, after, *refs):
        pieces, power = refs[:-1], refs[-1]
        core = place[3]
        total = jnp.zeros((3 * GROUPS, WIDTH), F32)
        for q, piece in zip(chunks, pieces):
            left = jnp.concatenate([ctf[:, lanes(2 * (((place[0] ^ q) * 8 + r) % 16) + core)] for r in range(8)], axis=1)
            parts = jnp.concatenate([part.astype(F32) for part in cut(left * left)], axis=0).astype(BF16)
            square = stack_of(piece).astype(F32)
            square = square * square
            high = square.astype(BF16)
            low = (square - high.astype(F32)).astype(BF16)
            dims = (((1,), (1,)), ((), ()))
            total = total + lax.dot_general(parts, high, dims, preferred_element_type=F32)
            total = total + lax.dot_general(parts, low, dims, preferred_element_type=F32)
        power[...] = after[:, :WIDTH] + total[:GROUPS] + total[GROUPS : 2 * GROUPS] + total[2 * GROUPS :]

    return kernel


def score_kernel(member):
    def kernel(place, power, meta_a, meta_b, *refs):
        pieces, out = refs[:4], refs[20]
        for k, meta in enumerate((meta_a, meta_b)):
            half = 0.5 * jnp.dot(hot_rows(meta), power[...], precision=HIGHEST, preferred_element_type=F32)
            sums = None
            for t in range(4):
                weights = [pieces[t][2 * n] for n in range(4)] + [pieces[n][2 * (place[1] ^ t) + 1] for n in range(4)]
                shifted = jnp.concatenate([refs[4 + 8 * k + t][member], refs[8 + 8 * k + t][member]], axis=1)
                part = lax.dot_general(
                    shifted, jnp.concatenate(weights, axis=1), (((1,), (1,)), ((), ())), preferred_element_type=F32
                )
                sums = part if sums is None else sums + part
            spare = jnp.zeros((ROWS - SLOTS * SHIFTS, WIDTH), F32)
            out[k, :, :WIDTH] = sums - jnp.concatenate([half] * SHIFTS + [spare], axis=0)

    return kernel


def settle_kernel(place, mine, theirs, stats):
    columns = []
    for k in range(2):

        def value(s):
            at = slice(SLOTS * s, SLOTS * (s + 1))
            return mine[k, at, :WIDTH] + theirs[k, at, :WIDTH]

        best = value(0)
        for s in range(1, SHIFTS):
            best = jnp.maximum(best, value(s))
        top = jnp.max(best, axis=1, keepdims=True)
        total = jnp.exp(value(0) - top)
        for s in range(1, SHIFTS):
            total = total + jnp.exp(value(s) - top)
        columns += [top, jnp.sum(total, axis=1, keepdims=True)]
    lane = lax.broadcasted_iota(jnp.int32, (SLOTS, LANE), 1)
    spread = jnp.where(lane == 0, columns[0], jnp.where(lane == 1, columns[1], jnp.where(lane == 2, columns[2], columns[3])))
    spread = jnp.concatenate([spread, jnp.zeros((LANE - SLOTS, LANE), F32)], axis=0).T[:8, :]
    for d in range(8):
        stats[d] = spread


def posterior_kernel(place, mine, theirs, stats, meta_a, meta_b, low, evidence, spare):
    parity = place[2]
    counted = jnp.zeros((GROUPS, WIDTH), F32)
    for k, meta in ((1, meta_b), (0, meta_a)):
        tops, totals = [], []
        for d in range(8):
            same = (parity == d % 2) == (k == 0)
            here = stats[d, :, :SLOTS]
            tops.append(jnp.where(same, here[0:1], here[2:3]))
            totals.append(jnp.where(same, here[1:2], here[3:4]))
        tops = jnp.concatenate(tops, axis=0)
        totals = jnp.concatenate(totals, axis=0)
        top = jnp.max(tops, axis=0, keepdims=True)
        total = jnp.sum(totals * jnp.exp(tops - top), axis=0, keepdims=True)
        row = lax.broadcasted_iota(jnp.int32, (8, SLOTS), 0)
        columns = jnp.where(row == 0, top, jnp.where(row == 1, total, top + jnp.log(total))).T
        live = meta[:, DEPTH + 1 : DEPTH + 2].astype(F32)
        scale = live / columns[:, 1:2]
        if k == 0:
            known = jnp.where(live > 0.0, columns[:, 2:3], 0.0)
            evidence[...] = jnp.broadcast_to(known, (SLOTS, LANE)).T[:8, :]
        gathered = None
        for s in range(SHIFTS):
            at = slice(SLOTS * s, SLOTS * (s + 1))
            value = jnp.exp(mine[k, at, :WIDTH] + theirs[k, at, :WIDTH] - columns[:, 0:1]) * scale
            spare[at, :] = value
            gathered = value if gathered is None else gathered + value
        hot = hot_rows(meta)
        counted = counted + lax.dot_general(
            hot, gathered, (((0,), (0,)), ((), ())), precision=HIGHEST, preferred_element_type=F32
        )
        spare[SLOTS * SHIFTS :, :] = jnp.zeros((ROWS - SLOTS * SHIFTS, WIDTH), F32)
        if k == 0:
            first = counted.astype(BF16).astype(F32)
            spare[COUNTED : COUNTED + GROUPS, :] = first
            spare[COUNTED + GROUPS : COUNTED + 2 * GROUPS, :] = counted - first
        low[k] = spare[...].T.astype(BF16)


def posterior_call(*args):
    out = [shape(2, WIDTH, ROWS, dtype=BF16), shape(8, SLOTS)]
    return pl.pallas_call(
        posterior_kernel,
        name="posterior",
        in_specs=[SMEM] + [VMEM] * (len(args) - 1),
        out_specs=[VMEM] * 2,
        out_shape=out,
        scratch_shapes=[pltpu.VMEM((ROWS, WIDTH), F32)],
        compiler_params=pltpu.CompilerParams(vmem_limit_bytes=LIMIT * MIB),
    )(*args)


def block_sums(low, groups, put):
    for n in (0, 2):
        at = slice(LANE * n, LANE * (n + 2))
        sums = jnp.dot(low, jnp.concatenate([g[:, at] for g in groups], axis=0), preferred_element_type=F32)
        for r in range(2):
            put(n + r, sums[:, r * LANE : (r + 1) * LANE])


def own_kernel(place, mine, a0, a1, b0, b1, out_a, out_b):
    low = jnp.concatenate([mine[0], mine[1]], axis=1)
    for groups, out in (((a0.at[0], a1.at[0]), out_a), ((b0.at[0], b1.at[0]), out_b)):

        def put(n, value):
            out[n] = value

        block_sums(low, groups, put)


def insert_kernel(chunks, begun=False, joined=False):
    def kernel(place, after, mine, theirs, *refs):
        starts, refs = (refs[:2], refs[2:]) if begun or joined else ((None, None), refs)
        members = (1,) if begun else (0, 1)
        shifted, outs = refs[: 4 * chunks], refs[4 * chunks :]
        lows = [theirs[0], theirs[1]] if begun else [mine[0], theirs[0], mine[1], theirs[1]]
        low = jnp.concatenate(lows, axis=1)
        tail = slice(ROWS - LANE, ROWS)
        first = COUNTED - ROWS + LANE
        both = (mine[0, :, tail].astype(F32) + theirs[0, :, tail].astype(F32)).T
        both = both[first : first + GROUPS] + both[first + GROUPS : first + 2 * GROUPS]
        both = jnp.concatenate([both, jnp.zeros((GROUPS, WIDE - WIDTH), F32)], axis=1)
        both = jnp.concatenate([both[:, :LANE], both[:, LANE:]], axis=0)
        outs[-1][...] = jnp.zeros((8, LANE), F32)
        for i, out in enumerate(outs[:-1]):
            start = starts[i % 2]

            def put(n, value):
                if start is not None:
                    value = value + start[n, :WIDTH].astype(F32)
                out[n, :WIDTH, :] = value.astype(out.dtype)

            block_sums(low, [pair.at[k] for pair in shifted[2 * i : 2 * i + 2] for k in members], put)
            for n in range(4):
                out[n, WIDTH:, :] = (both + start[n, WIDTH:].astype(F32) if joined else both).astype(out.dtype)

    return kernel


def gather_kernel(place, own_a, own_b, one_a, one_b, three_a, three_b, kept_a, kept_b, sent_a, sent_b):
    y = place[1]
    for out, planes in ((kept_a, (y, y ^ 3)), (sent_a, (y ^ 1, y ^ 2))):
        for i, n in enumerate(planes):
            out[i] = (own_a[n] + one_a[n].astype(F32) + three_a[n].astype(F32)).astype(out.dtype)
    for out, planes in ((kept_b, (0, 3)), (sent_b, (1, 2))):
        for i, n in enumerate(planes):
            out[i] = (own_b[n] + one_b[n].astype(F32) + three_b[n].astype(F32)).astype(out.dtype)


def middle_kernel(place, kept_a, kept_b, got_a, got_b, stay, same, other, across):
    side = place[2] == 0
    for out, (i, turned) in ((stay, (0, False)), (same, (1, False)), (other, (0, True)), (across, (1, True))):
        even = kept_a[i] + got_a[i].astype(F32)
        odd = kept_b[i] + got_b[i].astype(F32)
        out[...] = (jnp.where(side, odd, even) if turned else jnp.where(side, even, odd)).astype(out.dtype)


def finish_kernel(place, stay, same, other, across, insertions, weights):
    mine = stay[...] + same[...].astype(F32)
    theirs = other[...].astype(F32) + across[...].astype(F32)
    for k, sums in ((place[2], mine), (1 - place[2], theirs)):
        insertions[k] = sums[:WIDTH]
        weights[k] = jnp.concatenate([sums[WIDTH : WIDTH + GROUPS], sums[WIDTH + GROUPS :]], axis=1)[:, :WIDTH]


def swap(value, axis, d, n=4):
    return lax.ppermute(value, axis, [(i, i ^ d) for i in range(n)])


def body(particle_images, particle_groups, live_counts, ctf_table, projections):
    x, y, zl, core = (lax.axis_index(a) for a in ("grp", "y", "zl", "core"))
    place = jnp.stack([x, y, zl, core]).astype(jnp.int32)
    ring = ("cls", "zl")

    stacks = jnp.transpose(projections, (1, 2, 0))
    column = lax.all_to_all(spread_call(stacks), ("y", "zl"), 0, 0, tiled=True)

    tables = np.concatenate(shift_tables())
    kept, other, parts, turns, ctf = split_call(place, particle_groups, live_counts, particle_images, ctf_table, jnp.asarray(tables))
    halves = [kept, lax.ppermute(other, "core", SWAP)]

    column, to_pair, to_next = lax.optimization_barrier((column, kept, other))
    next_kept = lax.ppermute(to_pair, "zl", SWAP)
    next_other = lax.ppermute(to_next, ring, [(i, (i + 1) % 8 if i % 2 else (i + 7) % 8) for i in range(8)])
    pieces = [column] + [swap(column, "grp", d) for d in (1, 2, 3)]

    built = [build_call(place, column, halves[0], halves[1], parts, turns, "build_here", 6 * 10**9)]
    next_kept, next_other, _ = lax.optimization_barrier((next_kept, next_other, built[0][8]))
    halves += [next_kept, lax.ppermute(next_other, "core", SWAP)]
    built += [build_call(place, column, halves[2], halves[3], parts, turns, "build_next", 10**8)]
    shifted = [b[:8] for b in built]
    tokens = [b[8] for b in built]
    power = call(weigh_kernel((0,)), "weigh_own", shape(GROUPS, WIDTH), (place, ctf, tokens[0], column), LIMIT, 10**8)
    power = call(weigh_kernel((1, 2, 3)), "weigh", shape(GROUPS, WIDTH), (place, ctf, power, *pieces[1:], *tokens[1:]), LIMIT)
    score = shape(2, ROWS, WIDE)
    flops = 4 * ROWS * WIDE * DEPTH
    given = call(score_kernel(1), "score_given", score, (place, power, halves[1], halves[3], *pieces, *shifted[0], *shifted[1]), LIMIT, flops)
    taken = lax.ppermute(given, "core", SWAP)
    kept_score = call(score_kernel(0), "score_own", score, (place, power, halves[0], halves[2], *pieces, *shifted[0], *shifted[1]), LIMIT, flops)
    stats = call(settle_kernel, "settle", shape(8, 8, LANE), (place, kept_score, taken), LIMIT)
    stats = lax.all_to_all(stats, ring, 0, 0, tiled=True)
    low, evidence = posterior_call(place, kept_score, taken, stats, halves[0], halves[2])
    other_low = lax.ppermute(low, "core", SWAP)

    flops = 2 * 4 * ROWS * WIDE * 1024
    token = shape(8, LANE)

    def block(kind):
        return [shape(4, TALL, LANE, dtype=kind)] * 2

    def columns(chunk):
        return [pair[part + chunk] for part in (0, 4) for pair in shifted]

    begun = call(own_kernel, "insert_begin", [shape(4, WIDTH, LANE)] * 2, (place, low, *columns(2)), LIMIT, flops // 2)
    *send, after = call(
        insert_kernel(1, True), "insert_far", [*block(BF16), token], (place, evidence, low, other_low, *begun, *columns(2)), LIMIT, flops // 2
    )
    far = [swap(send[0], "grp", 2), swap(send[1], "y", 2)]
    *send, after = call(
        insert_kernel(2),
        "insert_near",
        [*block(BF16), *block(BF16), token],
        (place, after, low, other_low, *columns(1), *columns(3)),
        LIMIT,
        2 * flops,
    )
    near = [swap(send[0], "grp", 1), swap(send[1], "y", 1), swap(send[2], "grp", 3), swap(send[3], "y", 3)]
    *own, _ = call(
        insert_kernel(1, joined=True), "insert_own", [*block(F32), token], (place, after, low, other_low, *far, *columns(0)), LIMIT, flops
    )
    pair = (2, TALL, LANE)
    out = [shape(*pair)] * 2 + [shape(*pair, dtype=BF16)] * 2
    *kept, send_a, send_b = call(gather_kernel, "gather", out, (place, *own, *near), LIMIT)
    out = [shape(*pair[1:])] + [shape(*pair[1:], dtype=BF16)] * 3
    stay, *sent = call(middle_kernel, "middle", out, (place, *kept, swap(send_a, "y", 1), swap(send_b, "grp", 1)), LIMIT)
    plane = ("grp", "y", "zl")
    spots = [(i, j, k) for i in range(4) for j in range(4) for k in range(2)]

    def number(i, j, k):
        return i * 8 + j * 2 + k

    def turn(i, j, side):
        return (i, j ^ 3) if side == 0 else (i ^ 3, j)

    same = lax.ppermute(sent[0], plane, [(number(i, j, k), number(*turn(i, j, k), k)) for i, j, k in spots])
    other = lax.ppermute(sent[1], plane, [(number(i, j, k), number(i, j, 1 - k)) for i, j, k in spots])
    across = lax.ppermute(sent[2], plane, [(number(i, j, k), number(*turn(i, j, 1 - k), 1 - k)) for i, j, k in spots])
    insertions, tally = call(finish_kernel, "finish", [shape(2, WIDTH, LANE), shape(2, GROUPS, WIDTH)], (place, stay, same, other, across), LIMIT)
    return insertions, tally, evidence[0]


def solution(mesh):
    fine = Mesh(mesh.devices.reshape(4, 4, 4, 2, 2), ("cls", "grp", "y", "zl", "core"))
    shards = ("grp", "y", "zl", "core")
    return jax.shard_map(
        body,
        mesh=fine,
        in_specs=(P(shards, None), P(shards), P(shards), P(), P(shards, "cls", None)),
        out_specs=(P("cls", None, shards), P("cls", None, None), P(shards)),
        check_vma=False,
    )
```

```python
import math

import jax
import jax.numpy as jnp
import numpy as np
from jax import lax
from jax.experimental import pallas as pl
from jax.experimental.pallas import tpu as pltpu
from jax.sharding import Mesh, PartitionSpec as P

IMG = 64
SIDE = 5
SHIFTS = SIDE * SIDE
HALF = SHIFTS // 2
GROUPS = 8
FREQS = IMG * IMG
LANE = 128
SLOTS = 40
ROWS = 1024
WIDTH = 200
WIDE = 256
TALL = WIDTH + 16
COUNTED = SLOTS * SHIFTS
BLOCKS = 32
DEPTH = BLOCKS * LANE
CHUNK = DEPTH // 8
HIGHEST = lax.Precision.HIGHEST
F32 = jnp.float32
BF16 = jnp.bfloat16
MIB = 2**20
LIMIT = 4
VMEM = pl.BlockSpec(memory_space=pltpu.VMEM)
SMEM = pl.BlockSpec(memory_space=pltpu.SMEM)
SWAP = [(0, 1), (1, 0)]


def shift_tables():
    index = np.arange(FREQS)
    shift = np.arange(HALF)
    offx = shift // SIDE - SIDE // 2
    offy = shift % SIDE - SIDE // 2
    phase = (offx[:, None] * (index // IMG)[None, :] + offy[:, None] * (index % IMG)[None, :]) % IMG
    theta = (phase.astype(np.float32) * np.float32(2.0 * math.pi / IMG)).astype(np.float64)
    return np.cos(theta).astype(np.float32), np.sin(theta).astype(np.float32)


def call(kernel, name, out, args, limit, flops=0, moved=0):
    return pl.pallas_call(
        kernel,
        name=name,
        in_specs=[SMEM] + [VMEM] * (len(args) - 1),
        out_specs=jax.tree.map(lambda _: VMEM, out),
        out_shape=out,
        cost_estimate=pl.CostEstimate(flops=flops, bytes_accessed=moved, transcendentals=0),
        compiler_params=pltpu.CompilerParams(vmem_limit_bytes=limit * MIB),
    )(*args)


def shape(*dims, dtype=F32):
    return jax.ShapeDtypeStruct(dims, dtype)


def lanes(block):
    return pl.ds(pl.multiple_of(block * LANE, LANE), LANE)


def cut(value):
    first = value.astype(BF16)
    rest = value - first.astype(F32)
    second = rest.astype(BF16)
    return first, second, (rest - second.astype(F32)).astype(BF16)


def spread_kernel(stacks, out, held, sem):
    copy = pltpu.make_async_copy(stacks, held, sem)
    copy.start()
    copy.wait()
    for n in range(8):
        out[n] = held[n % 2]


def spread_call(stacks):
    return pl.pallas_call(
        spread_kernel,
        name="spread",
        in_specs=[pl.BlockSpec(memory_space=pltpu.HBM)],
        out_specs=VMEM,
        out_shape=shape(8, WIDTH, LANE, dtype=BF16),
        scratch_shapes=[pltpu.VMEM((2, WIDTH, LANE), BF16), pltpu.SemaphoreType.DMA],
        compiler_params=pltpu.CompilerParams(vmem_limit_bytes=LIMIT * MIB),
    )(pltpu.with_memory_space_constraint(stacks, pltpu.HBM))


def split_kernel(place, groups, count, images, ctf, tables, kept, given, parts, turns, held, images_in, ctf_in, sems):
    core = place[3]
    copies = [
        pltpu.make_async_copy(source, target, sems.at[i])
        for i, (source, target) in enumerate(((images, images_in), (ctf, ctf_in), (tables, turns)))
    ]
    for copy in copies:
        copy.start()
    copies[1].wait()
    held[...] = ctf_in[...]
    for i, part in enumerate(cut(ctf_in[...])):
        parts[16 * i : 16 * i + 16, :] = jnp.concatenate([part.astype(F32), jnp.zeros((8, FREQS), F32)], axis=0).astype(BF16)
    copies[0].wait()

    def turn(j, carry):
        kept[:, lanes(j)] = images_in[:, lanes(2 * j + core)]
        given[:, lanes(j)] = images_in[:, lanes(2 * j + 1 - core)]
        return carry

    lax.fori_loop(0, BLOCKS, turn, 0)
    row = lax.broadcasted_iota(jnp.int32, (SLOTS, LANE), 0)
    lane = lax.broadcasted_iota(jnp.int32, (SLOTS, LANE), 1)
    group = jnp.zeros((SLOTS, LANE), jnp.int32)
    for i in range(SLOTS):
        group = jnp.where(row == i, groups[i], group)
    live = jnp.where(row < count[0], 1, 0)
    meta = jnp.where(lane == 0, group, jnp.where(lane == 1, live, 0)).astype(F32).astype(BF16)
    kept[:, DEPTH:] = meta
    given[:, DEPTH:] = meta
    copies[2].wait()


def split_call(place, groups, count, images, ctf, tables):
    half = shape(SLOTS, DEPTH + LANE, dtype=BF16)
    anywhere = pl.BlockSpec(memory_space=pltpu.HBM)
    return pl.pallas_call(
        split_kernel,
        name="split",
        in_specs=[SMEM, SMEM, SMEM, anywhere, anywhere, anywhere],
        out_specs=[VMEM] * 5,
        out_shape=[half, half, shape(48, FREQS, dtype=BF16), shape(2 * HALF, FREQS), shape(GROUPS, FREQS)],
        scratch_shapes=[
            pltpu.VMEM((SLOTS, 2 * DEPTH), BF16),
            pltpu.VMEM((GROUPS, FREQS), F32),
            pltpu.SemaphoreType.DMA((3,)),
        ],
        compiler_params=pltpu.CompilerParams(vmem_limit_bytes=LIMIT * MIB),
    )(place, groups, count, *(pltpu.with_memory_space_constraint(v, pltpu.HBM) for v in (images, ctf, tables)))


def owner_block(place, p):
    later, first, second = p // 16, p % 16 // 4, p % 4
    across = jnp.where(later == 0, first, second)
    along = jnp.where(later == 0, second, place[1] ^ first)
    return (place[0] ^ across) * 8 + along * 2 + later


def build_kernel(place, after, images_a, images_b, parts, turns, *refs):
    outs, (token, rows) = refs[:8], refs[8:]
    core = place[3]
    lane = lax.broadcasted_iota(jnp.int32, (SLOTS, 48), 1)

    def member(k, carry):
        def read(at):
            return jnp.where(k == 0, images_a[:, at].astype(F32), images_b[:, at].astype(F32))

        group = read(slice(DEPTH, DEPTH + LANE))[:, :1]
        hot = jnp.where((group == (lane % 16).astype(F32)) & (lane % 16 < GROUPS), 1.0, 0.0).astype(BF16)
        rows[...] = jnp.dot(hot, parts[...], preferred_element_type=F32)
        for t, out in enumerate(outs):

            def turn(p, carry):
                j = owner_block(place, 4 * t + p)
                at = lanes(2 * (j % 16) + core)
                sign = jnp.where(j < 16, 1.0, -1.0).astype(F32)
                row = rows[:, at]
                first = read(lanes(j)) * row
                second = read(lanes(j ^ 16)) * (row * sign)
                here = lanes(p)
                for s in range(HALF):
                    a = first * turns[s : s + 1, at]
                    b = second * turns[HALF + s : HALF + s + 1, at]
                    pair = jnp.concatenate([a + b, a - b], axis=0).astype(BF16)
                    out[k, 2 * SLOTS * s : 2 * SLOTS * (s + 1), here] = pair
                tail = jnp.concatenate([first, jnp.zeros((ROWS - SLOTS * SHIFTS, LANE), F32)], axis=0)
                out[k, 2 * SLOTS * HALF : ROWS, here] = tail.astype(BF16)
                return carry

            lax.fori_loop(0, 4, turn, 0, unroll=4)
        return carry

    lax.fori_loop(0, 2, member, 0)
    token[...] = jnp.zeros_like(token)


def build_call(place, after, images_a, images_b, parts, turns, name, flops):
    return pl.pallas_call(
        build_kernel,
        name=name,
        in_specs=[SMEM] + [VMEM] * 5,
        out_specs=[VMEM] * 9,
        out_shape=[shape(2, ROWS, CHUNK, dtype=BF16)] * 8 + [shape(8, WIDE)],
        scratch_shapes=[pltpu.VMEM((SLOTS, FREQS), F32)],
        cost_estimate=pl.CostEstimate(flops=flops, bytes_accessed=10**5, transcendentals=0),
        compiler_params=pltpu.CompilerParams(vmem_limit_bytes=LIMIT * MIB),
    )(place, after, images_a, images_b, parts, turns)


def hot_rows(meta):
    group = meta[:, DEPTH : DEPTH + 1].astype(F32)
    lane = lax.broadcasted_iota(jnp.int32, (SLOTS, GROUPS), 1).astype(F32)
    return jnp.where(group == lane, 1.0, 0.0).astype(F32)


def stack_of(piece):
    return jnp.concatenate([piece[r] for r in range(8)], axis=1)


def weigh_kernel(chunks):
    def kernel(place, ctf, after, *refs):
        pieces, power = refs[:-1], refs[-1]
        core = place[3]
        total = jnp.zeros((3 * GROUPS, WIDTH), F32)
        for q, piece in zip(chunks, pieces):
            left = jnp.concatenate([ctf[:, lanes(2 * (((place[0] ^ q) * 8 + r) % 16) + core)] for r in range(8)], axis=1)
            parts = jnp.concatenate([part.astype(F32) for part in cut(left * left)], axis=0).astype(BF16)
            square = stack_of(piece).astype(F32)
            square = square * square
            high = square.astype(BF16)
            low = (square - high.astype(F32)).astype(BF16)
            dims = (((1,), (1,)), ((), ()))
            total = total + lax.dot_general(parts, high, dims, preferred_element_type=F32)
            total = total + lax.dot_general(parts, low, dims, preferred_element_type=F32)
        power[...] = after[:, :WIDTH] + total[:GROUPS] + total[GROUPS : 2 * GROUPS] + total[2 * GROUPS :]

    return kernel


def score_kernel(member):
    def kernel(place, power, meta_a, meta_b, *refs):
        pieces, out = refs[:4], refs[20]
        for k, meta in enumerate((meta_a, meta_b)):
            half = 0.5 * jnp.dot(hot_rows(meta), power[...], precision=HIGHEST, preferred_element_type=F32)
            sums = None
            for t in range(4):
                weights = [pieces[t][2 * n] for n in range(4)] + [pieces[n][2 * (place[1] ^ t) + 1] for n in range(4)]
                shifted = jnp.concatenate([refs[4 + 8 * k + t][member], refs[8 + 8 * k + t][member]], axis=1)
                part = lax.dot_general(
                    shifted, jnp.concatenate(weights, axis=1), (((1,), (1,)), ((), ())), preferred_element_type=F32
                )
                sums = part if sums is None else sums + part
            spare = jnp.zeros((ROWS - SLOTS * SHIFTS, WIDTH), F32)
            out[k, :, :WIDTH] = sums - jnp.concatenate([half] * SHIFTS + [spare], axis=0)

    return kernel


def settle_kernel(place, mine, theirs, stats):
    columns = []
    for k in range(2):

        def value(s):
            at = slice(SLOTS * s, SLOTS * (s + 1))
            return mine[k, at, :WIDTH] + theirs[k, at, :WIDTH]

        best = value(0)
        for s in range(1, SHIFTS):
            best = jnp.maximum(best, value(s))
        top = jnp.max(best, axis=1, keepdims=True)
        total = jnp.exp(value(0) - top)
        for s in range(1, SHIFTS):
            total = total + jnp.exp(value(s) - top)
        columns += [top, jnp.sum(total, axis=1, keepdims=True)]
    lane = lax.broadcasted_iota(jnp.int32, (SLOTS, LANE), 1)
    spread = jnp.where(lane == 0, columns[0], jnp.where(lane == 1, columns[1], jnp.where(lane == 2, columns[2], columns[3])))
    spread = jnp.concatenate([spread, jnp.zeros((LANE - SLOTS, LANE), F32)], axis=0).T[:8, :]
    for d in range(8):
        stats[d] = spread


def posterior_kernel(place, mine, theirs, stats, meta_a, meta_b, low, evidence, spare):
    parity = place[2]
    counted = jnp.zeros((GROUPS, WIDTH), F32)
    for k, meta in ((1, meta_b), (0, meta_a)):
        tops, totals = [], []
        for d in range(8):
            same = (parity == d % 2) == (k == 0)
            here = stats[d, :, :SLOTS]
            tops.append(jnp.where(same, here[0:1], here[2:3]))
            totals.append(jnp.where(same, here[1:2], here[3:4]))
        tops = jnp.concatenate(tops, axis=0)
        totals = jnp.concatenate(totals, axis=0)
        top = jnp.max(tops, axis=0, keepdims=True)
        total = jnp.sum(totals * jnp.exp(tops - top), axis=0, keepdims=True)
        row = lax.broadcasted_iota(jnp.int32, (8, SLOTS), 0)
        columns = jnp.where(row == 0, top, jnp.where(row == 1, total, top + jnp.log(total))).T
        live = meta[:, DEPTH + 1 : DEPTH + 2].astype(F32)
        scale = live / columns[:, 1:2]
        if k == 0:
            known = jnp.where(live > 0.0, columns[:, 2:3], 0.0)
            evidence[...] = jnp.broadcast_to(known, (SLOTS, LANE)).T[:8, :]
        gathered = None
        for s in range(SHIFTS):
            at = slice(SLOTS * s, SLOTS * (s + 1))
            value = jnp.exp(mine[k, at, :WIDTH] + theirs[k, at, :WIDTH] - columns[:, 0:1]) * scale
            spare[at, :] = value
            gathered = value if gathered is None else gathered + value
        hot = hot_rows(meta)
        counted = counted + lax.dot_general(
            hot, gathered, (((0,), (0,)), ((), ())), precision=HIGHEST, preferred_element_type=F32
        )
        spare[SLOTS * SHIFTS :, :] = jnp.zeros((ROWS - SLOTS * SHIFTS, WIDTH), F32)
        if k == 0:
            first = counted.astype(BF16).astype(F32)
            spare[COUNTED : COUNTED + GROUPS, :] = first
            spare[COUNTED + GROUPS : COUNTED + 2 * GROUPS, :] = counted - first
        low[k] = spare[...].T.astype(BF16)


def posterior_call(*args):
    out = [shape(2, WIDTH, ROWS, dtype=BF16), shape(8, SLOTS)]
    return pl.pallas_call(
        posterior_kernel,
        name="posterior",
        in_specs=[SMEM] + [VMEM] * (len(args) - 1),
        out_specs=[VMEM] * 2,
        out_shape=out,
        scratch_shapes=[pltpu.VMEM((ROWS, WIDTH), F32)],
        compiler_params=pltpu.CompilerParams(vmem_limit_bytes=LIMIT * MIB),
    )(*args)


def block_sums(low, groups, put):
    for n in (0, 2):
        at = slice(LANE * n, LANE * (n + 2))
        sums = jnp.dot(low, jnp.concatenate([g[:, at] for g in groups], axis=0), preferred_element_type=F32)
        for r in range(2):
            put(n + r, sums[:, r * LANE : (r + 1) * LANE])


def own_kernel(place, mine, a0, a1, b0, b1, out_a, out_b):
    low = jnp.concatenate([mine[0], mine[1]], axis=1)
    for groups, out in (((a0.at[0], a1.at[0]), out_a), ((b0.at[0], b1.at[0]), out_b)):

        def put(n, value):
            out[n] = value

        block_sums(low, groups, put)


def insert_kernel(chunks, begun=False, joined=False):
    def kernel(place, after, mine, theirs, *refs):
        starts, refs = (refs[:2], refs[2:]) if begun or joined else ((None, None), refs)
        members = (1,) if begun else (0, 1)
        shifted, outs = refs[: 4 * chunks], refs[4 * chunks :]
        lows = [theirs[0], theirs[1]] if begun else [mine[0], theirs[0], mine[1], theirs[1]]
        low = jnp.concatenate(lows, axis=1)
        tail = slice(ROWS - LANE, ROWS)
        first = COUNTED - ROWS + LANE
        both = (mine[0, :, tail].astype(F32) + theirs[0, :, tail].astype(F32)).T
        both = both[first : first + GROUPS] + both[first + GROUPS : first + 2 * GROUPS]
        both = jnp.concatenate([both, jnp.zeros((GROUPS, WIDE - WIDTH), F32)], axis=1)
        both = jnp.concatenate([both[:, :LANE], both[:, LANE:]], axis=0)
        outs[-1][...] = jnp.zeros((8, LANE), F32)
        for i, out in enumerate(outs[:-1]):
            start = starts[i % 2]

            def put(n, value):
                if start is not None:
                    value = value + start[n, :WIDTH].astype(F32)
                out[n, :WIDTH, :] = value.astype(out.dtype)

            block_sums(low, [pair.at[k] for pair in shifted[2 * i : 2 * i + 2] for k in members], put)
            for n in range(4):
                out[n, WIDTH:, :] = (both + start[n, WIDTH:].astype(F32) if joined else both).astype(out.dtype)

    return kernel


def gather_kernel(place, own_a, own_b, one_a, one_b, three_a, three_b, kept_a, kept_b, sent_a, sent_b):
    y = place[1]
    for out, planes in ((kept_a, (y, y ^ 3)), (sent_a, (y ^ 1, y ^ 2))):
        for i, n in enumerate(planes):
            out[i] = (own_a[n] + one_a[n].astype(F32) + three_a[n].astype(F32)).astype(out.dtype)
    for out, planes in ((kept_b, (0, 3)), (sent_b, (1, 2))):
        for i, n in enumerate(planes):
            out[i] = (own_b[n] + one_b[n].astype(F32) + three_b[n].astype(F32)).astype(out.dtype)


def middle_kernel(place, kept_a, kept_b, got_a, got_b, stay, same, other, across):
    side = place[2] == 0
    for out, (i, turned) in ((stay, (0, False)), (same, (1, False)), (other, (0, True)), (across, (1, True))):
        even = kept_a[i] + got_a[i].astype(F32)
        odd = kept_b[i] + got_b[i].astype(F32)
        out[...] = (jnp.where(side, odd, even) if turned else jnp.where(side, even, odd)).astype(out.dtype)


def finish_kernel(place, stay, same, other, across, insertions, weights):
    mine = stay[...] + same[...].astype(F32)
    theirs = other[...].astype(F32) + across[...].astype(F32)
    for k, sums in ((place[2], mine), (1 - place[2], theirs)):
        insertions[k] = sums[:WIDTH]
        weights[k] = jnp.concatenate([sums[WIDTH : WIDTH + GROUPS], sums[WIDTH + GROUPS :]], axis=1)[:, :WIDTH]


def swap(value, axis, d, n=4):
    return lax.ppermute(value, axis, [(i, i ^ d) for i in range(n)])


def body(particle_images, particle_groups, live_counts, ctf_table, projections):
    x, y, zl, core = (lax.axis_index(a) for a in ("grp", "y", "zl", "core"))
    place = jnp.stack([x, y, zl, core]).astype(jnp.int32)
    ring = ("cls", "zl")

    stacks = jnp.transpose(projections, (1, 2, 0))
    column = lax.all_to_all(spread_call(stacks), ("y", "zl"), 0, 0, tiled=True)

    tables = np.concatenate(shift_tables())
    kept, other, parts, turns, ctf = split_call(place, particle_groups, live_counts, particle_images, ctf_table, jnp.asarray(tables))
    halves = [kept, lax.ppermute(other, "core", SWAP)]

    column, to_pair, to_next = lax.optimization_barrier((column, kept, other))
    next_kept = lax.ppermute(to_pair, "zl", SWAP)
    next_other = lax.ppermute(to_next, ring, [(i, (i + 1) % 8 if i % 2 else (i + 7) % 8) for i in range(8)])
    first, third, second = (swap(column, "grp", d) for d in (1, 3, 2))
    pieces = [column, first, second, third]

    built = [build_call(place, column, halves[0], halves[1], parts, turns, "build_here", 6 * 10**9)]
    next_kept, next_other, _ = lax.optimization_barrier((next_kept, next_other, built[0][8]))
    halves += [next_kept, lax.ppermute(next_other, "core", SWAP)]
    built += [build_call(place, column, halves[2], halves[3], parts, turns, "build_next", 10**8)]
    shifted = [b[:8] for b in built]
    tokens = [b[8] for b in built]
    power = call(weigh_kernel((0,)), "weigh_own", shape(GROUPS, WIDTH), (place, ctf, tokens[0], column), LIMIT, 10**8)
    power = call(weigh_kernel((1, 3, 2)), "weigh", shape(GROUPS, WIDTH), (place, ctf, power, pieces[1], pieces[3], pieces[2], *tokens[1:]), LIMIT)
    score = shape(2, ROWS, WIDE)
    flops = 4 * ROWS * WIDE * DEPTH
    given = call(score_kernel(1), "score_given", score, (place, power, halves[1], halves[3], *pieces, *shifted[0], *shifted[1]), LIMIT, flops)
    taken = lax.ppermute(given, "core", SWAP)
    kept_score = call(score_kernel(0), "score_own", score, (place, power, halves[0], halves[2], *pieces, *shifted[0], *shifted[1]), LIMIT, flops)
    stats = call(settle_kernel, "settle", shape(8, 8, LANE), (place, kept_score, taken), LIMIT)
    stats = lax.all_to_all(stats, ring, 0, 0, tiled=True)
    low, evidence = posterior_call(place, kept_score, taken, stats, halves[0], halves[2])
    other_low = lax.ppermute(low, "core", SWAP)

    flops = 2 * 4 * ROWS * WIDE * 1024
    token = shape(8, LANE)

    def block(kind):
        return [shape(4, TALL, LANE, dtype=kind)] * 2

    def columns(chunk):
        return [pair[part + chunk] for part in (0, 4) for pair in shifted]

    begun = call(own_kernel, "insert_begin", [shape(4, WIDTH, LANE)] * 2, (place, low, *columns(2)), LIMIT, flops // 2)
    *send, after = call(
        insert_kernel(1, True), "insert_far", [*block(BF16), token], (place, evidence, low, other_low, *begun, *columns(2)), LIMIT, flops // 2
    )
    far = [swap(send[0], "grp", 2), swap(send[1], "y", 2)]
    *send, after = call(
        insert_kernel(2),
        "insert_near",
        [*block(BF16), *block(BF16), token],
        (place, after, low, other_low, *columns(1), *columns(3)),
        LIMIT,
        2 * flops,
    )
    near = [swap(send[0], "grp", 1), swap(send[1], "y", 1), swap(send[2], "grp", 3), swap(send[3], "y", 3)]
    *own, _ = call(
        insert_kernel(1, joined=True), "insert_own", [*block(F32), token], (place, after, low, other_low, *far, *columns(0)), LIMIT, flops
    )
    pair = (2, TALL, LANE)
    out = [shape(*pair)] * 2 + [shape(*pair, dtype=BF16)] * 2
    *kept, send_a, send_b = call(gather_kernel, "gather", out, (place, *own, *near), LIMIT)
    out = [shape(*pair[1:])] + [shape(*pair[1:], dtype=BF16)] * 3
    stay, *sent = call(middle_kernel, "middle", out, (place, *kept, swap(send_a, "y", 1), swap(send_b, "grp", 1)), LIMIT)
    plane = ("grp", "y", "zl")
    spots = [(i, j, k) for i in range(4) for j in range(4) for k in range(2)]

    def number(i, j, k):
        return i * 8 + j * 2 + k

    def turn(i, j, side):
        return (i, j ^ 3) if side == 0 else (i ^ 3, j)

    same = lax.ppermute(sent[0], plane, [(number(i, j, k), number(*turn(i, j, k), k)) for i, j, k in spots])
    other = lax.ppermute(sent[1], plane, [(number(i, j, k), number(i, j, 1 - k)) for i, j, k in spots])
    across = lax.ppermute(sent[2], plane, [(number(i, j, k), number(*turn(i, j, 1 - k), 1 - k)) for i, j, k in spots])
    insertions, tally = call(finish_kernel, "finish", [shape(2, WIDTH, LANE), shape(2, GROUPS, WIDTH)], (place, stay, same, other, across), LIMIT)
    return insertions, tally, evidence[0]


def solution(mesh):
    fine = Mesh(mesh.devices.reshape(4, 4, 4, 2, 2), ("cls", "grp", "y", "zl", "core"))
    shards = ("grp", "y", "zl", "core")
    return jax.shard_map(
        body,
        mesh=fine,
        in_specs=(P(shards, None), P(shards), P(shards), P(), P(shards, "cls", None)),
        out_specs=(P("cls", None, shards), P("cls", None, None), P(shards)),
        check_vma=False,
    )
```

```python
import math

import jax
import jax.numpy as jnp
import numpy as np
from jax import lax
from jax.experimental import pallas as pl
from jax.experimental.pallas import tpu as pltpu
from jax.sharding import Mesh, PartitionSpec as P

IMG = 64
SIDE = 5
SHIFTS = SIDE * SIDE
HALF = SHIFTS // 2
GROUPS = 8
FREQS = IMG * IMG
LANE = 128
SLOTS = 40
ROWS = 1024
WIDTH = 200
WIDE = 256
TALL = WIDTH + 16
COUNTED = SLOTS * SHIFTS
BLOCKS = 32
DEPTH = BLOCKS * LANE
CHUNK = DEPTH // 8
HIGHEST = lax.Precision.HIGHEST
F32 = jnp.float32
BF16 = jnp.bfloat16
MIB = 2**20
LIMIT = 4
VMEM = pl.BlockSpec(memory_space=pltpu.VMEM)
SMEM = pl.BlockSpec(memory_space=pltpu.SMEM)
SWAP = [(0, 1), (1, 0)]


def shift_tables():
    index = np.arange(FREQS)
    shift = np.arange(HALF)
    offx = shift // SIDE - SIDE // 2
    offy = shift % SIDE - SIDE // 2
    phase = (offx[:, None] * (index // IMG)[None, :] + offy[:, None] * (index % IMG)[None, :]) % IMG
    theta = (phase.astype(np.float32) * np.float32(2.0 * math.pi / IMG)).astype(np.float64)
    return np.cos(theta).astype(np.float32), np.sin(theta).astype(np.float32)


def call(kernel, name, out, args, limit, flops=0, moved=0):
    return pl.pallas_call(
        kernel,
        name=name,
        in_specs=[SMEM] + [VMEM] * (len(args) - 1),
        out_specs=jax.tree.map(lambda _: VMEM, out),
        out_shape=out,
        cost_estimate=pl.CostEstimate(flops=flops, bytes_accessed=moved, transcendentals=0),
        compiler_params=pltpu.CompilerParams(vmem_limit_bytes=limit * MIB),
    )(*args)


def shape(*dims, dtype=F32):
    return jax.ShapeDtypeStruct(dims, dtype)


def lanes(block):
    return pl.ds(pl.multiple_of(block * LANE, LANE), LANE)


def cut(value):
    first = value.astype(BF16)
    rest = value - first.astype(F32)
    second = rest.astype(BF16)
    return first, second, (rest - second.astype(F32)).astype(BF16)


def spread_kernel(stacks, out, held, sem):
    copy = pltpu.make_async_copy(stacks, held, sem)
    copy.start()
    copy.wait()
    for n in range(8):
        out[n] = held[n % 2]


def spread_call(stacks):
    return pl.pallas_call(
        spread_kernel,
        name="spread",
        in_specs=[pl.BlockSpec(memory_space=pltpu.HBM)],
        out_specs=VMEM,
        out_shape=shape(8, WIDTH, LANE, dtype=BF16),
        scratch_shapes=[pltpu.VMEM((2, WIDTH, LANE), BF16), pltpu.SemaphoreType.DMA],
        compiler_params=pltpu.CompilerParams(vmem_limit_bytes=LIMIT * MIB),
    )(pltpu.with_memory_space_constraint(stacks, pltpu.HBM))


def split_kernel(place, groups, count, images, ctf, tables, kept, given, parts, turns, held, images_in, ctf_in, sems):
    core = place[3]
    copies = [
        pltpu.make_async_copy(source, target, sems.at[i])
        for i, (source, target) in enumerate(((images, images_in), (ctf, ctf_in), (tables, turns)))
    ]
    for copy in copies:
        copy.start()
    copies[1].wait()
    held[...] = ctf_in[...]
    for i, part in enumerate(cut(ctf_in[...])):
        parts[16 * i : 16 * i + 16, :] = jnp.concatenate([part.astype(F32), jnp.zeros((8, FREQS), F32)], axis=0).astype(BF16)
    copies[0].wait()

    def turn(j, carry):
        kept[:, lanes(j)] = images_in[:, lanes(2 * j + core)]
        given[:, lanes(j)] = images_in[:, lanes(2 * j + 1 - core)]
        return carry

    lax.fori_loop(0, BLOCKS, turn, 0)
    row = lax.broadcasted_iota(jnp.int32, (SLOTS, LANE), 0)
    lane = lax.broadcasted_iota(jnp.int32, (SLOTS, LANE), 1)
    group = jnp.zeros((SLOTS, LANE), jnp.int32)
    for i in range(SLOTS):
        group = jnp.where(row == i, groups[i], group)
    live = jnp.where(row < count[0], 1, 0)
    meta = jnp.where(lane == 0, group, jnp.where(lane == 1, live, 0)).astype(F32).astype(BF16)
    kept[:, DEPTH:] = meta
    given[:, DEPTH:] = meta
    copies[2].wait()


def split_call(place, groups, count, images, ctf, tables):
    half = shape(SLOTS, DEPTH + LANE, dtype=BF16)
    anywhere = pl.BlockSpec(memory_space=pltpu.HBM)
    return pl.pallas_call(
        split_kernel,
        name="split",
        in_specs=[SMEM, SMEM, SMEM, anywhere, anywhere, anywhere],
        out_specs=[VMEM] * 5,
        out_shape=[half, half, shape(48, FREQS, dtype=BF16), shape(2 * HALF, FREQS), shape(GROUPS, FREQS)],
        scratch_shapes=[
            pltpu.VMEM((SLOTS, 2 * DEPTH), BF16),
            pltpu.VMEM((GROUPS, FREQS), F32),
            pltpu.SemaphoreType.DMA((3,)),
        ],
        compiler_params=pltpu.CompilerParams(vmem_limit_bytes=LIMIT * MIB),
    )(place, groups, count, *(pltpu.with_memory_space_constraint(v, pltpu.HBM) for v in (images, ctf, tables)))


def owner_block(place, p):
    later, first, second = p // 16, p % 16 // 4, p % 4
    across = jnp.where(later == 0, first, second)
    along = jnp.where(later == 0, second, place[1] ^ first)
    return (place[0] ^ across) * 8 + along * 2 + later


def build_kernel(place, after, images_a, images_b, parts, turns, *refs):
    outs, (token, rows) = refs[:8], refs[8:]
    core = place[3]
    lane = lax.broadcasted_iota(jnp.int32, (SLOTS, 48), 1)

    def member(k, carry):
        def read(at):
            return jnp.where(k == 0, images_a[:, at].astype(F32), images_b[:, at].astype(F32))

        group = read(slice(DEPTH, DEPTH + LANE))[:, :1]
        hot = jnp.where((group == (lane % 16).astype(F32)) & (lane % 16 < GROUPS), 1.0, 0.0).astype(BF16)
        rows[...] = jnp.dot(hot, parts[...], preferred_element_type=F32)
        for t, out in enumerate(outs):

            def turn(p, carry):
                j = owner_block(place, 4 * t + p)
                at = lanes(2 * (j % 16) + core)
                sign = jnp.where(j < 16, 1.0, -1.0).astype(F32)
                row = rows[:, at]
                first = read(lanes(j)) * row
                second = read(lanes(j ^ 16)) * (row * sign)
                here = lanes(p)
                for s in range(HALF):
                    a = first * turns[s : s + 1, at]
                    b = second * turns[HALF + s : HALF + s + 1, at]
                    pair = jnp.concatenate([a + b, a - b], axis=0).astype(BF16)
                    out[k, 2 * SLOTS * s : 2 * SLOTS * (s + 1), here] = pair
                tail = jnp.concatenate([first, jnp.zeros((ROWS - SLOTS * SHIFTS, LANE), F32)], axis=0)
                out[k, 2 * SLOTS * HALF : ROWS, here] = tail.astype(BF16)
                return carry

            lax.fori_loop(0, 4, turn, 0, unroll=4)
        return carry

    lax.fori_loop(0, 2, member, 0)
    token[...] = jnp.zeros_like(token)


def build_call(place, after, images_a, images_b, parts, turns, name, flops):
    return pl.pallas_call(
        build_kernel,
        name=name,
        in_specs=[SMEM] + [VMEM] * 5,
        out_specs=[VMEM] * 9,
        out_shape=[shape(2, ROWS, CHUNK, dtype=BF16)] * 8 + [shape(8, WIDE)],
        scratch_shapes=[pltpu.VMEM((SLOTS, FREQS), F32)],
        cost_estimate=pl.CostEstimate(flops=flops, bytes_accessed=10**5, transcendentals=0),
        compiler_params=pltpu.CompilerParams(vmem_limit_bytes=LIMIT * MIB),
    )(place, after, images_a, images_b, parts, turns)


def hot_rows(meta):
    group = meta[:, DEPTH : DEPTH + 1].astype(F32)
    lane = lax.broadcasted_iota(jnp.int32, (SLOTS, GROUPS), 1).astype(F32)
    return jnp.where(group == lane, 1.0, 0.0).astype(F32)


def stack_of(piece):
    return jnp.concatenate([piece[r] for r in range(8)], axis=1)


def weigh_kernel(chunks):
    def kernel(place, ctf, after, *refs):
        pieces, power = refs[:-1], refs[-1]
        core = place[3]
        total = jnp.zeros((3 * GROUPS, WIDTH), F32)
        for q, piece in zip(chunks, pieces):
            left = jnp.concatenate([ctf[:, lanes(2 * (((place[0] ^ q) * 8 + r) % 16) + core)] for r in range(8)], axis=1)
            parts = jnp.concatenate([part.astype(F32) for part in cut(left * left)], axis=0).astype(BF16)
            square = stack_of(piece).astype(F32)
            square = square * square
            high = square.astype(BF16)
            low = (square - high.astype(F32)).astype(BF16)
            dims = (((1,), (1,)), ((), ()))
            total = total + lax.dot_general(parts, high, dims, preferred_element_type=F32)
            total = total + lax.dot_general(parts, low, dims, preferred_element_type=F32)
        power[...] = after[:, :WIDTH] + total[:GROUPS] + total[GROUPS : 2 * GROUPS] + total[2 * GROUPS :]

    return kernel


def score_kernel(member):
    def kernel(place, power, meta_a, meta_b, *refs):
        pieces, out = refs[:4], refs[20]
        for k, meta in enumerate((meta_a, meta_b)):
            half = 0.5 * jnp.dot(hot_rows(meta), power[...], precision=HIGHEST, preferred_element_type=F32)
            sums = None
            for t in range(4):
                weights = [pieces[t][2 * n] for n in range(4)] + [pieces[n][2 * (place[1] ^ t) + 1] for n in range(4)]
                shifted = jnp.concatenate([refs[4 + 8 * k + t][member], refs[8 + 8 * k + t][member]], axis=1)
                part = lax.dot_general(
                    shifted, jnp.concatenate(weights, axis=1), (((1,), (1,)), ((), ())), preferred_element_type=F32
                )
                sums = part if sums is None else sums + part
            spare = jnp.zeros((ROWS - SLOTS * SHIFTS, WIDTH), F32)
            out[k, :, :WIDTH] = sums - jnp.concatenate([half] * SHIFTS + [spare], axis=0)

    return kernel


def settle_kernel(place, mine, theirs, stats):
    columns = []
    for k in range(2):

        def value(s):
            at = slice(SLOTS * s, SLOTS * (s + 1))
            return mine[k, at, :WIDTH] + theirs[k, at, :WIDTH]

        best = value(0)
        for s in range(1, SHIFTS):
            best = jnp.maximum(best, value(s))
        top = jnp.max(best, axis=1, keepdims=True)
        total = jnp.exp(value(0) - top)
        for s in range(1, SHIFTS):
            total = total + jnp.exp(value(s) - top)
        columns += [top, jnp.sum(total, axis=1, keepdims=True)]
    lane = lax.broadcasted_iota(jnp.int32, (SLOTS, LANE), 1)
    spread = jnp.where(lane == 0, columns[0], jnp.where(lane == 1, columns[1], jnp.where(lane == 2, columns[2], columns[3])))
    spread = jnp.concatenate([spread, jnp.zeros((LANE - SLOTS, LANE), F32)], axis=0).T[:8, :]
    for d in range(8):
        stats[d] = spread


def posterior_kernel(place, mine, theirs, stats, meta_a, meta_b, low, evidence, spare):
    parity = place[2]
    counted = jnp.zeros((GROUPS, WIDTH), F32)
    for k, meta in ((1, meta_b), (0, meta_a)):
        tops, totals = [], []
        for d in range(8):
            same = (parity == d % 2) == (k == 0)
            here = stats[d, :, :SLOTS]
            tops.append(jnp.where(same, here[0:1], here[2:3]))
            totals.append(jnp.where(same, here[1:2], here[3:4]))
        tops = jnp.concatenate(tops, axis=0)
        totals = jnp.concatenate(totals, axis=0)
        top = jnp.max(tops, axis=0, keepdims=True)
        total = jnp.sum(totals * jnp.exp(tops - top), axis=0, keepdims=True)
        row = lax.broadcasted_iota(jnp.int32, (8, SLOTS), 0)
        columns = jnp.where(row == 0, top, jnp.where(row == 1, total, top + jnp.log(total))).T
        live = meta[:, DEPTH + 1 : DEPTH + 2].astype(F32)
        scale = live / columns[:, 1:2]
        if k == 0:
            known = jnp.where(live > 0.0, columns[:, 2:3], 0.0)
            evidence[...] = jnp.broadcast_to(known, (SLOTS, LANE)).T[:8, :]
        gathered = None
        for s in range(SHIFTS):
            at = slice(SLOTS * s, SLOTS * (s + 1))
            value = jnp.exp(mine[k, at, :WIDTH] + theirs[k, at, :WIDTH] - columns[:, 0:1]) * scale
            spare[at, :] = value
            gathered = value if gathered is None else gathered + value
        hot = hot_rows(meta)
        counted = counted + lax.dot_general(
            hot, gathered, (((0,), (0,)), ((), ())), precision=HIGHEST, preferred_element_type=F32
        )
        spare[SLOTS * SHIFTS :, :] = jnp.zeros((ROWS - SLOTS * SHIFTS, WIDTH), F32)
        if k == 0:
            first = counted.astype(BF16).astype(F32)
            spare[COUNTED : COUNTED + GROUPS, :] = first
            spare[COUNTED + GROUPS : COUNTED + 2 * GROUPS, :] = counted - first
        low[k] = spare[...].T.astype(BF16)


def posterior_call(*args):
    out = [shape(2, WIDTH, ROWS, dtype=BF16), shape(8, SLOTS)]
    return pl.pallas_call(
        posterior_kernel,
        name="posterior",
        in_specs=[SMEM] + [VMEM] * (len(args) - 1),
        out_specs=[VMEM] * 2,
        out_shape=out,
        scratch_shapes=[pltpu.VMEM((ROWS, WIDTH), F32)],
        compiler_params=pltpu.CompilerParams(vmem_limit_bytes=LIMIT * MIB),
    )(*args)


def block_sums(low, groups, put):
    for n in (0, 2):
        at = slice(LANE * n, LANE * (n + 2))
        sums = jnp.dot(low, jnp.concatenate([g[:, at] for g in groups], axis=0), preferred_element_type=F32)
        for r in range(2):
            put(n + r, sums[:, r * LANE : (r + 1) * LANE])


def own_kernel(place, mine, a0, a1, b0, b1, out_a, out_b):
    low = jnp.concatenate([mine[0], mine[1]], axis=1)
    for groups, out in (((a0.at[0], a1.at[0]), out_a), ((b0.at[0], b1.at[0]), out_b)):

        def put(n, value):
            out[n] = value

        block_sums(low, groups, put)


def insert_kernel(chunks, begun=False, joined=False):
    def kernel(place, after, mine, theirs, *refs):
        starts, refs = (refs[:2], refs[2:]) if begun or joined else ((None, None), refs)
        members = (1,) if begun else (0, 1)
        shifted, outs = refs[: 4 * chunks], refs[4 * chunks :]
        lows = [theirs[0], theirs[1]] if begun else [mine[0], theirs[0], mine[1], theirs[1]]
        low = jnp.concatenate(lows, axis=1)
        tail = slice(ROWS - LANE, ROWS)
        first = COUNTED - ROWS + LANE
        both = (mine[0, :, tail].astype(F32) + theirs[0, :, tail].astype(F32)).T
        both = both[first : first + GROUPS] + both[first + GROUPS : first + 2 * GROUPS]
        both = jnp.concatenate([both, jnp.zeros((GROUPS, WIDE - WIDTH), F32)], axis=1)
        both = jnp.concatenate([both[:, :LANE], both[:, LANE:]], axis=0)
        outs[-1][...] = jnp.zeros((8, LANE), F32)
        for i, out in enumerate(outs[:-1]):
            start = starts[i % 2]

            def put(n, value):
                if start is not None:
                    value = value + start[n, :WIDTH].astype(F32)
                out[n, :WIDTH, :] = value.astype(out.dtype)

            block_sums(low, [pair.at[k] for pair in shifted[2 * i : 2 * i + 2] for k in members], put)
            for n in range(4):
                out[n, WIDTH:, :] = (both + start[n, WIDTH:].astype(F32) if joined else both).astype(out.dtype)

    return kernel


def gather_kernel(place, own_a, own_b, one_a, one_b, three_a, three_b, kept_a, kept_b, sent_a, sent_b):
    y = place[1]
    for out, planes in ((kept_a, (y, y ^ 3)), (sent_a, (y ^ 1, y ^ 2))):
        for i, n in enumerate(planes):
            out[i] = (own_a[n] + one_a[n].astype(F32) + three_a[n].astype(F32)).astype(out.dtype)
    for out, planes in ((kept_b, (0, 3)), (sent_b, (1, 2))):
        for i, n in enumerate(planes):
            out[i] = (own_b[n] + one_b[n].astype(F32) + three_b[n].astype(F32)).astype(out.dtype)


def middle_kernel(place, kept_a, kept_b, got_a, got_b, stay, same, other, across):
    side = place[2] == 0
    for out, (i, turned) in ((stay, (0, False)), (same, (1, False)), (other, (0, True)), (across, (1, True))):
        even = kept_a[i] + got_a[i].astype(F32)
        odd = kept_b[i] + got_b[i].astype(F32)
        out[...] = (jnp.where(side, odd, even) if turned else jnp.where(side, even, odd)).astype(out.dtype)


def finish_kernel(place, stay, same, across, other, insertions, weights):
    mine = stay[...] + same[...].astype(F32)
    theirs = other[...].astype(F32) + across[...].astype(F32)
    for k, sums in ((place[2], mine), (1 - place[2], theirs)):
        insertions[k] = sums[:WIDTH]
        weights[k] = jnp.concatenate([sums[WIDTH : WIDTH + GROUPS], sums[WIDTH + GROUPS :]], axis=1)[:, :WIDTH]


def swap(value, axis, d, n=4):
    return lax.ppermute(value, axis, [(i, i ^ d) for i in range(n)])


def body(particle_images, particle_groups, live_counts, ctf_table, projections):
    x, y, zl, core = (lax.axis_index(a) for a in ("grp", "y", "zl", "core"))
    place = jnp.stack([x, y, zl, core]).astype(jnp.int32)
    ring = ("cls", "zl")

    stacks = jnp.transpose(projections, (1, 2, 0))
    column = lax.all_to_all(spread_call(stacks), ("y", "zl"), 0, 0, tiled=True)

    tables = np.concatenate(shift_tables())
    kept, other, parts, turns, ctf = split_call(place, particle_groups, live_counts, particle_images, ctf_table, jnp.asarray(tables))
    halves = [kept, lax.ppermute(other, "core", SWAP)]

    column, to_pair, to_next = lax.optimization_barrier((column, kept, other))
    next_kept = lax.ppermute(to_pair, "zl", SWAP)
    next_other = lax.ppermute(to_next, ring, [(i, (i + 1) % 8 if i % 2 else (i + 7) % 8) for i in range(8)])
    first, third, second = (swap(column, "grp", d) for d in (1, 3, 2))
    pieces = [column, first, second, third]

    built = [build_call(place, column, halves[0], halves[1], parts, turns, "build_here", 6 * 10**9)]
    next_kept, next_other, _ = lax.optimization_barrier((next_kept, next_other, built[0][8]))
    halves += [next_kept, lax.ppermute(next_other, "core", SWAP)]
    built += [build_call(place, column, halves[2], halves[3], parts, turns, "build_next", 10**8)]
    shifted = [b[:8] for b in built]
    tokens = [b[8] for b in built]
    power = call(weigh_kernel((0,)), "weigh_own", shape(GROUPS, WIDTH), (place, ctf, tokens[0], column), LIMIT, 10**8)
    power = call(weigh_kernel((1, 3, 2)), "weigh", shape(GROUPS, WIDTH), (place, ctf, power, pieces[1], pieces[3], pieces[2], *tokens[1:]), LIMIT)
    score = shape(2, ROWS, WIDE)
    flops = 4 * ROWS * WIDE * DEPTH
    given = call(score_kernel(1), "score_given", score, (place, power, halves[1], halves[3], *pieces, *shifted[0], *shifted[1]), LIMIT, flops)
    taken = lax.ppermute(given, "core", SWAP)
    kept_score = call(score_kernel(0), "score_own", score, (place, power, halves[0], halves[2], *pieces, *shifted[0], *shifted[1]), LIMIT, flops)
    stats = call(settle_kernel, "settle", shape(8, 8, LANE), (place, kept_score, taken), LIMIT)
    stats = lax.all_to_all(stats, ring, 0, 0, tiled=True)
    low, evidence = posterior_call(place, kept_score, taken, stats, halves[0], halves[2])
    other_low = lax.ppermute(low, "core", SWAP)

    flops = 2 * 4 * ROWS * WIDE * 1024
    token = shape(8, LANE)

    def block(kind):
        return [shape(4, TALL, LANE, dtype=kind)] * 2

    def columns(chunk):
        return [pair[part + chunk] for part in (0, 4) for pair in shifted]

    begun = call(own_kernel, "insert_begin", [shape(4, WIDTH, LANE)] * 2, (place, low, *columns(2)), LIMIT, flops // 2)
    *send, after = call(
        insert_kernel(1, True), "insert_far", [*block(BF16), token], (place, evidence, low, other_low, *begun, *columns(2)), LIMIT, flops // 2
    )
    far = [swap(send[0], "grp", 2), swap(send[1], "y", 2)]
    *send, after = call(
        insert_kernel(2),
        "insert_near",
        [*block(BF16), *block(BF16), token],
        (place, after, low, other_low, *columns(1), *columns(3)),
        LIMIT,
        2 * flops,
    )
    near = [swap(send[0], "grp", 1), swap(send[1], "y", 1), swap(send[2], "grp", 3), swap(send[3], "y", 3)]
    *own, _ = call(
        insert_kernel(1, joined=True), "insert_own", [*block(F32), token], (place, after, low, other_low, *far, *columns(0)), LIMIT, flops
    )
    pair = (2, TALL, LANE)
    out = [shape(*pair)] * 2 + [shape(*pair, dtype=BF16)] * 2
    *kept, send_a, send_b = call(gather_kernel, "gather", out, (place, *own, *near), LIMIT)
    out = [shape(*pair[1:])] + [shape(*pair[1:], dtype=BF16)] * 3
    stay, *sent = call(middle_kernel, "middle", out, (place, *kept, swap(send_a, "y", 1), swap(send_b, "grp", 1)), LIMIT)
    plane = ("grp", "y", "zl")
    spots = [(i, j, k) for i in range(4) for j in range(4) for k in range(2)]

    def number(i, j, k):
        return i * 8 + j * 2 + k

    def turn(i, j, side):
        return (i, j ^ 3) if side == 0 else (i ^ 3, j)

    same = lax.ppermute(sent[0], plane, [(number(i, j, k), number(*turn(i, j, k), k)) for i, j, k in spots])
    across = lax.ppermute(sent[2], plane, [(number(i, j, k), number(*turn(i, j, 1 - k), 1 - k)) for i, j, k in spots])
    other = lax.ppermute(sent[1], plane, [(number(i, j, k), number(i, j, 1 - k)) for i, j, k in spots])
    insertions, tally = call(finish_kernel, "finish", [shape(2, WIDTH, LANE), shape(2, GROUPS, WIDTH)], (place, stay, same, across, other), LIMIT)
    return insertions, tally, evidence[0]


def solution(mesh):
    fine = Mesh(mesh.devices.reshape(4, 4, 4, 2, 2), ("cls", "grp", "y", "zl", "core"))
    shards = ("grp", "y", "zl", "core")
    return jax.shard_map(
        body,
        mesh=fine,
        in_specs=(P(shards, None), P(shards), P(shards), P(), P(shards, "cls", None)),
        out_specs=(P("cls", None, shards), P("cls", None, None), P(shards)),
        check_vma=False,
    )
```

```python
import math

import jax
import jax.numpy as jnp
import numpy as np
from jax import lax
from jax.experimental import pallas as pl
from jax.experimental.pallas import tpu as pltpu
from jax.sharding import Mesh, PartitionSpec as P

IMG = 64
SIDE = 5
SHIFTS = SIDE * SIDE
HALF = SHIFTS // 2
GROUPS = 8
FREQS = IMG * IMG
LANE = 128
SLOTS = 40
ROWS = 1024
WIDTH = 200
WIDE = 256
TALL = WIDTH + 16
COUNTED = SLOTS * SHIFTS
BLOCKS = 32
DEPTH = BLOCKS * LANE
CHUNK = DEPTH // 8
HIGHEST = lax.Precision.HIGHEST
F32 = jnp.float32
BF16 = jnp.bfloat16
MIB = 2**20
LIMIT = 4
VMEM = pl.BlockSpec(memory_space=pltpu.VMEM)
SMEM = pl.BlockSpec(memory_space=pltpu.SMEM)
SWAP = [(0, 1), (1, 0)]


def shift_tables():
    index = np.arange(FREQS)
    shift = np.arange(HALF)
    offx = shift // SIDE - SIDE // 2
    offy = shift % SIDE - SIDE // 2
    phase = (offx[:, None] * (index // IMG)[None, :] + offy[:, None] * (index % IMG)[None, :]) % IMG
    theta = (phase.astype(np.float32) * np.float32(2.0 * math.pi / IMG)).astype(np.float64)
    return np.cos(theta).astype(np.float32), np.sin(theta).astype(np.float32)


def call(kernel, name, out, args, limit, flops=0, moved=0):
    return pl.pallas_call(
        kernel,
        name=name,
        in_specs=[SMEM] + [VMEM] * (len(args) - 1),
        out_specs=jax.tree.map(lambda _: VMEM, out),
        out_shape=out,
        cost_estimate=pl.CostEstimate(flops=flops, bytes_accessed=moved, transcendentals=0),
        compiler_params=pltpu.CompilerParams(vmem_limit_bytes=limit * MIB),
    )(*args)


def shape(*dims, dtype=F32):
    return jax.ShapeDtypeStruct(dims, dtype)


def lanes(block):
    return pl.ds(pl.multiple_of(block * LANE, LANE), LANE)


def cut(value):
    first = value.astype(BF16)
    rest = value - first.astype(F32)
    second = rest.astype(BF16)
    return first, second, (rest - second.astype(F32)).astype(BF16)


def spread_kernel(stacks, out, held, sem):
    copy = pltpu.make_async_copy(stacks, held, sem)
    copy.start()
    copy.wait()
    for n in range(8):
        out[n] = held[n % 2]


def spread_call(stacks):
    return pl.pallas_call(
        spread_kernel,
        name="spread",
        in_specs=[pl.BlockSpec(memory_space=pltpu.HBM)],
        out_specs=VMEM,
        out_shape=shape(8, WIDTH, LANE, dtype=BF16),
        scratch_shapes=[pltpu.VMEM((2, WIDTH, LANE), BF16), pltpu.SemaphoreType.DMA],
        compiler_params=pltpu.CompilerParams(vmem_limit_bytes=LIMIT * MIB),
    )(pltpu.with_memory_space_constraint(stacks, pltpu.HBM))


def split_kernel(place, groups, count, images, ctf, tables, kept, given, parts, turns, held, images_in, ctf_in, sems):
    core = place[3]
    copies = [
        pltpu.make_async_copy(source, target, sems.at[i])
        for i, (source, target) in enumerate(((images, images_in), (ctf, ctf_in), (tables, turns)))
    ]
    for copy in copies:
        copy.start()
    copies[1].wait()
    held[...] = ctf_in[...]
    for i, part in enumerate(cut(ctf_in[...])):
        parts[16 * i : 16 * i + 16, :] = jnp.concatenate([part.astype(F32), jnp.zeros((8, FREQS), F32)], axis=0).astype(BF16)
    copies[0].wait()

    def turn(j, carry):
        kept[:, lanes(j)] = images_in[:, lanes(2 * j + core)]
        given[:, lanes(j)] = images_in[:, lanes(2 * j + 1 - core)]
        return carry

    lax.fori_loop(0, BLOCKS, turn, 0)
    row = lax.broadcasted_iota(jnp.int32, (SLOTS, LANE), 0)
    lane = lax.broadcasted_iota(jnp.int32, (SLOTS, LANE), 1)
    group = jnp.zeros((SLOTS, LANE), jnp.int32)
    for i in range(SLOTS):
        group = jnp.where(row == i, groups[i], group)
    live = jnp.where(row < count[0], 1, 0)
    meta = jnp.where(lane == 0, group, jnp.where(lane == 1, live, 0)).astype(F32).astype(BF16)
    kept[:, DEPTH:] = meta
    given[:, DEPTH:] = meta
    copies[2].wait()


def split_call(place, groups, count, images, ctf, tables):
    half = shape(SLOTS, DEPTH + LANE, dtype=BF16)
    anywhere = pl.BlockSpec(memory_space=pltpu.HBM)
    return pl.pallas_call(
        split_kernel,
        name="split",
        in_specs=[SMEM, SMEM, SMEM, anywhere, anywhere, anywhere],
        out_specs=[VMEM] * 5,
        out_shape=[half, half, shape(48, FREQS, dtype=BF16), shape(2 * HALF, FREQS), shape(GROUPS, FREQS)],
        scratch_shapes=[
            pltpu.VMEM((SLOTS, 2 * DEPTH), BF16),
            pltpu.VMEM((GROUPS, FREQS), F32),
            pltpu.SemaphoreType.DMA((3,)),
        ],
        compiler_params=pltpu.CompilerParams(vmem_limit_bytes=LIMIT * MIB),
    )(place, groups, count, *(pltpu.with_memory_space_constraint(v, pltpu.HBM) for v in (images, ctf, tables)))


def owner_block(place, p):
    later, first, second = p // 16, p % 16 // 4, p % 4
    across = jnp.where(later == 0, first, second)
    along = jnp.where(later == 0, second, place[1] ^ first)
    return (place[0] ^ across) * 8 + along * 2 + later


def build_kernel(place, after, images_a, images_b, parts, turns, *refs):
    outs, (token, rows) = refs[:8], refs[8:]
    core = place[3]
    lane = lax.broadcasted_iota(jnp.int32, (SLOTS, 48), 1)

    def member(k, carry):
        def read(at):
            return jnp.where(k == 0, images_a[:, at].astype(F32), images_b[:, at].astype(F32))

        group = read(slice(DEPTH, DEPTH + LANE))[:, :1]
        hot = jnp.where((group == (lane % 16).astype(F32)) & (lane % 16 < GROUPS), 1.0, 0.0).astype(BF16)
        rows[...] = jnp.dot(hot, parts[...], preferred_element_type=F32)
        for t, out in enumerate(outs):

            def turn(p, carry):
                j = owner_block(place, 4 * t + p)
                at = lanes(2 * (j % 16) + core)
                sign = jnp.where(j < 16, 1.0, -1.0).astype(F32)
                row = rows[:, at]
                first = read(lanes(j)) * row
                second = read(lanes(j ^ 16)) * (row * sign)
                here = lanes(p)
                for s in range(HALF):
                    a = first * turns[s : s + 1, at]
                    b = second * turns[HALF + s : HALF + s + 1, at]
                    pair = jnp.concatenate([a + b, a - b], axis=0).astype(BF16)
                    out[k, 2 * SLOTS * s : 2 * SLOTS * (s + 1), here] = pair
                tail = jnp.concatenate([first, jnp.zeros((ROWS - SLOTS * SHIFTS, LANE), F32)], axis=0)
                out[k, 2 * SLOTS * HALF : ROWS, here] = tail.astype(BF16)
                return carry

            lax.fori_loop(0, 4, turn, 0, unroll=4)
        return carry

    lax.fori_loop(0, 2, member, 0)
    token[...] = jnp.zeros_like(token)


def build_call(place, after, images_a, images_b, parts, turns, name, flops):
    return pl.pallas_call(
        build_kernel,
        name=name,
        in_specs=[SMEM] + [VMEM] * 5,
        out_specs=[VMEM] * 9,
        out_shape=[shape(2, ROWS, CHUNK, dtype=BF16)] * 8 + [shape(8, WIDE)],
        scratch_shapes=[pltpu.VMEM((SLOTS, FREQS), F32)],
        cost_estimate=pl.CostEstimate(flops=flops, bytes_accessed=10**5, transcendentals=0),
        compiler_params=pltpu.CompilerParams(vmem_limit_bytes=LIMIT * MIB),
    )(place, after, images_a, images_b, parts, turns)


def hot_rows(meta):
    group = meta[:, DEPTH : DEPTH + 1].astype(F32)
    lane = lax.broadcasted_iota(jnp.int32, (SLOTS, GROUPS), 1).astype(F32)
    return jnp.where(group == lane, 1.0, 0.0).astype(F32)


def stack_of(piece):
    return jnp.concatenate([piece[r] for r in range(8)], axis=1)


def weigh_kernel(chunks):
    def kernel(place, ctf, after, *refs):
        pieces, power = refs[:-1], refs[-1]
        core = place[3]
        total = jnp.zeros((3 * GROUPS, WIDTH), F32)
        for q, piece in zip(chunks, pieces):
            left = jnp.concatenate([ctf[:, lanes(2 * (((place[0] ^ q) * 8 + r) % 16) + core)] for r in range(8)], axis=1)
            parts = jnp.concatenate([part.astype(F32) for part in cut(left * left)], axis=0).astype(BF16)
            square = stack_of(piece).astype(F32)
            square = square * square
            high = square.astype(BF16)
            low = (square - high.astype(F32)).astype(BF16)
            dims = (((1,), (1,)), ((), ()))
            total = total + lax.dot_general(parts, high, dims, preferred_element_type=F32)
            total = total + lax.dot_general(parts, low, dims, preferred_element_type=F32)
        power[...] = after[:, :WIDTH] + total[:GROUPS] + total[GROUPS : 2 * GROUPS] + total[2 * GROUPS :]

    return kernel


def score_kernel(member):
    def kernel(place, power, meta_a, meta_b, *refs):
        pieces, out = refs[:4], refs[20]
        for k, meta in enumerate((meta_a, meta_b)):
            half = 0.5 * jnp.dot(hot_rows(meta), power[...], precision=HIGHEST, preferred_element_type=F32)
            sums = None
            for t in range(4):
                weights = [pieces[t][2 * n] for n in range(4)] + [pieces[n][2 * (place[1] ^ t) + 1] for n in range(4)]
                shifted = jnp.concatenate([refs[4 + 8 * k + t][member], refs[8 + 8 * k + t][member]], axis=1)
                part = lax.dot_general(
                    shifted, jnp.concatenate(weights, axis=1), (((1,), (1,)), ((), ())), preferred_element_type=F32
                )
                sums = part if sums is None else sums + part
            spare = jnp.zeros((ROWS - SLOTS * SHIFTS, WIDTH), F32)
            out[k, :, :WIDTH] = sums - jnp.concatenate([half] * SHIFTS + [spare], axis=0)

    return kernel


def settle_kernel(place, mine, theirs, stats):
    columns = []
    for k in range(2):

        def value(s):
            at = slice(SLOTS * s, SLOTS * (s + 1))
            return mine[k, at, :WIDTH] + theirs[k, at, :WIDTH]

        best = value(0)
        for s in range(1, SHIFTS):
            best = jnp.maximum(best, value(s))
        top = jnp.max(best, axis=1, keepdims=True)
        total = jnp.exp(value(0) - top)
        for s in range(1, SHIFTS):
            total = total + jnp.exp(value(s) - top)
        columns += [top, jnp.sum(total, axis=1, keepdims=True)]
    lane = lax.broadcasted_iota(jnp.int32, (SLOTS, LANE), 1)
    spread = jnp.where(lane == 0, columns[0], jnp.where(lane == 1, columns[1], jnp.where(lane == 2, columns[2], columns[3])))
    spread = jnp.concatenate([spread, jnp.zeros((LANE - SLOTS, LANE), F32)], axis=0).T[:8, :]
    for d in range(8):
        stats[d] = spread


def posterior_kernel(place, mine, theirs, stats, meta_a, meta_b, low, evidence, spare):
    parity = place[2]
    counted = jnp.zeros((GROUPS, WIDTH), F32)
    for k, meta in ((1, meta_b), (0, meta_a)):
        tops, totals = [], []
        for d in range(8):
            same = (parity == d % 2) == (k == 0)
            here = stats[d, :, :SLOTS]
            tops.append(jnp.where(same, here[0:1], here[2:3]))
            totals.append(jnp.where(same, here[1:2], here[3:4]))
        tops = jnp.concatenate(tops, axis=0)
        totals = jnp.concatenate(totals, axis=0)
        top = jnp.max(tops, axis=0, keepdims=True)
        total = jnp.sum(totals * jnp.exp(tops - top), axis=0, keepdims=True)
        row = lax.broadcasted_iota(jnp.int32, (8, SLOTS), 0)
        columns = jnp.where(row == 0, top, jnp.where(row == 1, total, top + jnp.log(total))).T
        live = meta[:, DEPTH + 1 : DEPTH + 2].astype(F32)
        scale = live / columns[:, 1:2]
        if k == 0:
            known = jnp.where(live > 0.0, columns[:, 2:3], 0.0)
            evidence[...] = jnp.broadcast_to(known, (SLOTS, LANE)).T[:8, :]
        gathered = None
        for s in range(SHIFTS):
            at = slice(SLOTS * s, SLOTS * (s + 1))
            value = jnp.exp(mine[k, at, :WIDTH] + theirs[k, at, :WIDTH] - columns[:, 0:1]) * scale
            spare[at, :] = value
            gathered = value if gathered is None else gathered + value
        hot = hot_rows(meta)
        counted = counted + lax.dot_general(
            hot, gathered, (((0,), (0,)), ((), ())), precision=HIGHEST, preferred_element_type=F32
        )
        spare[SLOTS * SHIFTS :, :] = jnp.zeros((ROWS - SLOTS * SHIFTS, WIDTH), F32)
        if k == 0:
            first = counted.astype(BF16).astype(F32)
            spare[COUNTED : COUNTED + GROUPS, :] = first
            spare[COUNTED + GROUPS : COUNTED + 2 * GROUPS, :] = counted - first
        low[k] = spare[...].T.astype(BF16)


def posterior_call(*args):
    out = [shape(2, WIDTH, ROWS, dtype=BF16), shape(8, SLOTS)]
    return pl.pallas_call(
        posterior_kernel,
        name="posterior",
        in_specs=[SMEM] + [VMEM] * (len(args) - 1),
        out_specs=[VMEM] * 2,
        out_shape=out,
        scratch_shapes=[pltpu.VMEM((ROWS, WIDTH), F32)],
        compiler_params=pltpu.CompilerParams(vmem_limit_bytes=LIMIT * MIB),
    )(*args)


def block_sums(low, groups, put):
    for n in (0, 2):
        at = slice(LANE * n, LANE * (n + 2))
        sums = jnp.dot(low, jnp.concatenate([g[:, at] for g in groups], axis=0), preferred_element_type=F32)
        for r in range(2):
            put(n + r, sums[:, r * LANE : (r + 1) * LANE])


def own_kernel(place, mine, a0, a1, b0, b1, out_a, out_b):
    low = jnp.concatenate([mine[0], mine[1]], axis=1)
    for groups, out in (((a0.at[0], a1.at[0]), out_a), ((b0.at[0], b1.at[0]), out_b)):

        def put(n, value):
            out[n] = value

        block_sums(low, groups, put)


def insert_kernel(chunks, begun=False, joined=False):
    def kernel(place, after, mine, theirs, *refs):
        starts, refs = (refs[:2], refs[2:]) if begun or joined else ((None, None), refs)
        members = (1,) if begun else (0, 1)
        shifted, outs = refs[: 4 * chunks], refs[4 * chunks :]
        lows = [theirs[0], theirs[1]] if begun else [mine[0], theirs[0], mine[1], theirs[1]]
        low = jnp.concatenate(lows, axis=1)
        tail = slice(ROWS - LANE, ROWS)
        first = COUNTED - ROWS + LANE
        both = (mine[0, :, tail].astype(F32) + theirs[0, :, tail].astype(F32)).T
        both = both[first : first + GROUPS] + both[first + GROUPS : first + 2 * GROUPS]
        both = jnp.concatenate([both, jnp.zeros((GROUPS, WIDE - WIDTH), F32)], axis=1)
        both = jnp.concatenate([both[:, :LANE], both[:, LANE:]], axis=0)
        outs[-1][...] = jnp.zeros((8, LANE), F32)
        for i, out in enumerate(outs[:-1]):
            start = starts[i % 2]

            def put(n, value):
                if start is not None:
                    value = value + start[n, :WIDTH].astype(F32)
                out[n, :WIDTH, :] = value.astype(out.dtype)

            block_sums(low, [pair.at[k] for pair in shifted[2 * i : 2 * i + 2] for k in members], put)
            for n in range(4):
                out[n, WIDTH:, :] = (both + start[n, WIDTH:].astype(F32) if joined else both).astype(out.dtype)

    return kernel


def gather_kernel(along):
    def kernel(place, own, one, three, kept, sent):
        y = place[1] if along else 0
        for out, planes in ((kept, (y, y ^ 3)), (sent, (y ^ 1, y ^ 2))):
            for i, n in enumerate(planes):
                out[i] = (own[n] + one[n].astype(F32) + three[n].astype(F32)).astype(out.dtype)

    return kernel


def middle_kernel(place, kept_a, kept_b, got_a, got_b, stay, same, other, across):
    side = place[2] == 0
    for out, (i, turned) in ((stay, (0, False)), (same, (1, False)), (other, (0, True)), (across, (1, True))):
        even = kept_a[i] + got_a[i].astype(F32)
        odd = kept_b[i] + got_b[i].astype(F32)
        out[...] = (jnp.where(side, odd, even) if turned else jnp.where(side, even, odd)).astype(out.dtype)


def finish_kernel(place, stay, same, across, other, insertions, weights):
    mine = stay[...] + same[...].astype(F32)
    theirs = other[...].astype(F32) + across[...].astype(F32)
    for k, sums in ((place[2], mine), (1 - place[2], theirs)):
        insertions[k] = sums[:WIDTH]
        weights[k] = jnp.concatenate([sums[WIDTH : WIDTH + GROUPS], sums[WIDTH + GROUPS :]], axis=1)[:, :WIDTH]


def swap(value, axis, d, n=4):
    return lax.ppermute(value, axis, [(i, i ^ d) for i in range(n)])


def body(particle_images, particle_groups, live_counts, ctf_table, projections):
    x, y, zl, core = (lax.axis_index(a) for a in ("grp", "y", "zl", "core"))
    place = jnp.stack([x, y, zl, core]).astype(jnp.int32)
    ring = ("cls", "zl")

    stacks = jnp.transpose(projections, (1, 2, 0))
    column = lax.all_to_all(spread_call(stacks), ("y", "zl"), 0, 0, tiled=True)

    tables = np.concatenate(shift_tables())
    kept, other, parts, turns, ctf = split_call(place, particle_groups, live_counts, particle_images, ctf_table, jnp.asarray(tables))
    halves = [kept, lax.ppermute(other, "core", SWAP)]

    column, to_pair, to_next = lax.optimization_barrier((column, kept, other))
    next_kept = lax.ppermute(to_pair, "zl", SWAP)
    next_other = lax.ppermute(to_next, ring, [(i, (i + 1) % 8 if i % 2 else (i + 7) % 8) for i in range(8)])
    first, third, second = (swap(column, "grp", d) for d in (1, 3, 2))
    pieces = [column, first, second, third]

    built = [build_call(place, column, halves[0], halves[1], parts, turns, "build_here", 6 * 10**9)]
    next_kept, next_other, _ = lax.optimization_barrier((next_kept, next_other, built[0][8]))
    halves += [next_kept, lax.ppermute(next_other, "core", SWAP)]
    built += [build_call(place, column, halves[2], halves[3], parts, turns, "build_next", 10**8)]
    shifted = [b[:8] for b in built]
    tokens = [b[8] for b in built]
    power = call(weigh_kernel((0,)), "weigh_own", shape(GROUPS, WIDTH), (place, ctf, tokens[0], column), LIMIT, 10**8)
    power = call(weigh_kernel((1, 3, 2)), "weigh", shape(GROUPS, WIDTH), (place, ctf, power, pieces[1], pieces[3], pieces[2], *tokens[1:]), LIMIT)
    score = shape(2, ROWS, WIDE)
    flops = 4 * ROWS * WIDE * DEPTH
    given = call(score_kernel(1), "score_given", score, (place, power, halves[1], halves[3], *pieces, *shifted[0], *shifted[1]), LIMIT, flops)
    taken = lax.ppermute(given, "core", SWAP)
    kept_score = call(score_kernel(0), "score_own", score, (place, power, halves[0], halves[2], *pieces, *shifted[0], *shifted[1]), LIMIT, flops)
    stats = call(settle_kernel, "settle", shape(8, 8, LANE), (place, kept_score, taken), LIMIT)
    stats = lax.all_to_all(stats, ring, 0, 0, tiled=True)
    low, evidence = posterior_call(place, kept_score, taken, stats, halves[0], halves[2])
    other_low = lax.ppermute(low, "core", SWAP)

    flops = 2 * 4 * ROWS * WIDE * 1024
    token = shape(8, LANE)

    def block(kind):
        return [shape(4, TALL, LANE, dtype=kind)] * 2

    def columns(chunk):
        return [pair[part + chunk] for part in (0, 4) for pair in shifted]

    begun = call(own_kernel, "insert_begin", [shape(4, WIDTH, LANE)] * 2, (place, low, *columns(2)), LIMIT, flops // 2)
    *send, after = call(
        insert_kernel(1, True), "insert_far", [*block(BF16), token], (place, evidence, low, other_low, *begun, *columns(2)), LIMIT, flops // 2
    )
    far = [swap(send[0], "grp", 2), swap(send[1], "y", 2)]
    *send, after = call(
        insert_kernel(2),
        "insert_near",
        [*block(BF16), *block(BF16), token],
        (place, after, low, other_low, *columns(1), *columns(3)),
        LIMIT,
        2 * flops,
    )
    near = [swap(send[0], "grp", 1), swap(send[1], "y", 1), swap(send[2], "grp", 3), swap(send[3], "y", 3)]
    *own, _ = call(
        insert_kernel(1, joined=True), "insert_own", [*block(F32), token], (place, after, low, other_low, *far, *columns(0)), LIMIT, flops
    )
    pair = (2, TALL, LANE)
    out = [shape(*pair), shape(*pair, dtype=BF16)]
    kept_a, send_a = call(gather_kernel(True), "gather_a", out, (place, own[0], near[0], near[2]), LIMIT)
    got_a = swap(send_a, "y", 1)
    kept_b, send_b = call(gather_kernel(False), "gather_b", out, (place, own[1], near[1], near[3]), LIMIT)
    got_b = swap(send_b, "grp", 1)
    out = [shape(*pair[1:])] + [shape(*pair[1:], dtype=BF16)] * 3
    stay, *sent = call(middle_kernel, "middle", out, (place, kept_a, kept_b, got_a, got_b), LIMIT)
    plane = ("grp", "y", "zl")
    spots = [(i, j, k) for i in range(4) for j in range(4) for k in range(2)]

    def number(i, j, k):
        return i * 8 + j * 2 + k

    def turn(i, j, side):
        return (i, j ^ 3) if side == 0 else (i ^ 3, j)

    same = lax.ppermute(sent[0], plane, [(number(i, j, k), number(*turn(i, j, k), k)) for i, j, k in spots])
    across = lax.ppermute(sent[2], plane, [(number(i, j, k), number(*turn(i, j, 1 - k), 1 - k)) for i, j, k in spots])
    other = lax.ppermute(sent[1], plane, [(number(i, j, k), number(i, j, 1 - k)) for i, j, k in spots])
    insertions, tally = call(finish_kernel, "finish", [shape(2, WIDTH, LANE), shape(2, GROUPS, WIDTH)], (place, stay, same, across, other), LIMIT)
    return insertions, tally, evidence[0]


def solution(mesh):
    fine = Mesh(mesh.devices.reshape(4, 4, 4, 2, 2), ("cls", "grp", "y", "zl", "core"))
    shards = ("grp", "y", "zl", "core")
    return jax.shard_map(
        body,
        mesh=fine,
        in_specs=(P(shards, None), P(shards), P(shards), P(), P(shards, "cls", None)),
        out_specs=(P("cls", None, shards), P("cls", None, None), P(shards)),
        check_vma=False,
    )
```
